256 devices in a mesh: ep: 8 (over y, core), seq: 32 (over z, x).
Axes of the slice: x: 4, y: 4, z: 8, core: 2. Of those that a mesh axis runs over, the one named last changes fastest.
Arguments:
- frames: bfloat16 [8, 22528, 512], P('ep', 'seq'), may hold values from -6 to 6
- lengths: int32 [8], P('ep'), may hold values from 11264 to 22528
- w_in: bfloat16 [512, 1024], replicated, may hold values from -0.25 to 0.25
- kernel: float32 [31, 512], replicated, may hold values from -1 to 1
- w_out: bfloat16 [512, 512], replicated, may hold values from -0.25 to 0.25
- pool_query: bfloat16 [8, 512], replicated, may hold values from -600 to 600
- w_value: bfloat16 [512, 512], replicated, may hold values from -0.25 to 0.25
- text_emb: bfloat16 [256, 512], replicated, may hold values from -6 to 6
- teacher: float32 [8, 256], P('ep'), may hold values from -6 to 6
Outputs:
- loss: float32 [], replicated
- grad_in: float32 [512, 1024], P('seq', 'ep')
- grad_out: float32 [512, 512], P('seq', 'ep')
- grad_kernel: float32 [31, 512], replicated
- grad_query: float32 [8, 512], replicated
- grad_value: float32 [512, 512], replicated
The draws below stay inside these ranges and needn't reach their ends.
All inputs are finite; a program needn't handle non-finite values.
Results may differ from the reference program's by a relative error of at most 0.03.
Values may be sent and summed in bfloat16 or wider, within the bound.
No kernel may reach another device: no remote copies, remote signals or barrier semaphores. Data moves between devices by JAX's collectives and lax.ppermute only.
A program may use at most 64 MiB of HBM per device.

```python
import jax
import jax.numpy as jnp
from jax import lax

D = 512
HEADS = 8
KSIZE = 31
CANDS = 256
FRAMES = 22528
EPISODES = 8


def draw_pool_query(key, part):
    key_vals, key_scale = jax.random.split(jax.random.fold_in(key, 17))
    scales = jnp.exp(jax.random.uniform(key_scale, (HEADS, 1), jnp.float32, jnp.log(0.5), jnp.log(2.0)))
    values = jax.random.truncated_normal(key_vals, -5.0, 5.0, (HEADS, D), jnp.float32)
    return (values * scales).astype(jnp.bfloat16)


def with_ends(entries, own_key, least, high):
    extent = entries.shape
    index_at = [jax.random.randint(jax.random.fold_in(own_key, axis), (), 0, extent[axis]) for axis in range(len(extent))]
    entries = entries.at[tuple(index_at)].set(least)
    longest = extent.index(max(extent))
    index_at[longest] = (index_at[longest] + 1) % extent[longest]
    return entries.at[tuple(index_at)].set(high)


def levels(rng, dims, cuts, least, high):
    gain, own = 1.0, jax.random.fold_in(rng, 6)
    for dim, shards_of in cuts:
        draws = jnp.exp(jax.random.uniform(jax.random.fold_in(own, dim), (shards_of,), jnp.float32, least / len(cuts), high / len(cuts)))
        gain = gain * jnp.repeat(draws, dims[dim] // shards_of).reshape([-1 if axis == dim else 1 for axis in range(len(dims))])
    return gain


def gaussian(key, shape, deviation, reach, cuts=(), dtype=jnp.bfloat16):
    loudness = levels(key, shape, cuts, -0.22, 0.18) if cuts else 1.0
    entries = jax.random.normal(key, shape, jnp.float32) * deviation * loudness
    return jnp.minimum(jnp.maximum(entries, -reach), reach).astype(dtype)


def setup_inputs(seed: int = 0) -> dict:
    seeds = jax.random.split(jax.random.key(seed), 10)
    return {
        "frames": gaussian(seeds[0], (EPISODES, FRAMES, D), 1.0, 6.0, ((0, 8), (1, 32))),
        "lengths": with_ends(jax.random.randint(seeds[1], (EPISODES,), FRAMES // 2, FRAMES + 1), jax.random.fold_in(seeds[1], 1), FRAMES // 2, FRAMES).astype(jnp.int32),
        "w_in": gaussian(seeds[2], (D, 2 * D), D ** -0.5, 0.25),
        "kernel": gaussian(seeds[3], (KSIZE, D), KSIZE ** -0.5, 1.0, (), jnp.float32),
        "w_out": gaussian(seeds[4], (D, D), D ** -0.5, 0.25),
        "pool_query": draw_pool_query(jax.random.fold_in(seeds[9], 71), 0),
        "w_value": gaussian(seeds[6], (D, D), D ** -0.5, 0.25),
        "text_emb": gaussian(seeds[7], (CANDS, D), 1.0, 6.0),
        "teacher": gaussian(seeds[8], (EPISODES, CANDS), 1.0, 6.0, ((0, 8),), jnp.float32),
    }


def episode_grads(x, length, teacher_row, w_in, kernel, w_out, pool_query, w_value, text_emb):
    hi = lax.Precision.HIGHEST
    rim = KSIZE // 2
    head_dim = D // HEADS
    valid = (jnp.arange(FRAMES) < length).astype(jnp.float32)[:, None]
    xf = x.astype(jnp.float32)
    mean_val = lax.optimization_barrier(jnp.mean(xf, axis=-1, keepdims=True))
    var_val = lax.optimization_barrier(jnp.mean((xf - mean_val) ** 2, axis=-1, keepdims=True))
    normed = ((xf - mean_val) * lax.rsqrt(var_val + 1e-05)).astype(jnp.bfloat16)
    mixed = jnp.dot(normed, w_in, preferred_element_type=jnp.float32)
    sig = jax.nn.sigmoid(mixed[:, D:])
    glu = (mixed[:, :D] * sig * valid).astype(jnp.bfloat16)
    padded = jnp.pad(glu, ((rim, rim), (0, 0)))
    conv = jnp.zeros((FRAMES, D), jnp.float32)
    for k in range(KSIZE):
        conv = conv + kernel[k] * padded[k:k + FRAMES].astype(jnp.float32)
    sconv = jax.nn.sigmoid(conv)
    act = (conv * sconv).astype(jnp.bfloat16)
    resid = xf + jnp.dot(act, w_out, preferred_element_type=jnp.float32)
    queries = pool_query.astype(jnp.float32)
    scores = jnp.dot(resid, queries.T, precision=hi) / jnp.sqrt(jnp.float32(D))
    masked = jnp.where(valid > 0, scores, -1e+30)
    top = lax.optimization_barrier(jnp.max(masked, axis=0))
    expo = jnp.where(valid > 0, jnp.exp(masked - top), 0.0)
    total = lax.optimization_barrier(jnp.sum(expo, axis=0))
    probs = expo / total
    vbar = jnp.dot(probs.T, resid, precision=hi)
    wvals = w_value.astype(jnp.float32).reshape(D, HEADS, head_dim)
    pooled = jnp.einsum('hd,dhk->hk', vbar, wvals, precision=hi).reshape(D)
    rms = jnp.sqrt(jnp.mean(pooled * pooled) + 1e-06)
    emb = pooled / rms
    texts = text_emb.astype(jnp.float32)
    score = jnp.dot(texts, emb, precision=hi) / jnp.sqrt(jnp.float32(D))
    diff = score - teacher_row
    loss = jnp.sum(diff * diff) / CANDS
    dscore = 2.0 * diff / CANDS
    demb = jnp.dot(dscore, texts, precision=hi) / jnp.sqrt(jnp.float32(D))
    dpooled = (demb - emb * jnp.mean(demb * emb)) / rms
    dp3 = dpooled.reshape(HEADS, head_dim)
    g_value = jnp.einsum('hd,hk->dhk', vbar, dp3, precision=hi).reshape(D, D)
    dvbar = jnp.einsum('dhk,hk->hd', wvals, dp3, precision=hi)
    proj = jnp.dot(resid, dvbar.T, precision=hi)
    centre = lax.optimization_barrier(jnp.sum(dvbar * vbar, axis=-1))
    dscores = probs * (proj - centre)
    g_query = jnp.dot(dscores.T, resid, precision=hi) / jnp.sqrt(jnp.float32(D))
    dresid = (jnp.dot(probs, dvbar, precision=hi) + jnp.dot(dscores, queries, precision=hi) / jnp.sqrt(jnp.float32(D))).astype(jnp.bfloat16)
    g_out = lax.dot_general(act, dresid, (((0,), (0,)), ((), ())), preferred_element_type=jnp.float32)
    dact = lax.dot_general(dresid, w_out, (((1,), (1,)), ((), ())), preferred_element_type=jnp.float32)
    dconv = (dact * sconv * (1.0 + conv * (1.0 - sconv))).astype(jnp.bfloat16)
    dconv_f = dconv.astype(jnp.float32)
    dpad = jnp.pad(dconv, ((rim, rim), (0, 0)))
    dglu = jnp.zeros((FRAMES, D), jnp.float32)
    taps = []
    for k in range(KSIZE):
        dglu = dglu + kernel[k] * dpad[2 * rim - k:2 * rim - k + FRAMES].astype(jnp.float32)
        taps.append(lax.optimization_barrier(jnp.sum(padded[k:k + FRAMES].astype(jnp.float32) * dconv_f, axis=0)))
    g_kernel = jnp.stack(taps)
    dglu = dglu * valid
    dmixed = jnp.concatenate([dglu * sig, dglu * mixed[:, :D] * sig * (1.0 - sig)], axis=-1).astype(jnp.bfloat16)
    g_in = lax.dot_general(normed, dmixed, (((0,), (0,)), ((), ())), preferred_element_type=jnp.float32)
    return (loss, g_in, g_out, g_kernel, g_query, g_value)

def reference(frames, lengths, w_in, kernel, w_out, pool_query, w_value, text_emb, teacher):

    def step(carry, item):
        x, length, row = item
        out = episode_grads(x, length, row, w_in, kernel, w_out, pool_query, w_value, text_emb)
        return (tuple((c + o for c, o in zip(carry, out))), None)
    init = (jnp.zeros((), jnp.float32), jnp.zeros((D, 2 * D), jnp.float32), jnp.zeros((D, D), jnp.float32), jnp.zeros((KSIZE, D), jnp.float32), jnp.zeros((HEADS, D), jnp.float32), jnp.zeros((D, D), jnp.float32))
    sums, unused = lax.scan(step, init, (frames, lengths, teacher))
    return (sums[0], sums[1], sums[2], sums[3], sums[4], sums[5])
```

```python
import jax
import jax.numpy as jnp
from jax import lax
from jax.sharding import PartitionSpec as P


def pair(value):
    high = lax.reduce_precision(value, exponent_bits=8, mantissa_bits=7)
    return high.astype(jnp.bfloat16), (value - high).astype(jnp.bfloat16)


def to_all(value, axis):
    count = lax.axis_size(axis)
    return lax.all_to_all(jnp.broadcast_to(value[None], (count, *value.shape)), axis, 0, 0)


def shards(frames, lengths, w_in, kernel, w_out, pool_query, w_value, text_emb, teacher):
    hi = lax.Precision.HIGHEST
    n_ep, n_seq = lax.axis_size("ep"), lax.axis_size("seq")
    x = frames[0]
    n_rows, width = x.shape
    n_taps = kernel.shape[0]
    rim = n_taps // 2
    halo, side = 2 * (rim + 1), rim + 1
    n_heads = pool_query.shape[0]
    head_dim = width // n_heads
    n_cands = text_emb.shape[0]
    root_width = jnp.sqrt(jnp.float32(width))

    forward = [(i, i + 1) for i in range(n_seq - 1)]
    backward = [(target, source) for source, target in forward]
    low = lax.ppermute(x[n_rows - halo :], "seq", forward)
    high = lax.ppermute(x[:halo], "seq", backward)
    ext = jnp.concatenate([low, x, high], axis=0)
    offset = lax.axis_index("seq") * n_rows - halo
    positions = offset + jnp.arange(n_rows + 2 * halo, dtype=jnp.int32)
    valid = ((positions >= 0) & (positions < lengths[0]))[:, None]

    xf = ext.astype(jnp.float32)
    mean_val = jnp.mean(xf, axis=-1, keepdims=True)
    var_val = jnp.mean((xf - mean_val) ** 2, axis=-1, keepdims=True)
    normed = ((xf - mean_val) * lax.rsqrt(var_val + 1e-05)).astype(jnp.bfloat16)
    mixed = jnp.dot(normed, w_in, preferred_element_type=jnp.float32)
    sig = jax.nn.sigmoid(mixed[:, width:])
    glu = jnp.where(valid, mixed[:, :width] * sig, 0.0).astype(jnp.bfloat16)

    wide = n_rows + 2 * side
    conv = jnp.zeros((wide, width), jnp.float32)
    first = side - rim
    for k in range(n_taps):
        conv = conv + kernel[k] * glu[first + k : first + k + wide].astype(jnp.float32)
    sconv = jax.nn.sigmoid(conv)
    act = (conv * sconv).astype(jnp.bfloat16)
    resid = xf[side : side + wide] + jnp.dot(act, w_out, preferred_element_type=jnp.float32)
    queries = pool_query.astype(jnp.float32)
    scores = jnp.einsum("sd,hd->sh", resid, queries, precision=hi) / root_width
    valid_w = valid[side : side + wide]
    masked = jnp.where(valid_w, scores, -1e30)
    mid = slice(side, side + n_rows)
    top_here = jnp.max(masked[mid], axis=0)
    expo = jnp.where(valid_w[mid], jnp.exp(masked[mid] - top_here), 0.0)
    vec_here = jnp.einsum("sh,sd->hd", expo, resid[mid], precision=hi)
    total_here = jnp.sum(expo, axis=0)
    stats = jnp.zeros((n_heads, 128), jnp.float32).at[:, 0].set(top_here).at[:, 1].set(total_here)
    every = to_all(jnp.concatenate([vec_here, stats], axis=1), "seq")
    tops, totals, vecs = every[:, :, width], every[:, :, width + 1], every[:, :, :width]
    top = jnp.max(tops, axis=0)
    scale = jnp.exp(tops - top)
    total = jnp.sum(scale * totals, axis=0)
    vbar = jnp.sum(scale[..., None] * vecs, axis=0) / total[:, None]

    wvals = w_value.astype(jnp.float32).reshape(width, n_heads, head_dim)
    pooled = jnp.einsum("hd,dhk->hk", vbar, wvals, precision=hi).reshape(width)
    rms = jnp.sqrt(jnp.mean(pooled * pooled) + 1e-06)
    emb = pooled / rms
    texts = text_emb.astype(jnp.float32)
    score = jnp.einsum("d,cd->c", emb, texts, precision=hi) / root_width
    diff = score - teacher[0]
    loss_here = jnp.sum(diff * diff) / n_cands
    dscore = 2.0 * diff / n_cands
    demb = jnp.einsum("c,cd->d", dscore, texts, precision=hi) / root_width
    dpooled = (demb - emb * jnp.mean(demb * emb)) / rms
    dp3 = dpooled.reshape(n_heads, head_dim)
    dvbar = jnp.einsum("dhk,hk->hd", wvals, dp3, precision=hi)

    episode = jnp.concatenate(
        [vbar, dpooled[None], jnp.broadcast_to(loss_here, (1, width))], axis=0
    )
    episodes = to_all(episode, "ep")
    loss = jnp.sum(episodes[:, n_heads + 1, 0])
    grad_value = jnp.einsum(
        "ehd,ehk->dhk",
        episodes[:, :n_heads],
        episodes[:, n_heads].reshape(n_ep, n_heads, head_dim),
        precision=hi,
    ).reshape(width, width)

    probs = jnp.where(valid_w, jnp.exp(masked - top), 0.0) / total
    proj = jnp.einsum("sd,hd->sh", resid, dvbar, precision=hi)
    centre = jnp.sum(dvbar * vbar, axis=-1)
    dscores = probs * (proj - centre)
    query_here = jnp.einsum("sh,sd->hd", dscores[mid], resid[mid], precision=hi) / root_width
    dresid = (
        jnp.einsum("sh,hd->sd", probs, dvbar, precision=hi)
        + jnp.einsum("sh,hd->sd", dscores, queries, precision=hi) / root_width
    ).astype(jnp.bfloat16)
    out_here = jnp.einsum("sd,sf->df", act[mid], dresid[mid], preferred_element_type=jnp.float32)
    dact = jnp.einsum("sf,df->sd", dresid, w_out, preferred_element_type=jnp.float32)
    dconv = (dact * sconv * (1.0 + conv * (1.0 - sconv))).astype(jnp.bfloat16)
    dconv_f = dconv[mid].astype(jnp.float32)
    dglu = jnp.zeros((n_rows, width), jnp.float32)
    taps = []
    for k in range(n_taps):
        start = side + rim - k
        dglu = dglu + kernel[k] * dconv[start : start + n_rows].astype(jnp.float32)
        start = halo + k - rim
        taps.append(jnp.sum(glu[start : start + n_rows].astype(jnp.float32) * dconv_f, axis=0))
    inner = slice(halo, halo + n_rows)
    dglu = jnp.where(valid[inner], dglu, 0.0)
    sig_in, gate_in = sig[inner], mixed[inner, :width]
    dmixed = jnp.concatenate(
        [dglu * sig_in, dglu * gate_in * sig_in * (1.0 - sig_in)], axis=-1
    ).astype(jnp.bfloat16)
    in_here = jnp.einsum("sd,sf->df", normed[inner], dmixed, preferred_element_type=jnp.float32)

    cols = width // n_ep
    small = jnp.concatenate([*[t[None] for t in taps], query_here], axis=0)
    small_rows = -(-small.shape[0] // 16) * 16
    small = jnp.pad(small, ((0, small_rows - small.shape[0]), (0, 0)))
    small = small.reshape(small_rows, width // 128, 128).transpose(1, 0, 2)
    small = small.reshape(n_ep, -1, 128)
    rows = width // n_seq
    part_in = in_here.astype(jnp.bfloat16).reshape(width, n_ep, 2 * cols).transpose(1, 0, 2)
    part_out = (
        out_here.astype(jnp.bfloat16)
        .reshape(n_seq, 2, rows // 2, n_ep, cols)
        .transpose(3, 0, 2, 1, 4)
        .reshape(n_ep, width // 2, 2 * cols)
    )
    first_sum = jnp.sum(
        lax.all_to_all(
            jnp.concatenate([part_in, part_out, *pair(small)], axis=1), "ep", 0, 0
        ).astype(jnp.float32),
        axis=0,
    )
    n_small = small.shape[1]
    rows_in, rows_out, small_high, small_low = jnp.split(
        first_sum, [width, width + width // 2, width + width // 2 + n_small], axis=0
    )
    small_pair = jnp.concatenate(pair(small_high + small_low), axis=0)
    second_sum = jnp.sum(
        lax.all_to_all(
            jnp.concatenate(
                [
                    rows_in.astype(jnp.bfloat16).reshape(n_seq, rows, 2 * cols),
                    rows_out.astype(jnp.bfloat16).reshape(n_seq, rows // 2, 2 * cols),
                    jnp.broadcast_to(small_pair[None], (n_seq, *small_pair.shape)),
                ],
                axis=1,
            ),
            "seq",
            0,
            0,
        ).astype(jnp.float32),
        axis=0,
    )
    grad_in, grad_out, small_high, small_low = jnp.split(
        second_sum, [rows, rows + rows // 2, rows + rows // 2 + n_small], axis=0
    )
    grad_out = jnp.concatenate([grad_out[:, :cols], grad_out[:, cols:]], axis=0)
    small = to_all(small_high + small_low, "ep").reshape(width // 128, small_rows, 128)
    small = small.transpose(1, 0, 2).reshape(small_rows, width)
    grad_kernel, grad_query = small[:n_taps], small[n_taps : n_taps + n_heads]
    return (loss, grad_in, grad_out, grad_kernel, grad_query, grad_value)


def solution(mesh):
    return jax.shard_map(
        shards,
        mesh=mesh,
        in_specs=(P("ep", "seq", None), P("ep"), P(), P(), P(), P(), P(), P(), P("ep", None)),
        out_specs=(P(), P("seq", "ep"), P("seq", "ep"), P(), P(), P()),
        check_vma=False,
    )
```

```python
import functools

import jax
import jax.numpy as jnp
from jax import lax
from jax.experimental import pallas as pl
from jax.experimental.pallas import tpu as pltpu
from jax.sharding import PartitionSpec as P

F32, BF16 = jnp.float32, jnp.bfloat16
NN = (((1,), (0,)), ((), ()))
NT = (((1,), (1,)), ((), ()))
TN = (((0,), (0,)), ((), ()))
LANES = 128
STEP = 32
SIDE = 16


def dot(a, b, dims=NN):
    return lax.dot_general(a, b, dims, preferred_element_type=F32)


def split3(value):
    high = value.astype(BF16)
    rest = value - high.astype(F32)
    mid = rest.astype(BF16)
    return high, mid, (rest - mid.astype(F32)).astype(BF16)


def stacked(value):
    return jnp.concatenate(split3(value), axis=0)


def folded(value, count=3, rows=8):
    total = value[0:rows]
    for i in range(1, count):
        total = total + value[i * rows : (i + 1) * rows]
    return total


def lane_groups(shape, pieces):
    group = lax.broadcasted_iota(jnp.int32, shape, 1) // 8
    out = jnp.zeros(shape, F32)
    for g, piece in enumerate(pieces):
        out = jnp.where(group == g, piece.astype(F32), out)
    return out.astype(BF16)


def across(column):
    lane = lax.broadcasted_iota(jnp.int32, (8, LANES), 1)
    head = lax.broadcasted_iota(jnp.int32, (8, LANES), 0)
    return jnp.sum(jnp.where(lane % 8 == head, column, 0.0), axis=0, keepdims=True)


def down(row):
    lane = lax.broadcasted_iota(jnp.int32, (8, LANES), 1)
    head = lax.broadcasted_iota(jnp.int32, (8, LANES), 0)
    return jnp.sum(jnp.where(lane == head, row, 0.0), axis=1, keepdims=True)


def gated(x, w_in, width):
    xf = x.astype(F32)
    centred = xf - jnp.mean(xf, axis=-1, keepdims=True)
    var = jnp.mean(centred * centred, axis=-1, keepdims=True)
    normed = (centred * lax.rsqrt(var + 1e-05)).astype(BF16)
    mixed = dot(normed, w_in)
    return normed, mixed[:, :width], jax.nn.sigmoid(mixed[:, width:])


def row_mask(first, rows, length):
    at = first + lax.broadcasted_iota(jnp.int32, (rows, 1), 0)
    return (at >= 0) & (at < length)


def project_kernel(place, x_ref, w_in_ref, normed_ref, sig_ref, slope_ref, glu_ref):
    rows, width = x_ref.shape
    chunk = rows // 4
    for i in range(4):
        part = pl.ds(i * chunk, chunk)
        normed, gate, sig = gated(x_ref[part, :], w_in_ref[...], width)
        valid = row_mask(place[0] + i * chunk, chunk, place[1])
        normed_ref[part, :] = normed
        sig_ref[part, :] = sig.astype(BF16)
        both = gate * sig
        slope_ref[part, :] = (both * (1.0 - sig)).astype(BF16)
        glu_ref[part, :] = jnp.where(valid, both, 0.0).astype(BF16)


def shifted(block):
    rows = block.shape[0]
    return [block if s == 0 else pltpu.roll(block, rows - s, 0) for s in range(8)]


def forward_kernel(
    place, low_ref, high_ref, x_ref, own_glu_ref, w_in_ref, taps_ref, w_out_ref, query_ref,
    glu_ref, act_ref, slope_ref, resid_ref, sums_ref, glu_f,
):
    rows, width = x_ref.shape
    wide = rows + 2 * SIDE
    n_taps = taps_ref.shape[0]
    halo = jnp.concatenate([low_ref[...], high_ref[...]], axis=0)
    unused, gate, sig = gated(halo, w_in_ref[...], width)
    both = gate * sig
    valid_low = row_mask(place[0] - STEP, STEP, place[1])
    valid_high = row_mask(place[0] + rows, STEP, place[1])
    low = jnp.where(valid_low, both[:STEP], 0.0).astype(BF16)
    high = jnp.where(valid_high, both[STEP:], 0.0).astype(BF16)
    glu_ref[0:STEP, :] = low
    glu_ref[STEP : STEP + rows, :] = own_glu_ref[...]
    glu_ref[STEP + rows :, :] = high
    glu_f[0:STEP, :] = low.astype(F32)
    glu_f[STEP : STEP + rows, :] = own_glu_ref[...].astype(F32)
    glu_f[STEP + rows :, :] = high.astype(F32)

    @pl.loop(0, wide // STEP)
    def _(i):
        start = pl.multiple_of(i * STEP, STEP)
        for c in range(width // LANES):
            cols = slice(c * LANES, (c + 1) * LANES)
            views = shifted(glu_f[pl.ds(start, 2 * STEP), cols])
            acc = jnp.zeros((STEP, LANES), F32)
            for k in range(n_taps):
                q, s = divmod(k + 1, 8)
                acc = acc + taps_ref[k : k + 1, cols] * views[s][8 * q : 8 * q + STEP]
            s = jax.nn.sigmoid(acc)
            act_ref[pl.ds(start, STEP), cols] = (acc * s).astype(BF16)
            slope_ref[pl.ds(start, STEP), cols] = (s * (1.0 + acc * (1.0 - s))).astype(BF16)

    w_out = w_out_ref[...]
    resid_ref[0:SIDE, :] = low_ref[STEP - SIDE :, :].astype(F32) + dot(act_ref[0:SIDE, :], w_out)
    resid_ref[SIDE + rows :, :] = high_ref[0:SIDE, :].astype(F32) + dot(
        act_ref[SIDE + rows :, :], w_out
    )
    queries = jnp.concatenate([query_ref[...]] * (LANES // 8), axis=0)
    root = jnp.sqrt(jnp.float32(width))
    parts = 2
    chunk = rows // parts
    scores = []
    for i in range(parts):
        own = pl.ds(SIDE + i * chunk, chunk)
        resid = x_ref[pl.ds(i * chunk, chunk), :].astype(F32) + dot(act_ref[own, :], w_out)
        resid_ref[own, :] = resid
        score = sum(dot(piece, queries, NT) for piece in split3(resid)) / root
        valid = row_mask(place[0] + i * chunk, chunk, place[1])
        scores.append(jnp.where(valid, score, -1e30))
    top = functools.reduce(
        jnp.maximum, [jnp.max(score, axis=0, keepdims=True) for score in scores]
    )
    total = jnp.zeros((1, LANES), F32)
    vec = jnp.zeros((LANES, width), F32)
    for i in range(parts):
        valid = row_mask(place[0] + i * chunk, chunk, place[1])
        expo = jnp.where(valid, jnp.exp(scores[i] - top), 0.0)
        total = total + jnp.sum(expo, axis=0, keepdims=True)
        weights = lane_groups(expo.shape, split3(expo))
        for piece in split3(resid_ref[pl.ds(SIDE + i * chunk, chunk), :]):
            vec = vec + dot(weights, piece, TN)
    lane = lax.broadcasted_iota(jnp.int32, (8, LANES), 1)
    sums = jnp.concatenate(
        [folded(vec), jnp.where(lane == 0, down(top), down(total))], axis=1
    )

    @pl.loop(0, sums_ref.shape[0])
    def _(i):
        sums_ref[i] = sums


def backward_kernel(
    place, sums_ref, w_value_ref, text_ref, teacher_ref, query_ref, resid_ref, act_ref, slope_ref,
    glu_ref, normed_ref, sig_ref, gate_slope_ref, w_out_ref, taps_ref,
    episode_ref, mine_ref, other_ref,
    dconv_f, glu_f, dresid_s, dmixed_s, in_s, tap_s, small_s,
):
    rows, width = normed_ref.shape
    wide = rows + 2 * SIDE
    n_taps = taps_ref.shape[0]
    n_cands = text_ref.shape[0]
    head_dim = width // 8
    root = jnp.sqrt(jnp.float32(width))

    stats = sums_ref[:, :, width:]
    tops, totals = stats[:, :, 0:1], stats[:, :, 1:2]
    top = jnp.max(tops, axis=0)
    scale = jnp.exp(tops - top[None])
    total = jnp.sum(scale * totals, axis=0)
    vbar = jnp.sum(scale * sums_ref[:, :, :width], axis=0) / total
    at = lax.broadcasted_iota(jnp.int32, (8, width), 1) // head_dim
    own_head = at == lax.broadcasted_iota(jnp.int32, (8, width), 0)
    w_value = w_value_ref[...]
    texts = text_ref[...]
    full = folded(dot(stacked(vbar), w_value))
    pooled = jnp.sum(jnp.where(own_head, full, 0.0), axis=0, keepdims=True)
    pooled = jnp.broadcast_to(pooled, (8, width))
    rms = jnp.sqrt(jnp.mean(pooled * pooled, axis=-1, keepdims=True) + 1e-06)
    emb = pooled / rms
    diff = folded(dot(stacked(emb), texts, NT)) / root - teacher_ref[...]
    loss = jnp.sum(diff * diff, axis=-1, keepdims=True) / n_cands
    demb = folded(dot(stacked(2.0 * diff / n_cands), texts)) / root
    dpooled = (demb - emb * jnp.mean(demb * emb, axis=-1, keepdims=True)) / rms
    dvbar = folded(dot(stacked(jnp.where(own_head, dpooled, 0.0)), w_value, NT))
    centre = jnp.sum(dvbar * vbar, axis=-1, keepdims=True)
    row = lax.broadcasted_iota(jnp.int32, (8, width), 0)
    episode_ref[0:8, :] = vbar
    episode_ref[8:16, :] = jnp.where(row == 0, dpooled, jnp.where(row == 1, loss, 0.0))

    top_l, total_l, centre_l = across(top), across(total), across(centre)
    query = query_ref[...]
    queries = jnp.concatenate([query] * (LANES // 8), axis=0)
    d_high, d_mid, d_low = split3(dvbar)
    many = lambda piece: jnp.concatenate([piece] * (LANES // 8), axis=0)
    dv_high, dv_mid, dv_low = many(d_high), many(d_mid), many(d_low)
    mixing = jnp.concatenate(
        [d_high, d_mid, d_high, d_mid, query, query, query, jnp.zeros((LANES - 56, width), BF16)],
        axis=0,
    )
    w_out = w_out_ref[...]
    parts = 2
    chunk = wide // parts
    grad_query = jnp.zeros((LANES, width), F32)
    for i in range(parts):
        here = pl.ds(i * chunk, chunk)
        r_high, r_mid, r_low = split3(resid_ref[here, :])
        score = (dot(r_high, queries, NT) + dot(r_mid, queries, NT) + dot(r_low, queries, NT)) / root
        valid = row_mask(place[0] - SIDE + i * chunk, chunk, place[1])
        probs = jnp.where(valid, jnp.exp(score - top_l), 0.0) / total_l
        proj = dot(r_high, dv_high, NT) + (dot(r_high, dv_mid, NT) + dot(r_mid, dv_high, NT))
        proj = proj + (
            dot(r_high, dv_low, NT) + dot(r_mid, dv_mid, NT) + dot(r_low, dv_high, NT)
        )
        dscores = probs * (proj - centre_l) / root
        p_high, p_mid, unused = split3(probs)
        s_pieces = split3(dscores)
        mixed = lane_groups(probs.shape, (p_high, p_high, p_mid, p_mid, *s_pieces))
        dresid = dot(mixed, mixing).astype(BF16)
        dresid_s[here, :] = dresid
        own = lax.broadcasted_iota(jnp.int32, (chunk, 1), 0) + i * chunk
        own = (own >= SIDE) & (own < SIDE + rows)
        weights = lane_groups(probs.shape, s_pieces)
        weights = jnp.where(own, weights.astype(F32), 0.0).astype(BF16)
        for piece in (r_high, r_mid, r_low):
            grad_query = grad_query + dot(weights, piece, TN)
        dact = dot(dresid, w_out, NT)
        dconv = (dact * slope_ref[here, :].astype(F32)).astype(BF16)
        dconv_f[here, :] = dconv.astype(F32)
    small_s[0:8, :] = folded(grad_query)

    glu_f[...] = glu_ref[...].astype(F32)
    tap_s[...] = jnp.zeros_like(tap_s)

    @pl.loop(0, rows // STEP)
    def _(i):
        start = pl.multiple_of(i * STEP, STEP)
        valid = row_mask(place[0] + start, STEP, place[1])
        for c in range(width // LANES):
            cols = slice(c * LANES, (c + 1) * LANES)
            views = shifted(dconv_f[pl.ds(start, 2 * STEP), cols])
            acc = jnp.zeros((STEP, LANES), F32)
            for k in range(n_taps):
                q, s = divmod(n_taps - k, 8)
                acc = acc + taps_ref[k : k + 1, cols] * views[s][8 * q : 8 * q + STEP]
            dglu = jnp.where(valid, acc, 0.0)
            here = pl.ds(start, STEP)
            dmixed_s[here, cols] = (dglu * sig_ref[here, cols].astype(F32)).astype(BF16)
            dmixed_s[here, slice(width + c * LANES, width + (c + 1) * LANES)] = (
                dglu * gate_slope_ref[here, cols].astype(F32)
            ).astype(BF16)
            own = views[0][SIDE : SIDE + STEP]
            views = shifted(glu_f[pl.ds(start + SIDE, 2 * STEP), cols])
            for k in range(n_taps):
                q, s = divmod(k + 1, 8)
                product = own * views[s][8 * q : 8 * q + STEP]
                tap_s[k, :, cols] += folded(product, STEP // 8)

    small_s[8 : 8 + n_taps, :] = jnp.sum(tap_s[...], axis=1)
    small_s[8 + n_taps :, :] = jnp.zeros((small_s.shape[0] - 8 - n_taps, width), F32)

    grad_out = dot(act_ref[SIDE : SIDE + rows, :], dresid_s[SIDE : SIDE + rows, :], TN)
    in_s[...] = dot(normed_ref[...], dmixed_s[...], TN).astype(BF16)
    core = place[2]
    halves = grad_out.reshape(width // 16, 2, 8, width)
    first, second = (halves[:, j].reshape(width // 2, width) for j in range(2))
    low_lane = lax.broadcasted_iota(jnp.int32, (width // 2, LANES), 1) < LANES // 2
    for y in range(width // LANES):
        a = first[:, y * LANES : (y + 1) * LANES]
        b = second[:, y * LANES : (y + 1) * LANES]
        even = jnp.where(low_lane, a, pltpu.roll(b, LANES // 2, 1))
        odd = jnp.where(low_lane, pltpu.roll(a, LANES // 2, 1), b)
        for ref, which, block in (
            (mine_ref, core, jnp.where(core == 0, even, odd)),
            (other_ref, 1 - core, jnp.where(core == 0, odd, even)),
        ):
            at = pl.multiple_of((2 * y + which) * LANES, LANES)
            ref[y, 0:width, :] = in_s[:, pl.ds(at, LANES)]
            ref[y, width : width + width // 2, :] = block.astype(BF16)
            half = small_s.shape[0] // 2
            share = small_s[pl.ds(pl.multiple_of(which * half, 8), half), y * LANES : (y + 1) * LANES]
            high = share.astype(BF16).astype(F32)
            ref[y, width + width // 2 :, :] = jnp.concatenate(
                [high, share - high], axis=0
            ).astype(BF16)


def pair(value, axis):
    high = lax.reduce_precision(value, exponent_bits=8, mantissa_bits=7)
    return jnp.concatenate([high, value - high], axis=axis).astype(BF16)


def call(kernel, outs, scratch, n_args, flops):
    vmem = pl.BlockSpec(memory_space=pltpu.VMEM)
    return pl.pallas_call(
        kernel,
        out_shape=outs,
        in_specs=[pl.BlockSpec(memory_space=pltpu.SMEM)] + [vmem] * n_args,
        out_specs=[vmem] * len(outs),
        scratch_shapes=scratch,
        compiler_params=pltpu.CompilerParams(vmem_limit_bytes=48 * 2**20),
        cost_estimate=pl.CostEstimate(flops=flops, bytes_accessed=8 * 2**20, transcendentals=2**20),
    )


def shards(frames, lengths, w_in, kernel, w_out, pool_query, w_value, text_emb, teacher):
    n_ep, n_seq = lax.axis_size("ep"), lax.axis_size("seq")
    x = frames[0]
    rows, width = x.shape
    n_taps, n_heads = kernel.shape[0], pool_query.shape[0]
    wide, whole = rows + 2 * SIDE, rows + 2 * STEP
    shape = jax.ShapeDtypeStruct

    forward = [(i, i + 1) for i in range(n_seq - 1)]
    backward = [(target, source) for source, target in forward]
    low = lax.ppermute(x[rows - STEP :], "seq", forward)
    high = lax.ppermute(x[:STEP], "seq", backward)
    core = lax.axis_index("ep") % 2
    place = jnp.stack([lax.axis_index("seq") * rows, lengths[0], core]).astype(jnp.int32)

    own = shape((rows, width), BF16)
    normed, sig, gate_slope, own_glu = call(project_kernel, [own] * 4, [], 2, 2 * rows * width * width * 2)(
        place, x, w_in
    )
    glu, act, slope, resid, sums = call(
        forward_kernel,
        [
            shape((whole, width), BF16),
            shape((wide, width), BF16),
            shape((wide, width), BF16),
            shape((wide, width), F32),
            shape((n_seq, n_heads, width + LANES), F32),
        ],
        [pltpu.VMEM((whole, width), F32)],
        8,
        2 * rows * width * width * 4,
    )(place, low, high, x, own_glu, w_in, kernel, w_out, pool_query)
    sums = lax.all_to_all(sums, "seq", 0, 0)

    small_rows = 48
    payload = shape((n_ep // 2, width + width // 2 + small_rows, LANES), BF16)
    episode, mine, other = call(
        backward_kernel,
        [shape((16, width), F32), payload, payload],
        [
            pltpu.VMEM((wide, width), F32),
            pltpu.VMEM((whole, width), F32),
            pltpu.VMEM((wide, width), BF16),
            pltpu.VMEM((rows, 2 * width), BF16),
            pltpu.VMEM((width, 2 * width), BF16),
            pltpu.VMEM((n_taps, 8, width), F32),
            pltpu.VMEM((small_rows, width), F32),
        ],
        14,
        2 * rows * width * width * 8,
    )(
        place, sums, w_value, text_emb, teacher, pool_query, resid, act, slope,
        glu, normed, sig, gate_slope, w_out, kernel,
    )

    half = small_rows // 2
    big = width + width // 2

    def packed(total):
        share = total[..., big : big + half, :] + total[..., big + half :, :]
        return total[..., :big, :].astype(BF16), pair(share, -2)

    got = lax.ppermute(other, "ep", [(i, i ^ 1) for i in range(n_ep)])
    total = mine.astype(F32) + got.astype(F32)
    groups = [[2 * y + c for y in range(n_ep // 2)] for c in range(2)]
    got = lax.all_to_all(
        jnp.concatenate(packed(total), axis=-2), "ep", 0, 0, axis_index_groups=groups
    )
    grads, share = packed(jnp.sum(got.astype(F32), axis=0))
    in_rows = width // n_seq
    out_rows = in_rows // 2
    got = lax.all_to_all(
        jnp.concatenate(
            [
                grads[:width].reshape(n_seq, in_rows, LANES),
                grads[width:].reshape(n_seq, out_rows, LANES),
                jnp.broadcast_to(share[None], (n_seq, *share.shape)),
            ],
            axis=1,
        ),
        "seq",
        0,
        0,
    )
    total = jnp.sum(got.astype(F32), axis=0)
    grad_in = total[:in_rows]
    grad_out = total[in_rows : in_rows + out_rows]
    grad_out = jnp.concatenate([grad_out[:, : LANES // 2], grad_out[:, LANES // 2 :]], axis=0)
    share = total[in_rows + out_rows :]
    share = share[:half] + share[half:]
    last = jnp.concatenate([share, episode.reshape(-1, LANES)], axis=0)
    last = lax.all_to_all(jnp.broadcast_to(last[None], (n_ep, *last.shape)), "ep", 0, 0)
    small = last[:, :half].reshape(width // LANES, small_rows, LANES)
    small = small.transpose(1, 0, 2).reshape(small_rows, width)
    grad_query, grad_kernel = small[:n_heads], small[n_heads : n_heads + n_taps]
    episodes = last[:, half:].reshape(n_ep, 16, width)
    loss = jnp.sum(episodes[:, n_heads + 1, 0])
    grad_value = jnp.einsum(
        "ehd,ehk->dhk",
        episodes[:, :n_heads],
        episodes[:, n_heads].reshape(n_ep, n_heads, width // n_heads),
        precision=lax.Precision.HIGHEST,
    ).reshape(width, width)
    return (loss, grad_in, grad_out, grad_kernel, grad_query, grad_value)


def solution(mesh):
    return jax.shard_map(
        shards,
        mesh=mesh,
        in_specs=(P("ep", "seq", None), P("ep"), P(), P(), P(), P(), P(), P(), P("ep", None)),
        out_specs=(P(), P("seq", "ep"), P("seq", "ep"), P(), P(), P()),
        check_vma=False,
    )
```

```python
import functools

import jax
import jax.numpy as jnp
from jax import lax
from jax.experimental import pallas as pl
from jax.experimental.pallas import tpu as pltpu
from jax.sharding import PartitionSpec as P

F32, BF16 = jnp.float32, jnp.bfloat16
NN = (((1,), (0,)), ((), ()))
NT = (((1,), (1,)), ((), ()))
TN = (((0,), (0,)), ((), ()))
LANES = 128
STEP = 32
SIDE = 16


def dot(a, b, dims=NN):
    return lax.dot_general(a, b, dims, preferred_element_type=F32)


def split3(value):
    high = value.astype(BF16)
    rest = value - high.astype(F32)
    mid = rest.astype(BF16)
    return high, mid, (rest - mid.astype(F32)).astype(BF16)


def stacked(value):
    return jnp.concatenate(split3(value), axis=0)


def folded(value, count=3, rows=8):
    total = value[0:rows]
    for i in range(1, count):
        total = total + value[i * rows : (i + 1) * rows]
    return total


def lane_groups(shape, pieces):
    group = lax.broadcasted_iota(jnp.int32, shape, 1) // 8
    out = jnp.zeros(shape, F32)
    for g, piece in enumerate(pieces):
        out = jnp.where(group == g, piece.astype(F32), out)
    return out.astype(BF16)


def across(column):
    lane = lax.broadcasted_iota(jnp.int32, (8, LANES), 1)
    head = lax.broadcasted_iota(jnp.int32, (8, LANES), 0)
    return jnp.sum(jnp.where(lane % 8 == head, column, 0.0), axis=0, keepdims=True)


def down(row):
    lane = lax.broadcasted_iota(jnp.int32, (8, LANES), 1)
    head = lax.broadcasted_iota(jnp.int32, (8, LANES), 0)
    return jnp.sum(jnp.where(lane == head, row, 0.0), axis=1, keepdims=True)


def gated(x, w_in, width):
    xf = x.astype(F32)
    centred = xf - jnp.mean(xf, axis=-1, keepdims=True)
    var = jnp.mean(centred * centred, axis=-1, keepdims=True)
    normed = (centred * lax.rsqrt(var + 1e-05)).astype(BF16)
    mixed = dot(normed, w_in)
    return normed, mixed[:, :width], jax.nn.sigmoid(mixed[:, width:])


def row_mask(first, rows, length):
    at = first + lax.broadcasted_iota(jnp.int32, (rows, 1), 0)
    return (at >= 0) & (at < length)


def project_kernel(place, x_ref, w_in_ref, normed_ref, sig_ref, slope_ref, glu_ref):
    rows, width = x_ref.shape
    chunk = rows // 4
    for i in range(4):
        part = pl.ds(i * chunk, chunk)
        normed, gate, sig = gated(x_ref[part, :], w_in_ref[...], width)
        valid = row_mask(place[0] + i * chunk, chunk, place[1])
        normed_ref[part, :] = normed
        sig_ref[part, :] = sig.astype(BF16)
        both = gate * sig
        slope_ref[part, :] = (both * (1.0 - sig)).astype(BF16)
        glu_ref[part, :] = jnp.where(valid, both, 0.0).astype(BF16)


def shifted(block):
    rows = block.shape[0]
    return [block if s == 0 else pltpu.roll(block, rows - s, 0) for s in range(8)]


def forward_kernel(
    place, low_ref, high_ref, x_ref, own_glu_ref, w_in_ref, taps_ref, w_out_ref, query_ref,
    glu_ref, act_ref, slope_ref, resid_ref, sums_ref, glu_f,
):
    rows, width = x_ref.shape
    wide = rows + 2 * SIDE
    n_taps = taps_ref.shape[0]
    halo = jnp.concatenate([low_ref[...], high_ref[...]], axis=0)
    unused, gate, sig = gated(halo, w_in_ref[...], width)
    both = gate * sig
    valid_low = row_mask(place[0] - STEP, STEP, place[1])
    valid_high = row_mask(place[0] + rows, STEP, place[1])
    low = jnp.where(valid_low, both[:STEP], 0.0).astype(BF16)
    high = jnp.where(valid_high, both[STEP:], 0.0).astype(BF16)
    glu_ref[0:STEP, :] = low
    glu_ref[STEP : STEP + rows, :] = own_glu_ref[...]
    glu_ref[STEP + rows :, :] = high
    glu_f[0:STEP, :] = low.astype(F32)
    glu_f[STEP : STEP + rows, :] = own_glu_ref[...].astype(F32)
    glu_f[STEP + rows :, :] = high.astype(F32)

    @pl.loop(0, wide // STEP)
    def _(i):
        start = pl.multiple_of(i * STEP, STEP)
        for c in range(width // LANES):
            cols = slice(c * LANES, (c + 1) * LANES)
            views = shifted(glu_f[pl.ds(start, 2 * STEP), cols])
            acc = jnp.zeros((STEP, LANES), F32)
            for k in range(n_taps):
                q, s = divmod(k + 1, 8)
                acc = acc + taps_ref[k : k + 1, cols] * views[s][8 * q : 8 * q + STEP]
            s = jax.nn.sigmoid(acc)
            act_ref[pl.ds(start, STEP), cols] = (acc * s).astype(BF16)
            slope_ref[pl.ds(start, STEP), cols] = (s * (1.0 + acc * (1.0 - s))).astype(BF16)

    w_out = w_out_ref[...]
    resid_ref[0:SIDE, :] = low_ref[STEP - SIDE :, :].astype(F32) + dot(act_ref[0:SIDE, :], w_out)
    resid_ref[SIDE + rows :, :] = high_ref[0:SIDE, :].astype(F32) + dot(
        act_ref[SIDE + rows :, :], w_out
    )
    queries = jnp.concatenate([query_ref[...]] * (LANES // 8), axis=0)
    root = jnp.sqrt(jnp.float32(width))
    parts = 2
    chunk = rows // parts
    scores = []
    for i in range(parts):
        own = pl.ds(SIDE + i * chunk, chunk)
        resid = x_ref[pl.ds(i * chunk, chunk), :].astype(F32) + dot(act_ref[own, :], w_out)
        resid_ref[own, :] = resid
        score = sum(dot(piece, queries, NT) for piece in split3(resid)) / root
        valid = row_mask(place[0] + i * chunk, chunk, place[1])
        scores.append(jnp.where(valid, score, -1e30))
    top = functools.reduce(
        jnp.maximum, [jnp.max(score, axis=0, keepdims=True) for score in scores]
    )
    total = jnp.zeros((1, LANES), F32)
    vec = jnp.zeros((LANES, width), F32)
    for i in range(parts):
        valid = row_mask(place[0] + i * chunk, chunk, place[1])
        expo = jnp.where(valid, jnp.exp(scores[i] - top), 0.0)
        total = total + jnp.sum(expo, axis=0, keepdims=True)
        weights = lane_groups(expo.shape, split3(expo))
        for piece in split3(resid_ref[pl.ds(SIDE + i * chunk, chunk), :]):
            vec = vec + dot(weights, piece, TN)
    lane = lax.broadcasted_iota(jnp.int32, (8, LANES), 1)
    sums = jnp.concatenate(
        [folded(vec), jnp.where(lane == 0, down(top), down(total))], axis=1
    )

    @pl.loop(0, sums_ref.shape[0])
    def _(i):
        sums_ref[i] = sums


def backward_kernel(
    place, sums_ref, w_value_ref, text_ref, teacher_ref, query_ref, resid_ref, act_ref, slope_ref,
    glu_ref, normed_ref, sig_ref, gate_slope_ref, w_out_ref, taps_ref,
    mine_ref, other_ref,
    dconv_f, glu_f, dresid_s, dmixed_s, in_s, tap_s, small_s,
):
    rows, width = normed_ref.shape
    wide = rows + 2 * SIDE
    n_taps = taps_ref.shape[0]
    n_cands = text_ref.shape[0]
    head_dim = width // 8
    root = jnp.sqrt(jnp.float32(width))

    stats = sums_ref[:, :, width:]
    tops, totals = stats[:, :, 0:1], stats[:, :, 1:2]
    top = jnp.max(tops, axis=0)
    scale = jnp.exp(tops - top[None])
    total = jnp.sum(scale * totals, axis=0)
    vbar = jnp.sum(scale * sums_ref[:, :, :width], axis=0) / total
    at = lax.broadcasted_iota(jnp.int32, (8, width), 1) // head_dim
    own_head = at == lax.broadcasted_iota(jnp.int32, (8, width), 0)
    w_value = w_value_ref[...]
    texts = text_ref[...]
    full = folded(dot(stacked(vbar), w_value))
    pooled = jnp.sum(jnp.where(own_head, full, 0.0), axis=0, keepdims=True)
    pooled = jnp.broadcast_to(pooled, (8, width))
    rms = jnp.sqrt(jnp.mean(pooled * pooled, axis=-1, keepdims=True) + 1e-06)
    emb = pooled / rms
    diff = folded(dot(stacked(emb), texts, NT)) / root - teacher_ref[...]
    loss = jnp.sum(diff * diff, axis=-1, keepdims=True) / n_cands
    demb = folded(dot(stacked(2.0 * diff / n_cands), texts)) / root
    dpooled = (demb - emb * jnp.mean(demb * emb, axis=-1, keepdims=True)) / rms
    dvbar = folded(dot(stacked(jnp.where(own_head, dpooled, 0.0)), w_value, NT))
    centre = jnp.sum(dvbar * vbar, axis=-1, keepdims=True)
    row = lax.broadcasted_iota(jnp.int32, (8, width), 0)
    loss_high = loss.astype(BF16).astype(F32)
    rest = jnp.where(row == 4, loss_high, jnp.where(row == 5, loss - loss_high, 0.0))[:, :LANES]
    blocks = [slice(c * LANES, (c + 1) * LANES) for c in range(width // LANES)]
    for c, cols in enumerate(blocks):
        rest = jnp.where(row[:, :LANES] == c, dpooled[:, cols], rest)
    episode = jnp.concatenate([*[vbar[:, cols] for cols in blocks], rest], axis=0)

    top_l, total_l, centre_l = across(top), across(total), across(centre)
    query = query_ref[...]
    queries = jnp.concatenate([query] * (LANES // 8), axis=0)
    d_high, d_mid, d_low = split3(dvbar)
    many = lambda piece: jnp.concatenate([piece] * (LANES // 8), axis=0)
    dv_high, dv_mid, dv_low = many(d_high), many(d_mid), many(d_low)
    mixing = jnp.concatenate(
        [d_high, d_mid, d_high, d_mid, query, query, query, jnp.zeros((LANES - 56, width), BF16)],
        axis=0,
    )
    w_out = w_out_ref[...]
    parts = 2
    chunk = wide // parts
    grad_query = jnp.zeros((LANES, width), F32)
    for i in range(parts):
        here = pl.ds(i * chunk, chunk)
        r_high, r_mid, r_low = split3(resid_ref[here, :])
        score = (dot(r_high, queries, NT) + dot(r_mid, queries, NT) + dot(r_low, queries, NT)) / root
        valid = row_mask(place[0] - SIDE + i * chunk, chunk, place[1])
        probs = jnp.where(valid, jnp.exp(score - top_l), 0.0) / total_l
        proj = dot(r_high, dv_high, NT) + (dot(r_high, dv_mid, NT) + dot(r_mid, dv_high, NT))
        proj = proj + (
            dot(r_high, dv_low, NT) + dot(r_mid, dv_mid, NT) + dot(r_low, dv_high, NT)
        )
        dscores = probs * (proj - centre_l) / root
        p_high, p_mid, unused = split3(probs)
        s_pieces = split3(dscores)
        mixed = lane_groups(probs.shape, (p_high, p_high, p_mid, p_mid, *s_pieces))
        dresid = dot(mixed, mixing).astype(BF16)
        dresid_s[here, :] = dresid
        own = lax.broadcasted_iota(jnp.int32, (chunk, 1), 0) + i * chunk
        own = (own >= SIDE) & (own < SIDE + rows)
        weights = lane_groups(probs.shape, s_pieces)
        weights = jnp.where(own, weights.astype(F32), 0.0).astype(BF16)
        for piece in (r_high, r_mid, r_low):
            grad_query = grad_query + dot(weights, piece, TN)
        dact = dot(dresid, w_out, NT)
        dconv = (dact * slope_ref[here, :].astype(F32)).astype(BF16)
        dconv_f[here, :] = dconv.astype(F32)
    query_sum = folded(grad_query)
    high = query_sum.astype(BF16).astype(F32)
    half = small_s.shape[0] // 2
    small_s[0:8, :] = jnp.where(row < 4, high, pltpu.roll(query_sum - high, 4, 0))
    small_s[half : half + 8, :] = jnp.where(row < 4, pltpu.roll(high, 4, 0), query_sum - high)

    glu_f[...] = glu_ref[...].astype(F32)
    tap_s[...] = jnp.zeros_like(tap_s)

    @pl.loop(0, rows // STEP)
    def _(i):
        start = pl.multiple_of(i * STEP, STEP)
        valid = row_mask(place[0] + start, STEP, place[1])
        for c in range(width // LANES):
            cols = slice(c * LANES, (c + 1) * LANES)
            views = shifted(dconv_f[pl.ds(start, 2 * STEP), cols])
            acc = jnp.zeros((STEP, LANES), F32)
            for k in range(n_taps):
                q, s = divmod(n_taps - k, 8)
                acc = acc + taps_ref[k : k + 1, cols] * views[s][8 * q : 8 * q + STEP]
            dglu = jnp.where(valid, acc, 0.0)
            here = pl.ds(start, STEP)
            dmixed_s[here, cols] = (dglu * sig_ref[here, cols].astype(F32)).astype(BF16)
            dmixed_s[here, slice(width + c * LANES, width + (c + 1) * LANES)] = (
                dglu * gate_slope_ref[here, cols].astype(F32)
            ).astype(BF16)
            own = views[0][SIDE : SIDE + STEP]
            views = shifted(glu_f[pl.ds(start + SIDE, 2 * STEP), cols])
            for k in range(n_taps):
                q, s = divmod(k + 1, 8)
                product = own * views[s][8 * q : 8 * q + STEP]
                tap_s[k, :, cols] += folded(product, STEP // 8)

    tap_sum = jnp.sum(tap_s[...], axis=1)
    small_s[8:half, :] = tap_sum[: half - 8]
    small_s[half + 8 :, :] = tap_sum[half - 8 :]

    grad_out = dot(act_ref[SIDE : SIDE + rows, :], dresid_s[SIDE : SIDE + rows, :], TN)
    in_s[...] = dot(normed_ref[...], dmixed_s[...], TN).astype(BF16)
    core = place[2]
    halves = grad_out.reshape(width // 16, 2, 8, width)
    first, second = (halves[:, j].reshape(width // 2, width) for j in range(2))
    low_lane = lax.broadcasted_iota(jnp.int32, (width // 2, LANES), 1) < LANES // 2
    for y in range(width // LANES):
        a = first[:, y * LANES : (y + 1) * LANES]
        b = second[:, y * LANES : (y + 1) * LANES]
        even = jnp.where(low_lane, a, pltpu.roll(b, LANES // 2, 1))
        odd = jnp.where(low_lane, pltpu.roll(a, LANES // 2, 1), b)
        for ref, which, block in (
            (mine_ref, core, jnp.where(core == 0, even, odd)),
            (other_ref, 1 - core, jnp.where(core == 0, odd, even)),
        ):
            at = pl.multiple_of((2 * y + which) * LANES, LANES)
            ref[y, 0:width, :] = in_s[:, pl.ds(at, LANES)]
            ref[y, width : width + width // 2, :] = block.astype(BF16)
            share = small_s[pl.ds(pl.multiple_of(which * half, 8), half), y * LANES : (y + 1) * LANES]
            ref[y, width + width // 2 :, :] = jnp.concatenate([share, episode], axis=0).astype(BF16)


def paired(rows):
    row = lax.broadcasted_iota(jnp.int32, rows.shape, 0)
    value = rows + pltpu.roll(rows, 4, 0)
    high = value.astype(BF16).astype(F32)
    return jnp.where(row < 4, high, value - high)


def cores_kernel(big, half, mine_ref, got_ref, out_ref):
    for y in range(mine_ref.shape[0]):
        total = mine_ref[y, 0:big, :].astype(F32) + got_ref[y, 0:big, :].astype(F32)
        out_ref[y, 0:big, :] = total.astype(BF16)
        mine, got = mine_ref[y, big:, :].astype(F32), got_ref[y, big:, :].astype(F32)
        share = mine[:half] + got[:half]
        out_ref[y, big:, :] = jnp.concatenate(
            [paired(share[:8]), share[8:], mine[half:], got[half:], jnp.zeros((8, LANES), F32)],
            axis=0,
        ).astype(BF16)


def rows_kernel(big, half, got_ref, out_ref):
    n_y, n_seq = got_ref.shape[0], out_ref.shape[0]
    total = got_ref[0, 0:big, :].astype(F32)
    share = got_ref[0, big:, :].astype(F32)[:half]
    for y in range(1, n_y):
        total = total + got_ref[y, 0:big, :].astype(F32)
        share = share + got_ref[y, big:, :].astype(F32)[:half]
    share = jnp.concatenate([paired(share[:8]), share[8:]], axis=0)
    split = 2 * big // 3
    out_ref[...] = jnp.concatenate(
        [
            total[:split].reshape(n_seq, split // n_seq, LANES),
            total[split:].reshape(n_seq, (big - split) // n_seq, LANES),
            jnp.broadcast_to(share[None], (n_seq, half, LANES)),
        ],
        axis=1,
    ).astype(BF16)


def value_kernel(big, half, got_ref, grad_ref, loss_ref):
    width = grad_ref.shape[0]
    head = lax.broadcasted_iota(jnp.int32, (8, width), 1) // (width // 8)
    own_head = head == lax.broadcasted_iota(jnp.int32, (8, width), 0)
    vectors, others = [], []
    loss = jnp.zeros((1, LANES), F32)
    n_blocks = width // LANES
    size = 8 * (n_blocks + 1)
    for y in range(got_ref.shape[0]):
        rows = got_ref[y, big:, :].astype(F32)
        for start in (half, half + size):
            episode = rows[start : start + size]
            rest = episode[8 * n_blocks :]
            vectors.append(
                jnp.concatenate([episode[8 * c : 8 * c + 8] for c in range(n_blocks)], axis=1)
            )
            dpooled = jnp.concatenate([rest[c : c + 1] for c in range(n_blocks)], axis=1)
            others.append(jnp.where(own_head, dpooled, 0.0))
            loss = loss + rest[4:5] + rest[5:6]
    vectors, others = (jnp.concatenate(v, axis=0).astype(BF16) for v in (vectors, others))
    grad_ref[...] = dot(vectors, others, TN)
    loss_ref[...] = loss


def owner_kernel(got_ref, grad_in_ref, grad_out_ref, out_ref):
    total = got_ref[0].astype(F32)
    for s in range(1, got_ref.shape[0]):
        total = total + got_ref[s].astype(F32)
    in_rows, cols = grad_in_ref.shape[0], grad_out_ref.shape[1]
    out_rows = grad_out_ref.shape[0] // 2
    grad_in_ref[...] = total[:in_rows]
    pair_rows = total[in_rows : in_rows + out_rows]
    grad_out_ref[0:out_rows, :] = pair_rows[:, :cols]
    grad_out_ref[out_rows:, :] = pair_rows[:, cols:]
    share = total[in_rows + out_rows :]
    share = jnp.concatenate([share[:8] + pltpu.roll(share[:8], 4, 0), share[8:]], axis=0)
    for e in range(out_ref.shape[0]):
        out_ref[e] = share


def last_kernel(got_ref, taps_ref, query_ref):
    n_taps = taps_ref.shape[0]
    for y in range(got_ref.shape[0] // 2):
        cols = slice(y * LANES, (y + 1) * LANES)
        first, second = got_ref[2 * y], got_ref[2 * y + 1]
        row = lax.broadcasted_iota(jnp.int32, (8, LANES), 0)
        query_ref[:, cols] = jnp.where(row < 4, first[:8], second[:8])
        taps_ref[0:16, cols] = first[8:]
        taps_ref[16:n_taps, cols] = second[8 : 8 + n_taps - 16]


def call(kernel, outs, scratch, n_args, flops, placed=True):
    vmem = pl.BlockSpec(memory_space=pltpu.VMEM)
    return pl.pallas_call(
        kernel,
        out_shape=outs,
        in_specs=[pl.BlockSpec(memory_space=pltpu.SMEM)] * placed + [vmem] * n_args,
        out_specs=[vmem] * len(outs),
        scratch_shapes=scratch,
        compiler_params=pltpu.CompilerParams(vmem_limit_bytes=48 * 2**20),
        cost_estimate=pl.CostEstimate(flops=flops, bytes_accessed=8 * 2**20, transcendentals=2**20),
    )


def shards(frames, lengths, w_in, kernel, w_out, pool_query, w_value, text_emb, teacher):
    n_ep, n_seq = lax.axis_size("ep"), lax.axis_size("seq")
    x = frames[0]
    rows, width = x.shape
    n_taps, n_heads = kernel.shape[0], pool_query.shape[0]
    wide, whole = rows + 2 * SIDE, rows + 2 * STEP
    shape = jax.ShapeDtypeStruct

    forward = [(i, i + 1) for i in range(n_seq - 1)]
    backward = [(target, source) for source, target in forward]
    low = lax.ppermute(x[rows - STEP :], "seq", forward)
    high = lax.ppermute(x[:STEP], "seq", backward)
    core = lax.axis_index("ep") % 2
    place = jnp.stack([lax.axis_index("seq") * rows, lengths[0], core]).astype(jnp.int32)

    own = shape((rows, width), BF16)
    normed, sig, gate_slope, own_glu = call(project_kernel, [own] * 4, [], 2, 2 * rows * width * width * 2)(
        place, x, w_in
    )
    glu, act, slope, resid, sums = call(
        forward_kernel,
        [
            shape((whole, width), BF16),
            shape((wide, width), BF16),
            shape((wide, width), BF16),
            shape((wide, width), F32),
            shape((n_seq, n_heads, width + LANES), F32),
        ],
        [pltpu.VMEM((whole, width), F32)],
        8,
        2 * rows * width * width * 4,
    )(place, low, high, x, own_glu, w_in, kernel, w_out, pool_query)
    sums = lax.all_to_all(sums, "seq", 0, 0)

    small_rows = 48
    half = small_rows // 2
    big = width + width // 2
    n_y = n_ep // 2
    size = 8 * (width // LANES + 1)
    payload = shape((n_y, big + half + size, LANES), BF16)
    mine, other = call(
        backward_kernel,
        [payload, payload],
        [
            pltpu.VMEM((wide, width), F32),
            pltpu.VMEM((whole, width), F32),
            pltpu.VMEM((wide, width), BF16),
            pltpu.VMEM((rows, 2 * width), BF16),
            pltpu.VMEM((width, 2 * width), BF16),
            pltpu.VMEM((n_taps + 1, 8, width), F32),
            pltpu.VMEM((small_rows, width), F32),
        ],
        14,
        2 * rows * width * width * 8,
    )(
        place, sums, w_value, text_emb, teacher, pool_query, resid, act, slope,
        glu, normed, sig, gate_slope, w_out, kernel,
    )

    light = functools.partial(call, scratch=[], flops=2**20, placed=False)
    got = lax.ppermute(other, "ep", [(i, i ^ 1) for i in range(n_ep)])
    (total,) = light(
        functools.partial(cores_kernel, big, half),
        [shape((n_y, big + half + 2 * size + 8, LANES), BF16)],
        n_args=2,
    )(mine, got)
    groups = [[2 * y + c for y in range(n_y)] for c in range(2)]
    got = lax.all_to_all(total, "ep", 0, 0, axis_index_groups=groups)
    (total,) = light(
        functools.partial(rows_kernel, big, half),
        [shape((n_seq, big // n_seq + half, LANES), BF16)],
        n_args=1,
    )(got)
    grad_value, loss = light(
        functools.partial(value_kernel, big, half),
        [shape((width, width), F32), shape((1, LANES), F32)],
        n_args=1,
    )(got)
    loss = loss[0, 0]
    got = lax.all_to_all(total, "seq", 0, 0)
    grad_in, grad_out, share = light(
        owner_kernel,
        [
            shape((width // n_seq, 2 * width // n_ep), F32),
            shape((width // n_seq, width // n_ep), F32),
            shape((n_ep, half, LANES), F32),
        ],
        n_args=1,
    )(got)
    got = lax.all_to_all(share, "ep", 0, 0)
    grad_kernel, grad_query = light(
        last_kernel, [shape((n_taps, width), F32), shape((n_heads, width), F32)], n_args=1
    )(got)
    return (loss, grad_in, grad_out, grad_kernel, grad_query, grad_value)


def solution(mesh):
    return jax.shard_map(
        shards,
        mesh=mesh,
        in_specs=(P("ep", "seq", None), P("ep"), P(), P(), P(), P(), P(), P(), P("ep", None)),
        out_specs=(P(), P("seq", "ep"), P("seq", "ep"), P(), P(), P()),
        check_vma=False,
    )
```

```python
import functools

import jax
import jax.numpy as jnp
from jax import lax
from jax.experimental import pallas as pl
from jax.experimental.pallas import tpu as pltpu
from jax.sharding import PartitionSpec as P

F32, BF16 = jnp.float32, jnp.bfloat16
NN = (((1,), (0,)), ((), ()))
NT = (((1,), (1,)), ((), ()))
TN = (((0,), (0,)), ((), ()))
LANES = 128
STEP = 32
SIDE = 16


def dot(a, b, dims=NN):
    return lax.dot_general(a, b, dims, preferred_element_type=F32)


def split3(value):
    high = value.astype(BF16)
    rest = value - high.astype(F32)
    mid = rest.astype(BF16)
    return high, mid, (rest - mid.astype(F32)).astype(BF16)


def stacked(value):
    return jnp.concatenate(split3(value), axis=0)


def folded(value, count=3, rows=8):
    total = value[0:rows]
    for i in range(1, count):
        total = total + value[i * rows : (i + 1) * rows]
    return total


def lane_groups(shape, pieces):
    group = lax.broadcasted_iota(jnp.int32, shape, 1) // 8
    out = jnp.zeros(shape, F32)
    for g, piece in enumerate(pieces):
        out = jnp.where(group == g, piece.astype(F32), out)
    return out.astype(BF16)


def across(column):
    lane = lax.broadcasted_iota(jnp.int32, (8, LANES), 1)
    head = lax.broadcasted_iota(jnp.int32, (8, LANES), 0)
    return jnp.sum(jnp.where(lane % 8 == head, column, 0.0), axis=0, keepdims=True)


def down(row):
    lane = lax.broadcasted_iota(jnp.int32, (8, LANES), 1)
    head = lax.broadcasted_iota(jnp.int32, (8, LANES), 0)
    return jnp.sum(jnp.where(lane == head, row, 0.0), axis=1, keepdims=True)


def gated(x, w_in, width):
    xf = x.astype(F32)
    centred = xf - jnp.mean(xf, axis=-1, keepdims=True)
    var = jnp.mean(centred * centred, axis=-1, keepdims=True)
    normed = (centred * lax.rsqrt(var + 1e-05)).astype(BF16)
    mixed = dot(normed, w_in)
    return normed, mixed[:, :width], jax.nn.sigmoid(mixed[:, width:])


def row_mask(first, rows, length):
    at = first + lax.broadcasted_iota(jnp.int32, (rows, 1), 0)
    return (at >= 0) & (at < length)


def project_kernel(place, x_ref, w_in_ref, normed_ref, sig_ref, slope_ref, glu_ref):
    rows, width = x_ref.shape
    chunk = rows // 4
    for i in range(4):
        part = pl.ds(i * chunk, chunk)
        normed, gate, sig = gated(x_ref[part, :], w_in_ref[...], width)
        valid = row_mask(place[0] + i * chunk, chunk, place[1])
        normed_ref[part, :] = normed
        sig_ref[part, :] = sig.astype(BF16)
        both = gate * sig
        slope_ref[part, :] = (both * (1.0 - sig)).astype(BF16)
        glu_ref[part, :] = jnp.where(valid, both, 0.0).astype(BF16)


def shifted(block):
    rows = block.shape[0]
    return [block if s == 0 else pltpu.roll(block, rows - s, 0) for s in range(8)]


def forward_kernel(
    place, low_ref, high_ref, x_ref, own_glu_ref, w_in_ref, taps_ref, w_out_ref, query_ref,
    glu_ref, act_ref, slope_ref, resid_ref, sums_ref, glu_f,
):
    rows, width = x_ref.shape
    wide = rows + 2 * SIDE
    n_taps = taps_ref.shape[0]
    halo = jnp.concatenate([low_ref[...], high_ref[...]], axis=0)
    unused, gate, sig = gated(halo, w_in_ref[...], width)
    both = gate * sig
    valid_low = row_mask(place[0] - STEP, STEP, place[1])
    valid_high = row_mask(place[0] + rows, STEP, place[1])
    low = jnp.where(valid_low, both[:STEP], 0.0).astype(BF16)
    high = jnp.where(valid_high, both[STEP:], 0.0).astype(BF16)
    glu_ref[0:STEP, :] = low
    glu_ref[STEP : STEP + rows, :] = own_glu_ref[...]
    glu_ref[STEP + rows :, :] = high
    glu_f[0:STEP, :] = low.astype(F32)
    glu_f[STEP : STEP + rows, :] = own_glu_ref[...].astype(F32)
    glu_f[STEP + rows :, :] = high.astype(F32)

    @pl.loop(0, wide // STEP)
    def _(i):
        start = pl.multiple_of(i * STEP, STEP)
        for c in range(width // LANES):
            cols = slice(c * LANES, (c + 1) * LANES)
            views = shifted(glu_f[pl.ds(start, 2 * STEP), cols])
            acc = jnp.zeros((STEP, LANES), F32)
            for k in range(n_taps):
                q, s = divmod(k + 1, 8)
                acc = acc + taps_ref[k : k + 1, cols] * views[s][8 * q : 8 * q + STEP]
            s = jax.nn.sigmoid(acc)
            act_ref[pl.ds(start, STEP), cols] = (acc * s).astype(BF16)
            slope_ref[pl.ds(start, STEP), cols] = (s * (1.0 + acc * (1.0 - s))).astype(BF16)

    w_out = w_out_ref[...]
    resid_ref[0:SIDE, :] = low_ref[STEP - SIDE :, :].astype(F32) + dot(act_ref[0:SIDE, :], w_out)
    resid_ref[SIDE + rows :, :] = high_ref[0:SIDE, :].astype(F32) + dot(
        act_ref[SIDE + rows :, :], w_out
    )
    queries = jnp.concatenate([query_ref[...]] * (LANES // 8), axis=0)
    root = jnp.sqrt(jnp.float32(width))
    parts = 2
    chunk = rows // parts
    scores = []
    for i in range(parts):
        own = pl.ds(SIDE + i * chunk, chunk)
        resid = x_ref[pl.ds(i * chunk, chunk), :].astype(F32) + dot(act_ref[own, :], w_out)
        resid_ref[own, :] = resid
        score = sum(dot(piece, queries, NT) for piece in split3(resid)) / root
        valid = row_mask(place[0] + i * chunk, chunk, place[1])
        scores.append(jnp.where(valid, score, -1e30))
    top = functools.reduce(
        jnp.maximum, [jnp.max(score, axis=0, keepdims=True) for score in scores]
    )
    total = jnp.zeros((1, LANES), F32)
    vec = jnp.zeros((LANES, width), F32)
    for i in range(parts):
        valid = row_mask(place[0] + i * chunk, chunk, place[1])
        expo = jnp.where(valid, jnp.exp(scores[i] - top), 0.0)
        total = total + jnp.sum(expo, axis=0, keepdims=True)
        weights = lane_groups(expo.shape, split3(expo))
        for piece in split3(resid_ref[pl.ds(SIDE + i * chunk, chunk), :])[:2]:
            vec = vec + dot(weights, piece, TN)
    lane = lax.broadcasted_iota(jnp.int32, (8, LANES), 1)
    sums = jnp.concatenate(
        [folded(vec), jnp.where(lane == 0, down(top), down(total))], axis=1
    )

    @pl.loop(0, sums_ref.shape[0])
    def _(i):
        sums_ref[i] = sums


def backward_kernel(
    place, sums_ref, w_value_ref, text_ref, teacher_ref, query_ref, resid_ref, act_ref, slope_ref,
    glu_ref, normed_ref, sig_ref, gate_slope_ref, w_out_ref, taps_ref,
    mine_ref, other_ref,
    dconv_f, glu_f, dresid_s, dmixed_s, in_s, tap_s, small_s,
):
    rows, width = normed_ref.shape
    wide = rows + 2 * SIDE
    n_taps = taps_ref.shape[0]
    n_cands = text_ref.shape[0]
    head_dim = width // 8
    root = jnp.sqrt(jnp.float32(width))

    stats = sums_ref[:, :, width:]
    tops, totals = stats[:, :, 0:1], stats[:, :, 1:2]
    top = jnp.max(tops, axis=0)
    scale = jnp.exp(tops - top[None])
    total = jnp.sum(scale * totals, axis=0)
    vbar = jnp.sum(scale * sums_ref[:, :, :width], axis=0) / total
    at = lax.broadcasted_iota(jnp.int32, (8, width), 1) // head_dim
    own_head = at == lax.broadcasted_iota(jnp.int32, (8, width), 0)
    w_value = w_value_ref[...]
    texts = text_ref[...]
    full = folded(dot(stacked(vbar), w_value))
    pooled = jnp.sum(jnp.where(own_head, full, 0.0), axis=0, keepdims=True)
    pooled = jnp.broadcast_to(pooled, (8, width))
    rms = jnp.sqrt(jnp.mean(pooled * pooled, axis=-1, keepdims=True) + 1e-06)
    emb = pooled / rms
    diff = folded(dot(stacked(emb), texts, NT)) / root - teacher_ref[...]
    loss = jnp.sum(diff * diff, axis=-1, keepdims=True) / n_cands
    demb = folded(dot(stacked(2.0 * diff / n_cands), texts)) / root
    dpooled = (demb - emb * jnp.mean(demb * emb, axis=-1, keepdims=True)) / rms
    dvbar = folded(dot(stacked(jnp.where(own_head, dpooled, 0.0)), w_value, NT))
    centre = jnp.sum(dvbar * vbar, axis=-1, keepdims=True)
    row = lax.broadcasted_iota(jnp.int32, (8, width), 0)
    loss_high = loss.astype(BF16).astype(F32)
    rest = jnp.where(row == 4, loss_high, jnp.where(row == 5, loss - loss_high, 0.0))[:, :LANES]
    blocks = [slice(c * LANES, (c + 1) * LANES) for c in range(width // LANES)]
    for c, cols in enumerate(blocks):
        rest = jnp.where(row[:, :LANES] == c, dpooled[:, cols], rest)
    episode = jnp.concatenate([*[vbar[:, cols] for cols in blocks], rest], axis=0)

    top_l, total_l, centre_l = across(top), across(total), across(centre)
    query = query_ref[...]
    d_high, d_mid, d_low = split3(dvbar)
    many = lambda piece: [piece] * (LANES // 8)
    both = jnp.concatenate(many(query) + many(d_high), axis=0)
    queries, dv_mid = both[:LANES], jnp.concatenate(many(d_mid), axis=0)
    mixing = jnp.concatenate(
        [d_high, d_mid, d_high, d_mid, query, query, query, jnp.zeros((LANES - 56, width), BF16)],
        axis=0,
    )
    w_out = w_out_ref[...]
    parts = 2
    chunk = wide // parts
    grad_query = jnp.zeros((LANES, width), F32)
    for i in range(parts):
        here = pl.ds(i * chunk, chunk)
        r_high, r_mid, r_low = split3(resid_ref[here, :])
        products = dot(r_high, both, NT) + dot(r_mid, both, NT)
        score = (products[:, :LANES] + dot(r_low, queries, NT)) / root
        valid = row_mask(place[0] - SIDE + i * chunk, chunk, place[1])
        probs = jnp.where(valid, jnp.exp(score - top_l), 0.0) / total_l
        proj = products[:, LANES:] + dot(r_high, dv_mid, NT)
        dscores = probs * (proj - centre_l) / root
        p_high, p_mid, unused = split3(probs)
        s_pieces = split3(dscores)
        mixed = lane_groups(probs.shape, (p_high, p_high, p_mid, p_mid, *s_pieces))
        dresid = dot(mixed, mixing).astype(BF16)
        dresid_s[here, :] = dresid
        own = lax.broadcasted_iota(jnp.int32, (chunk, 1), 0) + i * chunk
        own = (own >= SIDE) & (own < SIDE + rows)
        weights = lane_groups(probs.shape, s_pieces)
        weights = jnp.where(own, weights.astype(F32), 0.0).astype(BF16)
        for piece in (r_high, r_mid):
            grad_query = grad_query + dot(weights, piece, TN)
        dact = dot(dresid, w_out, NT)
        dconv = (dact * slope_ref[here, :].astype(F32)).astype(BF16)
        dconv_f[here, :] = dconv.astype(F32)
    query_sum = folded(grad_query)
    high = query_sum.astype(BF16).astype(F32)
    half = small_s.shape[0] // 2
    small_s[0:8, :] = jnp.where(row < 4, high, pltpu.roll(query_sum - high, 4, 0))
    small_s[half : half + 8, :] = jnp.where(row < 4, pltpu.roll(high, 4, 0), query_sum - high)

    glu_f[...] = glu_ref[...].astype(F32)
    tap_s[...] = jnp.zeros_like(tap_s)

    @pl.loop(0, rows // STEP)
    def _(i):
        start = pl.multiple_of(i * STEP, STEP)
        valid = row_mask(place[0] + start, STEP, place[1])
        for c in range(width // LANES):
            cols = slice(c * LANES, (c + 1) * LANES)
            views = shifted(dconv_f[pl.ds(start, 2 * STEP), cols])
            acc = jnp.zeros((STEP, LANES), F32)
            for k in range(n_taps):
                q, s = divmod(n_taps - k, 8)
                acc = acc + taps_ref[k : k + 1, cols] * views[s][8 * q : 8 * q + STEP]
            dglu = jnp.where(valid, acc, 0.0)
            here = pl.ds(start, STEP)
            dmixed_s[here, cols] = (dglu * sig_ref[here, cols].astype(F32)).astype(BF16)
            dmixed_s[here, slice(width + c * LANES, width + (c + 1) * LANES)] = (
                dglu * gate_slope_ref[here, cols].astype(F32)
            ).astype(BF16)
            own = views[0][SIDE : SIDE + STEP]
            views = shifted(glu_f[pl.ds(start + SIDE, 2 * STEP), cols])
            for k in range(n_taps):
                q, s = divmod(k + 1, 8)
                product = own * views[s][8 * q : 8 * q + STEP]
                tap_s[k, :, cols] += folded(product, STEP // 8)

    tap_sum = jnp.sum(tap_s[...], axis=1)
    small_s[8:half, :] = tap_sum[: half - 8]
    small_s[half + 8 :, :] = tap_sum[half - 8 :]

    grad_out = dot(act_ref[SIDE : SIDE + rows, :], dresid_s[SIDE : SIDE + rows, :], TN)
    in_s[...] = dot(normed_ref[...], dmixed_s[...], TN).astype(BF16)
    core = place[2]
    halves = grad_out.reshape(width // 16, 2, 8, width)
    first, second = (halves[:, j].reshape(width // 2, width) for j in range(2))
    low_lane = lax.broadcasted_iota(jnp.int32, (width // 2, LANES), 1) < LANES // 2
    for y in range(width // LANES):
        a = first[:, y * LANES : (y + 1) * LANES]
        b = second[:, y * LANES : (y + 1) * LANES]
        even = jnp.where(low_lane, a, pltpu.roll(b, LANES // 2, 1))
        odd = jnp.where(low_lane, pltpu.roll(a, LANES // 2, 1), b)
        for ref, which, block in (
            (mine_ref, core, jnp.where(core == 0, even, odd)),
            (other_ref, 1 - core, jnp.where(core == 0, odd, even)),
        ):
            at = pl.multiple_of((2 * y + which) * LANES, LANES)
            ref[y, 0:width, :] = in_s[:, pl.ds(at, LANES)]
            ref[y, width : width + width // 2, :] = block.astype(BF16)
            share = small_s[pl.ds(pl.multiple_of(which * half, 8), half), y * LANES : (y + 1) * LANES]
            ref[y, width + width // 2 :, :] = jnp.concatenate([share, episode], axis=0).astype(BF16)


def paired(rows):
    row = lax.broadcasted_iota(jnp.int32, rows.shape, 0)
    value = rows + pltpu.roll(rows, 4, 0)
    high = value.astype(BF16).astype(F32)
    return jnp.where(row < 4, high, value - high)


def cores_kernel(big, half, mine_ref, got_ref, out_ref):
    for y in range(mine_ref.shape[0]):
        total = mine_ref[y, 0:big, :].astype(F32) + got_ref[y, 0:big, :].astype(F32)
        out_ref[y, 0:big, :] = total.astype(BF16)
        mine, got = mine_ref[y, big:, :].astype(F32), got_ref[y, big:, :].astype(F32)
        share = mine[:half] + got[:half]
        out_ref[y, big:, :] = jnp.concatenate(
            [paired(share[:8]), share[8:], mine[half:], got[half:], jnp.zeros((8, LANES), F32)],
            axis=0,
        ).astype(BF16)


def rows_kernel(big, half, got_ref, out_ref):
    n_y, n_seq = got_ref.shape[0], out_ref.shape[0]
    total = got_ref[0, 0:big, :].astype(F32)
    share = got_ref[0, big:, :].astype(F32)[:half]
    for y in range(1, n_y):
        total = total + got_ref[y, 0:big, :].astype(F32)
        share = share + got_ref[y, big:, :].astype(F32)[:half]
    share = jnp.concatenate([paired(share[:8]), share[8:]], axis=0)
    split = 2 * big // 3
    out_ref[...] = jnp.concatenate(
        [
            total[:split].reshape(n_seq, split // n_seq, LANES),
            total[split:].reshape(n_seq, (big - split) // n_seq, LANES),
            jnp.broadcast_to(share[None], (n_seq, half, LANES)),
        ],
        axis=1,
    ).astype(BF16)


def value_kernel(big, half, got_ref, grad_ref, loss_ref):
    width = grad_ref.shape[0]
    head = lax.broadcasted_iota(jnp.int32, (8, width), 1) // (width // 8)
    own_head = head == lax.broadcasted_iota(jnp.int32, (8, width), 0)
    vectors, others = [], []
    loss = jnp.zeros((1, LANES), F32)
    n_blocks = width // LANES
    size = 8 * (n_blocks + 1)
    for y in range(got_ref.shape[0]):
        rows = got_ref[y, big:, :].astype(F32)
        for start in (half, half + size):
            episode = rows[start : start + size]
            rest = episode[8 * n_blocks :]
            vectors.append(
                jnp.concatenate([episode[8 * c : 8 * c + 8] for c in range(n_blocks)], axis=1)
            )
            dpooled = jnp.concatenate([rest[c : c + 1] for c in range(n_blocks)], axis=1)
            others.append(jnp.where(own_head, dpooled, 0.0))
            loss = loss + rest[4:5] + rest[5:6]
    vectors, others = (jnp.concatenate(v, axis=0).astype(BF16) for v in (vectors, others))
    grad_ref[...] = dot(vectors, others, TN)
    loss_ref[...] = loss


def owner_kernel(got_ref, grad_in_ref, grad_out_ref, out_ref):
    total = got_ref[0].astype(F32)
    for s in range(1, got_ref.shape[0]):
        total = total + got_ref[s].astype(F32)
    in_rows, cols = grad_in_ref.shape[0], grad_out_ref.shape[1]
    out_rows = grad_out_ref.shape[0] // 2
    grad_in_ref[...] = total[:in_rows]
    pair_rows = total[in_rows : in_rows + out_rows]
    grad_out_ref[0:out_rows, :] = pair_rows[:, :cols]
    grad_out_ref[out_rows:, :] = pair_rows[:, cols:]
    share = total[in_rows + out_rows :]
    share = jnp.concatenate([share[:8] + pltpu.roll(share[:8], 4, 0), share[8:]], axis=0)
    for e in range(out_ref.shape[0]):
        out_ref[e] = share


def last_kernel(got_ref, taps_ref, query_ref):
    n_taps = taps_ref.shape[0]
    for y in range(got_ref.shape[0] // 2):
        cols = slice(y * LANES, (y + 1) * LANES)
        first, second = got_ref[2 * y], got_ref[2 * y + 1]
        row = lax.broadcasted_iota(jnp.int32, (8, LANES), 0)
        query_ref[:, cols] = jnp.where(row < 4, first[:8], second[:8])
        taps_ref[0:16, cols] = first[8:]
        taps_ref[16:n_taps, cols] = second[8 : 8 + n_taps - 16]


def call(kernel, outs, scratch, n_args, flops, placed=True):
    vmem = pl.BlockSpec(memory_space=pltpu.VMEM)
    return pl.pallas_call(
        kernel,
        out_shape=outs,
        in_specs=[pl.BlockSpec(memory_space=pltpu.SMEM)] * placed + [vmem] * n_args,
        out_specs=[vmem] * len(outs),
        scratch_shapes=scratch,
        compiler_params=pltpu.CompilerParams(vmem_limit_bytes=24 * 2**20),
        cost_estimate=pl.CostEstimate(flops=flops, bytes_accessed=8 * 2**20, transcendentals=2**20),
    )


def shards(frames, lengths, w_in, kernel, w_out, pool_query, w_value, text_emb, teacher):
    n_ep, n_seq = lax.axis_size("ep"), lax.axis_size("seq")
    x = frames[0]
    rows, width = x.shape
    n_taps, n_heads = kernel.shape[0], pool_query.shape[0]
    wide, whole = rows + 2 * SIDE, rows + 2 * STEP
    shape = jax.ShapeDtypeStruct

    forward = [(i, i + 1) for i in range(n_seq - 1)]
    backward = [(target, source) for source, target in forward]
    low = lax.ppermute(x[rows - STEP :], "seq", forward)
    high = lax.ppermute(x[:STEP], "seq", backward)
    core = lax.axis_index("ep") % 2
    place = jnp.stack([lax.axis_index("seq") * rows, lengths[0], core]).astype(jnp.int32)

    own = shape((rows, width), BF16)
    normed, sig, gate_slope, own_glu = call(
        project_kernel, [own] * 4, [], 2, 2 * rows * width * width * 2
    )(place, x, w_in)
    glu, act, slope, resid, sums = call(
        forward_kernel,
        [
            shape((whole, width), BF16),
            shape((wide, width), BF16),
            shape((wide, width), BF16),
            shape((wide, width), F32),
            shape((n_seq, n_heads, width + LANES), F32),
        ],
        [pltpu.VMEM((whole, width), F32)],
        8,
        2 * rows * width * width * 4,
    )(place, low, high, x, own_glu, w_in, kernel, w_out, pool_query)
    sums = lax.all_to_all(sums, "seq", 0, 0)

    small_rows = 48
    half = small_rows // 2
    big = width + width // 2
    n_y = n_ep // 2
    size = 8 * (width // LANES + 1)
    payload = shape((n_y, big + half + size, LANES), BF16)
    mine, other = call(
        backward_kernel,
        [payload, payload],
        [
            pltpu.VMEM((wide, width), F32),
            pltpu.VMEM((whole, width), F32),
            pltpu.VMEM((wide, width), BF16),
            pltpu.VMEM((rows, 2 * width), BF16),
            pltpu.VMEM((width, 2 * width), BF16),
            pltpu.VMEM((n_taps + 1, 8, width), F32),
            pltpu.VMEM((small_rows, width), F32),
        ],
        14,
        2 * rows * width * width * 8,
    )(
        place, sums, w_value, text_emb, teacher, pool_query, resid, act, slope,
        glu, normed, sig, gate_slope, w_out, kernel,
    )

    light = functools.partial(call, scratch=[], flops=2**20, placed=False)
    got = lax.ppermute(other, "ep", [(i, i ^ 1) for i in range(n_ep)])
    (total,) = light(
        functools.partial(cores_kernel, big, half),
        [shape((n_y, big + half + 2 * size + 8, LANES), BF16)],
        n_args=2,
    )(mine, got)
    groups = [[2 * y + c for y in range(n_y)] for c in range(2)]
    got = lax.all_to_all(total, "ep", 0, 0, axis_index_groups=groups)
    (total,) = light(
        functools.partial(rows_kernel, big, half),
        [shape((n_seq, big // n_seq + half, LANES), BF16)],
        n_args=1,
    )(got)
    grad_value, loss = light(
        functools.partial(value_kernel, big, half),
        [shape((width, width), F32), shape((1, LANES), F32)],
        n_args=1,
    )(got)
    loss = loss[0, 0]
    got = lax.all_to_all(total, "seq", 0, 0)
    grad_in, grad_out, share = light(
        owner_kernel,
        [
            shape((width // n_seq, 2 * width // n_ep), F32),
            shape((width // n_seq, width // n_ep), F32),
            shape((n_ep, half, LANES), F32),
        ],
        n_args=1,
    )(got)
    got = lax.all_to_all(share, "ep", 0, 0)
    grad_kernel, grad_query = light(
        last_kernel, [shape((n_taps, width), F32), shape((n_heads, width), F32)], n_args=1
    )(got)
    return (loss, grad_in, grad_out, grad_kernel, grad_query, grad_value)


def solution(mesh):
    return jax.shard_map(
        shards,
        mesh=mesh,
        in_specs=(P("ep", "seq", None), P("ep"), P(), P(), P(), P(), P(), P(), P("ep", None)),
        out_specs=(P(), P("seq", "ep"), P("seq", "ep"), P(), P(), P()),
        check_vma=False,
    )
```

```python
import functools

import jax
import jax.numpy as jnp
from jax import lax
from jax.experimental import pallas as pl
from jax.experimental.pallas import tpu as pltpu
from jax.sharding import PartitionSpec as P

F32, BF16 = jnp.float32, jnp.bfloat16
NN = (((1,), (0,)), ((), ()))
NT = (((1,), (1,)), ((), ()))
TN = (((0,), (0,)), ((), ()))
LANES = 128
STEP = 32
SIDE = 16


def dot(a, b, dims=NN):
    return lax.dot_general(a, b, dims, preferred_element_type=F32)


def split3(value):
    high = value.astype(BF16)
    rest = value - high.astype(F32)
    mid = rest.astype(BF16)
    return high, mid, (rest - mid.astype(F32)).astype(BF16)


def stacked(value):
    return jnp.concatenate(split3(value), axis=0)


def folded(value, count=3, rows=8):
    total = value[0:rows]
    for i in range(1, count):
        total = total + value[i * rows : (i + 1) * rows]
    return total


def lane_groups(shape, pieces):
    group = lax.broadcasted_iota(jnp.int32, shape, 1) // 8
    out = jnp.zeros(shape, F32)
    for g, piece in enumerate(pieces):
        out = jnp.where(group == g, piece.astype(F32), out)
    return out.astype(BF16)


def across(column):
    lane = lax.broadcasted_iota(jnp.int32, (8, LANES), 1)
    head = lax.broadcasted_iota(jnp.int32, (8, LANES), 0)
    return jnp.sum(jnp.where(lane % 8 == head, column, 0.0), axis=0, keepdims=True)


def down(row):
    lane = lax.broadcasted_iota(jnp.int32, (8, LANES), 1)
    head = lax.broadcasted_iota(jnp.int32, (8, LANES), 0)
    return jnp.sum(jnp.where(lane == head, row, 0.0), axis=1, keepdims=True)


def gated(x, w_in, width):
    xf = x.astype(F32)
    centred = xf - jnp.mean(xf, axis=-1, keepdims=True)
    var = jnp.mean(centred * centred, axis=-1, keepdims=True)
    normed = (centred * lax.rsqrt(var + 1e-05)).astype(BF16)
    mixed = dot(normed, w_in)
    return normed, mixed[:, :width], jax.nn.sigmoid(mixed[:, width:])


def row_mask(first, rows, length):
    at = first + lax.broadcasted_iota(jnp.int32, (rows, 1), 0)
    return (at >= 0) & (at < length)


def project_kernel(place, x_ref, w_in_ref, normed_ref, sig_ref, slope_ref, glu_ref):
    rows, width = x_ref.shape
    chunk = rows // 4
    for i in range(4):
        part = pl.ds(i * chunk, chunk)
        normed, gate, sig = gated(x_ref[part, :], w_in_ref[...], width)
        valid = row_mask(place[0] + i * chunk, chunk, place[1])
        normed_ref[part, :] = normed
        sig_ref[part, :] = sig.astype(BF16)
        both = gate * sig
        slope_ref[part, :] = (both * (1.0 - sig)).astype(BF16)
        glu_ref[part, :] = jnp.where(valid, both, 0.0).astype(BF16)


def shifted(block):
    rows = block.shape[0]
    return [block if s == 0 else pltpu.roll(block, rows - s, 0) for s in range(8)]


def forward_kernel(
    place, low_ref, high_ref, x_ref, own_glu_ref, w_in_ref, taps_ref, w_out_ref, query_ref,
    glu_ref, act_ref, slope_ref, resid_ref, sums_ref, glu_f,
):
    rows, width = x_ref.shape
    wide = rows + 2 * SIDE
    n_taps = taps_ref.shape[0]
    halo = jnp.concatenate([low_ref[...], high_ref[...]], axis=0)
    unused, gate, sig = gated(halo, w_in_ref[...], width)
    both = gate * sig
    valid_low = row_mask(place[0] - STEP, STEP, place[1])
    valid_high = row_mask(place[0] + rows, STEP, place[1])
    low = jnp.where(valid_low, both[:STEP], 0.0).astype(BF16)
    high = jnp.where(valid_high, both[STEP:], 0.0).astype(BF16)
    glu_ref[0:STEP, :] = low
    glu_ref[STEP : STEP + rows, :] = own_glu_ref[...]
    glu_ref[STEP + rows :, :] = high
    glu_f[0:STEP, :] = low.astype(F32)
    glu_f[STEP : STEP + rows, :] = own_glu_ref[...].astype(F32)
    glu_f[STEP + rows :, :] = high.astype(F32)

    @pl.loop(0, wide // STEP)
    def _(i):
        start = pl.multiple_of(i * STEP, STEP)
        for c in range(width // LANES):
            cols = slice(c * LANES, (c + 1) * LANES)
            views = shifted(glu_f[pl.ds(start, 2 * STEP), cols])
            acc = jnp.zeros((STEP, LANES), F32)
            for k in range(n_taps):
                q, s = divmod(k + 1, 8)
                acc = acc + taps_ref[k : k + 1, cols] * views[s][8 * q : 8 * q + STEP]
            s = jax.nn.sigmoid(acc)
            act_ref[pl.ds(start, STEP), cols] = (acc * s).astype(BF16)
            slope_ref[pl.ds(start, STEP), cols] = (s * (1.0 + acc * (1.0 - s))).astype(BF16)

    w_out = w_out_ref[...]
    resid_ref[0:SIDE, :] = low_ref[STEP - SIDE :, :].astype(F32) + dot(act_ref[0:SIDE, :], w_out)
    resid_ref[SIDE + rows :, :] = high_ref[0:SIDE, :].astype(F32) + dot(
        act_ref[SIDE + rows :, :], w_out
    )
    queries = jnp.concatenate([query_ref[...]] * (LANES // 8), axis=0)
    root = jnp.sqrt(jnp.float32(width))
    parts = 2
    chunk = rows // parts
    scores = []
    for i in range(parts):
        own = pl.ds(SIDE + i * chunk, chunk)
        resid = x_ref[pl.ds(i * chunk, chunk), :].astype(F32) + dot(act_ref[own, :], w_out)
        resid_ref[own, :] = resid
        score = sum(dot(piece, queries, NT) for piece in split3(resid)) / root
        valid = row_mask(place[0] + i * chunk, chunk, place[1])
        scores.append(jnp.where(valid, score, -1e30))
    top = functools.reduce(
        jnp.maximum, [jnp.max(score, axis=0, keepdims=True) for score in scores]
    )
    total = jnp.zeros((1, LANES), F32)
    vec = jnp.zeros((LANES, width), F32)
    for i in range(parts):
        valid = row_mask(place[0] + i * chunk, chunk, place[1])
        expo = jnp.where(valid, jnp.exp(scores[i] - top), 0.0)
        total = total + jnp.sum(expo, axis=0, keepdims=True)
        weights = lane_groups(expo.shape, split3(expo))
        for piece in split3(resid_ref[pl.ds(SIDE + i * chunk, chunk), :])[:2]:
            vec = vec + dot(weights, piece, TN)
    lane = lax.broadcasted_iota(jnp.int32, (8, LANES), 1)
    sums = jnp.concatenate(
        [folded(vec), jnp.where(lane == 0, down(top), down(total))], axis=1
    )

    @pl.loop(0, sums_ref.shape[0])
    def _(i):
        sums_ref[i] = sums


def middle_kernel(
    place, sums_ref, w_value_ref, text_ref, teacher_ref, query_ref, resid_ref, slope_ref,
    glu_ref, w_out_ref,
    share_ref, episode_ref, dresid_ref, dconv_ref,
    glu_f, tap_s,
):
    wide, width = resid_ref.shape
    rows = wide - 2 * SIDE
    n_taps = tap_s.shape[0] - 1
    n_cands = text_ref.shape[0]
    head_dim = width // 8
    root = jnp.sqrt(jnp.float32(width))

    stats = sums_ref[:, :, width:]
    tops, totals = stats[:, :, 0:1], stats[:, :, 1:2]
    top = jnp.max(tops, axis=0)
    scale = jnp.exp(tops - top[None])
    total = jnp.sum(scale * totals, axis=0)
    vbar = jnp.sum(scale * sums_ref[:, :, :width], axis=0) / total
    at = lax.broadcasted_iota(jnp.int32, (8, width), 1) // head_dim
    own_head = at == lax.broadcasted_iota(jnp.int32, (8, width), 0)
    w_value = w_value_ref[...]
    texts = text_ref[...]
    full = folded(dot(stacked(vbar), w_value))
    pooled = jnp.sum(jnp.where(own_head, full, 0.0), axis=0, keepdims=True)
    pooled = jnp.broadcast_to(pooled, (8, width))
    rms = jnp.sqrt(jnp.mean(pooled * pooled, axis=-1, keepdims=True) + 1e-06)
    emb = pooled / rms
    diff = folded(dot(stacked(emb), texts, NT)) / root - teacher_ref[...]
    loss = jnp.sum(diff * diff, axis=-1, keepdims=True) / n_cands
    demb = folded(dot(stacked(2.0 * diff / n_cands), texts)) / root
    dpooled = (demb - emb * jnp.mean(demb * emb, axis=-1, keepdims=True)) / rms
    dvbar = folded(dot(stacked(jnp.where(own_head, dpooled, 0.0)), w_value, NT))
    centre = jnp.sum(dvbar * vbar, axis=-1, keepdims=True)
    row = lax.broadcasted_iota(jnp.int32, (8, width), 0)
    loss_high = loss.astype(BF16).astype(F32)
    rest = jnp.where(row == 4, loss_high, jnp.where(row == 5, loss - loss_high, 0.0))[:, :LANES]
    blocks = [slice(c * LANES, (c + 1) * LANES) for c in range(width // LANES)]
    for c, cols in enumerate(blocks):
        rest = jnp.where(row[:, :LANES] == c, dpooled[:, cols], rest)
    episode_ref[...] = jnp.concatenate([*[vbar[:, cols] for cols in blocks], rest], axis=0)

    top_l, total_l, centre_l = across(top), across(total), across(centre)
    query = query_ref[...]
    d_high, d_mid, d_low = split3(dvbar)
    many = lambda piece: [piece] * (LANES // 8)
    both = jnp.concatenate(many(query) + many(d_high), axis=0)
    queries, dv_mid = both[:LANES], jnp.concatenate(many(d_mid), axis=0)
    mixing = jnp.concatenate(
        [d_high, d_mid, d_high, d_mid, query, query, query, jnp.zeros((LANES - 56, width), BF16)],
        axis=0,
    )
    w_out = w_out_ref[...]
    parts = 2
    chunk = wide // parts
    grad_query = jnp.zeros((LANES, width), F32)
    for i in range(parts):
        here = pl.ds(i * chunk, chunk)
        r_high, r_mid, r_low = split3(resid_ref[here, :])
        products = dot(r_high, both, NT) + dot(r_mid, both, NT)
        score = (products[:, :LANES] + dot(r_low, queries, NT)) / root
        valid = row_mask(place[0] - SIDE + i * chunk, chunk, place[1])
        probs = jnp.where(valid, jnp.exp(score - top_l), 0.0) / total_l
        proj = products[:, LANES:] + dot(r_high, dv_mid, NT)
        dscores = probs * (proj - centre_l) / root
        p_high, p_mid, unused = split3(probs)
        s_pieces = split3(dscores)
        mixed = lane_groups(probs.shape, (p_high, p_high, p_mid, p_mid, *s_pieces))
        dresid = dot(mixed, mixing).astype(BF16)
        dresid_ref[here, :] = dresid
        own = lax.broadcasted_iota(jnp.int32, (chunk, 1), 0) + i * chunk
        own = (own >= SIDE) & (own < SIDE + rows)
        weights = lane_groups(probs.shape, s_pieces)
        weights = jnp.where(own, weights.astype(F32), 0.0).astype(BF16)
        for piece in (r_high, r_mid):
            grad_query = grad_query + dot(weights, piece, TN)
        dact = dot(dresid, w_out, NT)
        dconv = (dact * slope_ref[here, :].astype(F32)).astype(BF16)
        dconv_ref[here, :] = dconv.astype(F32)
    query_sum = folded(grad_query)

    glu_f[...] = glu_ref[...].astype(F32)
    tap_s[...] = jnp.zeros_like(tap_s)

    @pl.loop(0, rows // STEP)
    def _(i):
        start = pl.multiple_of(i * STEP + SIDE, SIDE)
        for c in range(width // LANES):
            cols = slice(c * LANES, (c + 1) * LANES)
            own = dconv_ref[pl.ds(start, STEP), cols]
            views = shifted(glu_f[pl.ds(start, 2 * STEP), cols])
            for k in range(n_taps):
                q, s = divmod(k + 1, 8)
                product = own * views[s][8 * q : 8 * q + STEP]
                tap_s[k, :, cols] += folded(product, STEP // 8)

    small = jnp.concatenate([query_sum, jnp.sum(tap_s[...], axis=1)], axis=0)
    per = share_ref.shape[0] // len(blocks)
    for c, cols in enumerate(blocks):
        for j in range(per):
            if 8 * j < small.shape[0]:
                share_ref[c * per + j] = small[8 * j : 8 * j + 8, cols]
            else:
                share_ref[c * per + j] = jnp.zeros((8, LANES), F32)


def backward_kernel(
    place, dconv_ref, dresid_ref, act_ref, normed_ref, sig_ref, gate_slope_ref, taps_ref, episode_ref,
    mine_ref, other_ref,
    dmixed_s, in_s,
):
    rows, width = normed_ref.shape
    n_taps = taps_ref.shape[0]

    @pl.loop(0, rows // STEP)
    def _(i):
        start = pl.multiple_of(i * STEP, STEP)
        valid = row_mask(place[0] + start, STEP, place[1])
        for c in range(width // LANES):
            cols = slice(c * LANES, (c + 1) * LANES)
            views = shifted(dconv_ref[pl.ds(start, 2 * STEP), cols])
            acc = jnp.zeros((STEP, LANES), F32)
            for k in range(n_taps):
                q, s = divmod(n_taps - k, 8)
                acc = acc + taps_ref[k : k + 1, cols] * views[s][8 * q : 8 * q + STEP]
            dglu = jnp.where(valid, acc, 0.0)
            here = pl.ds(start, STEP)
            dmixed_s[here, cols] = (dglu * sig_ref[here, cols].astype(F32)).astype(BF16)
            dmixed_s[here, slice(width + c * LANES, width + (c + 1) * LANES)] = (
                dglu * gate_slope_ref[here, cols].astype(F32)
            ).astype(BF16)

    grad_out = dot(act_ref[SIDE : SIDE + rows, :], dresid_ref[SIDE : SIDE + rows, :], TN)
    in_s[...] = dot(normed_ref[...], dmixed_s[...], TN).astype(BF16)
    core = place[2]
    big = width + width // 2
    tail = mine_ref.shape[1] - big - episode_ref.shape[0]
    episode = jnp.concatenate([episode_ref[...], jnp.zeros((tail, LANES), F32)], axis=0).astype(BF16)
    halves = grad_out.reshape(width // 16, 2, 8, width)
    first, second = (halves[:, j].reshape(width // 2, width) for j in range(2))
    low_lane = lax.broadcasted_iota(jnp.int32, (width // 2, LANES), 1) < LANES // 2
    for y in range(width // LANES):
        a = first[:, y * LANES : (y + 1) * LANES]
        b = second[:, y * LANES : (y + 1) * LANES]
        even = jnp.where(low_lane, a, pltpu.roll(b, LANES // 2, 1))
        odd = jnp.where(low_lane, pltpu.roll(a, LANES // 2, 1), b)
        for ref, which, block in (
            (mine_ref, core, jnp.where(core == 0, even, odd)),
            (other_ref, 1 - core, jnp.where(core == 0, odd, even)),
        ):
            at = pl.multiple_of((2 * y + which) * LANES, LANES)
            ref[y, 0:width, :] = in_s[:, pl.ds(at, LANES)]
            ref[y, width:big, :] = block.astype(BF16)
            ref[y, big:, :] = episode


def paired(value):
    high = value.astype(BF16).astype(F32)
    return jnp.concatenate([high, value - high], axis=0)


def cores_kernel(big, size, mine_ref, got_ref, share_ref, got_share_ref, out_ref):
    share = paired(share_ref[...] + got_share_ref[...])
    for y in range(mine_ref.shape[0]):
        total = mine_ref[y, 0:big, :].astype(F32) + got_ref[y, 0:big, :].astype(F32)
        out_ref[y, 0:big, :] = total.astype(BF16)
        mine, got = mine_ref[y, big:, :].astype(F32), got_ref[y, big:, :].astype(F32)
        out_ref[y, big:, :] = jnp.concatenate([share, mine[:size], got[:size]], axis=0).astype(BF16)


def rows_kernel(big, got_ref, out_ref):
    n_y, n_seq = got_ref.shape[0], out_ref.shape[0]
    total = got_ref[0, 0:big, :].astype(F32)
    share = got_ref[0, big:, :].astype(F32)[:16]
    for y in range(1, n_y):
        total = total + got_ref[y, 0:big, :].astype(F32)
        share = share + got_ref[y, big:, :].astype(F32)[:16]
    share = paired(share[:8] + share[8:])
    split = 2 * big // 3
    out_ref[...] = jnp.concatenate(
        [
            total[:split].reshape(n_seq, split // n_seq, LANES),
            total[split:].reshape(n_seq, (big - split) // n_seq, LANES),
            jnp.broadcast_to(share[None], (n_seq, *share.shape)),
        ],
        axis=1,
    ).astype(BF16)


def value_kernel(big, got_ref, grad_ref, loss_ref):
    width = grad_ref.shape[0]
    head = lax.broadcasted_iota(jnp.int32, (8, width), 1) // (width // 8)
    own_head = head == lax.broadcasted_iota(jnp.int32, (8, width), 0)
    vectors, others = [], []
    loss = jnp.zeros((1, LANES), F32)
    n_blocks = width // LANES
    size = 8 * (n_blocks + 1)
    for y in range(got_ref.shape[0]):
        rows = got_ref[y, big:, :].astype(F32)
        for start in (16, 16 + size):
            episode = rows[start : start + size]
            rest = episode[8 * n_blocks :]
            vectors.append(
                jnp.concatenate([episode[8 * c : 8 * c + 8] for c in range(n_blocks)], axis=1)
            )
            dpooled = jnp.concatenate([rest[c : c + 1] for c in range(n_blocks)], axis=1)
            others.append(jnp.where(own_head, dpooled, 0.0))
            loss = loss + rest[4:5] + rest[5:6]
    vectors, others = (jnp.concatenate(v, axis=0).astype(BF16) for v in (vectors, others))
    grad_ref[...] = dot(vectors, others, TN)
    loss_ref[...] = loss


def owner_kernel(got_ref, grad_in_ref, grad_out_ref, taps_ref, query_ref):
    n_seq = got_ref.shape[0]
    in_rows, cols = grad_in_ref.shape[0], grad_out_ref.shape[1]
    out_rows = grad_out_ref.shape[0] // 2
    n_taps = taps_ref.shape[0]
    per = n_seq // (taps_ref.shape[1] // LANES)
    total = jnp.zeros((in_rows + out_rows, LANES), F32)
    for s in range(n_seq):
        block = got_ref[s].astype(F32)
        total = total + block[: in_rows + out_rows]
        share = block[in_rows + out_rows :]
        share = share[:8] + share[8:]
        c, j = divmod(s, per)
        lanes = slice(c * LANES, (c + 1) * LANES)
        if j == 0:
            query_ref[:, lanes] = share
        elif 8 * (j - 1) < n_taps:
            last = min(8 * j, n_taps)
            taps_ref[8 * (j - 1) : last, lanes] = share[: last - 8 * (j - 1)]
    grad_in_ref[...] = total[:in_rows]
    pair_rows = total[in_rows:]
    grad_out_ref[0:out_rows, :] = pair_rows[:, :cols]
    grad_out_ref[out_rows:, :] = pair_rows[:, cols:]


def call(kernel, outs, scratch, n_args, flops, placed=True):
    vmem = pl.BlockSpec(memory_space=pltpu.VMEM)
    return pl.pallas_call(
        kernel,
        out_shape=outs,
        in_specs=[pl.BlockSpec(memory_space=pltpu.SMEM)] * placed + [vmem] * n_args,
        out_specs=[vmem] * len(outs),
        scratch_shapes=scratch,
        compiler_params=pltpu.CompilerParams(vmem_limit_bytes=24 * 2**20),
        cost_estimate=pl.CostEstimate(flops=flops, bytes_accessed=8 * 2**20, transcendentals=2**20),
    )


def shards(frames, lengths, w_in, kernel, w_out, pool_query, w_value, text_emb, teacher):
    n_ep, n_seq = lax.axis_size("ep"), lax.axis_size("seq")
    x = frames[0]
    rows, width = x.shape
    n_taps, n_heads = kernel.shape[0], pool_query.shape[0]
    wide, whole = rows + 2 * SIDE, rows + 2 * STEP
    shape = jax.ShapeDtypeStruct

    forward = [(i, i + 1) for i in range(n_seq - 1)]
    backward = [(target, source) for source, target in forward]
    low = lax.ppermute(x[rows - STEP :], "seq", forward)
    high = lax.ppermute(x[:STEP], "seq", backward)
    core = lax.axis_index("ep") % 2
    place = jnp.stack([lax.axis_index("seq") * rows, lengths[0], core]).astype(jnp.int32)

    own = shape((rows, width), BF16)
    normed, sig, gate_slope, own_glu = call(
        project_kernel, [own] * 4, [], 2, 2 * rows * width * width * 2
    )(place, x, w_in)
    glu, act, slope, resid, sums = call(
        forward_kernel,
        [
            shape((whole, width), BF16),
            shape((wide, width), BF16),
            shape((wide, width), BF16),
            shape((wide, width), F32),
            shape((n_seq, n_heads, width + LANES), F32),
        ],
        [pltpu.VMEM((whole, width), F32)],
        8,
        2 * rows * width * width * 4,
    )(place, low, high, x, own_glu, w_in, kernel, w_out, pool_query)
    sums = lax.all_to_all(sums, "seq", 0, 0)

    big = width + width // 2
    n_y = n_ep // 2
    size = 8 * (width // LANES + 1)
    share, episode, dresid, dconv = call(
        middle_kernel,
        [
            shape((n_seq, 8, LANES), F32),
            shape((size, LANES), F32),
            shape((wide, width), BF16),
            shape((wide, width), F32),
        ],
        [pltpu.VMEM((whole, width), F32), pltpu.VMEM((n_taps + 1, 8, width), F32)],
        9,
        2 * rows * width * width * 4,
    )(place, sums, w_value, text_emb, teacher, pool_query, resid, slope, glu, w_out)

    share = lax.all_to_all(share, "seq", 0, 0)

    payload = shape((n_y, big + size + 8, LANES), BF16)
    mine, other = call(
        backward_kernel,
        [payload, payload],
        [pltpu.VMEM((rows, 2 * width), BF16), pltpu.VMEM((width, 2 * width), BF16)],
        8,
        2 * rows * width * width * 40,
    )(place, dconv, dresid, act, normed, sig, gate_slope, kernel, episode)

    light = functools.partial(call, scratch=[], flops=2**20, placed=False)
    other, share = lax.optimization_barrier((other, share))
    swap = [(i, i ^ 1) for i in range(n_ep)]
    got = lax.ppermute(other, "ep", swap)
    share = jnp.sum(share, axis=0)
    got_share = lax.ppermute(share, "ep", swap)
    (total,) = light(
        functools.partial(cores_kernel, big, size),
        [shape((n_y, big + 16 + 2 * size, LANES), BF16)],
        n_args=4,
    )(mine, got, share, got_share)
    groups = [[2 * y + c for y in range(n_y)] for c in range(2)]
    got = lax.all_to_all(total, "ep", 0, 0, axis_index_groups=groups)
    (total,) = light(
        functools.partial(rows_kernel, big),
        [shape((n_seq, big // n_seq + 16, LANES), BF16)],
        n_args=1,
    )(got)
    grad_value, loss = light(
        functools.partial(value_kernel, big),
        [shape((width, width), F32), shape((1, LANES), F32)],
        n_args=1,
    )(got)
    loss = loss[0, 0]
    got = lax.all_to_all(total, "seq", 0, 0)
    grad_in, grad_out, grad_kernel, grad_query = light(
        owner_kernel,
        [
            shape((width // n_seq, 2 * width // n_ep), F32),
            shape((width // n_seq, width // n_ep), F32),
            shape((n_taps, width), F32),
            shape((n_heads, width), F32),
        ],
        n_args=1,
    )(got)
    return (loss, grad_in, grad_out, grad_kernel, grad_query, grad_value)


def solution(mesh):
    return jax.shard_map(
        shards,
        mesh=mesh,
        in_specs=(P("ep", "seq", None), P("ep"), P(), P(), P(), P(), P(), P(), P("ep", None)),
        out_specs=(P(), P("seq", "ep"), P("seq", "ep"), P(), P(), P()),
        check_vma=False,
    )
```

```python
import functools

import jax
import jax.numpy as jnp
from jax import lax
from jax.experimental import pallas as pl
from jax.experimental.pallas import tpu as pltpu
from jax.sharding import PartitionSpec as P

F32, BF16 = jnp.float32, jnp.bfloat16
NN = (((1,), (0,)), ((), ()))
NT = (((1,), (1,)), ((), ()))
TN = (((0,), (0,)), ((), ()))
LANES = 128
STEP = 32
SIDE = 16


def dot(a, b, dims=NN):
    return lax.dot_general(a, b, dims, preferred_element_type=F32)


def split3(value):
    high = value.astype(BF16)
    rest = value - high.astype(F32)
    mid = rest.astype(BF16)
    return high, mid, (rest - mid.astype(F32)).astype(BF16)


def stacked(value):
    return jnp.concatenate(split3(value), axis=0)


def folded(value, count=3, rows=8):
    total = value[0:rows]
    for i in range(1, count):
        total = total + value[i * rows : (i + 1) * rows]
    return total


def lane_groups(shape, pieces):
    group = lax.broadcasted_iota(jnp.int32, shape, 1) // 8
    out = jnp.zeros(shape, F32)
    for g, piece in enumerate(pieces):
        out = jnp.where(group == g, piece.astype(F32), out)
    return out.astype(BF16)


def across(column):
    lane = lax.broadcasted_iota(jnp.int32, (8, LANES), 1)
    head = lax.broadcasted_iota(jnp.int32, (8, LANES), 0)
    return jnp.sum(jnp.where(lane % 8 == head, column, 0.0), axis=0, keepdims=True)


def down(row):
    lane = lax.broadcasted_iota(jnp.int32, (8, LANES), 1)
    head = lax.broadcasted_iota(jnp.int32, (8, LANES), 0)
    return jnp.sum(jnp.where(lane == head, row, 0.0), axis=1, keepdims=True)


def gated(x, w_in, width):
    xf = x.astype(F32)
    centred = xf - jnp.mean(xf, axis=-1, keepdims=True)
    var = jnp.mean(centred * centred, axis=-1, keepdims=True)
    normed = (centred * lax.rsqrt(var + 1e-05)).astype(BF16)
    mixed = dot(normed, w_in)
    return normed, mixed[:, :width], jax.nn.sigmoid(mixed[:, width:])


def row_mask(first, rows, length):
    at = first + lax.broadcasted_iota(jnp.int32, (rows, 1), 0)
    return (at >= 0) & (at < length)


def project_kernel(place, x_ref, w_in_ref, normed_ref, sig_ref, slope_ref, glu_ref):
    rows, width = x_ref.shape
    chunk = rows // 4
    for i in range(4):
        part = pl.ds(i * chunk, chunk)
        normed, gate, sig = gated(x_ref[part, :], w_in_ref[...], width)
        valid = row_mask(place[0] + i * chunk, chunk, place[1])
        normed_ref[part, :] = normed
        sig_ref[part, :] = sig.astype(BF16)
        both = gate * sig
        slope_ref[part, :] = (both * (1.0 - sig)).astype(BF16)
        glu_ref[part, :] = jnp.where(valid, both, 0.0).astype(BF16)


def shifted(block):
    rows = block.shape[0]
    return [block if s == 0 else pltpu.roll(block, rows - s, 0) for s in range(8)]


def forward_kernel(
    place, low_ref, high_ref, x_ref, own_glu_ref, w_in_ref, taps_ref, w_out_ref, query_ref,
    glu_ref, act_ref, slope_ref, resid_ref, sums_ref, glu_f,
):
    rows, width = x_ref.shape
    wide = rows + 2 * SIDE
    n_taps = taps_ref.shape[0]
    halo = jnp.concatenate([low_ref[...], high_ref[...]], axis=0)
    unused, gate, sig = gated(halo, w_in_ref[...], width)
    both = gate * sig
    valid_low = row_mask(place[0] - STEP, STEP, place[1])
    valid_high = row_mask(place[0] + rows, STEP, place[1])
    low = jnp.where(valid_low, both[:STEP], 0.0).astype(BF16)
    high = jnp.where(valid_high, both[STEP:], 0.0).astype(BF16)
    glu_ref[0:STEP, :] = low
    glu_ref[STEP : STEP + rows, :] = own_glu_ref[...]
    glu_ref[STEP + rows :, :] = high
    glu_f[0:STEP, :] = low.astype(F32)
    glu_f[STEP : STEP + rows, :] = own_glu_ref[...].astype(F32)
    glu_f[STEP + rows :, :] = high.astype(F32)

    @pl.loop(0, wide // STEP)
    def _(i):
        start = pl.multiple_of(i * STEP, STEP)
        for c in range(width // LANES):
            cols = slice(c * LANES, (c + 1) * LANES)
            views = shifted(glu_f[pl.ds(start, 2 * STEP), cols])
            acc = jnp.zeros((STEP, LANES), F32)
            for k in range(n_taps):
                q, s = divmod(k + 1, 8)
                acc = acc + taps_ref[k : k + 1, cols] * views[s][8 * q : 8 * q + STEP]
            s = jax.nn.sigmoid(acc)
            act_ref[pl.ds(start, STEP), cols] = (acc * s).astype(BF16)
            slope_ref[pl.ds(start, STEP), cols] = (s * (1.0 + acc * (1.0 - s))).astype(BF16)

    w_out = w_out_ref[...]
    resid_ref[0:SIDE, :] = low_ref[STEP - SIDE :, :].astype(F32) + dot(act_ref[0:SIDE, :], w_out)
    resid_ref[SIDE + rows :, :] = high_ref[0:SIDE, :].astype(F32) + dot(
        act_ref[SIDE + rows :, :], w_out
    )
    queries = jnp.concatenate([query_ref[...]] * (LANES // 8), axis=0)
    root = jnp.sqrt(jnp.float32(width))
    parts = 2
    chunk = rows // parts
    scores = []
    for i in range(parts):
        own = pl.ds(SIDE + i * chunk, chunk)
        resid = x_ref[pl.ds(i * chunk, chunk), :].astype(F32) + dot(act_ref[own, :], w_out)
        resid_ref[own, :] = resid
        score = sum(dot(piece, queries, NT) for piece in split3(resid)) / root
        valid = row_mask(place[0] + i * chunk, chunk, place[1])
        scores.append(jnp.where(valid, score, -1e30))
    top = functools.reduce(
        jnp.maximum, [jnp.max(score, axis=0, keepdims=True) for score in scores]
    )
    total = jnp.zeros((1, LANES), F32)
    vec = jnp.zeros((LANES, width), F32)
    for i in range(parts):
        valid = row_mask(place[0] + i * chunk, chunk, place[1])
        expo = jnp.where(valid, jnp.exp(scores[i] - top), 0.0)
        total = total + jnp.sum(expo, axis=0, keepdims=True)
        weights = lane_groups(expo.shape, split3(expo))
        for piece in split3(resid_ref[pl.ds(SIDE + i * chunk, chunk), :])[:2]:
            vec = vec + dot(weights, piece, TN)
    lane = lax.broadcasted_iota(jnp.int32, (8, LANES), 1)
    sums = jnp.concatenate(
        [folded(vec), jnp.where(lane == 0, down(top), down(total))], axis=1
    )

    @pl.loop(0, sums_ref.shape[0])
    def _(i):
        sums_ref[i] = sums


def backward_kernel(
    place, sums_ref, w_value_ref, text_ref, teacher_ref, query_ref, resid_ref, act_ref, slope_ref,
    glu_ref, normed_ref, sig_ref, gate_slope_ref, w_out_ref, taps_ref,
    mine_ref, other_ref,
    dconv_f, glu_f, dresid_s, dmixed_s, in_s, tap_s, small_s,
):
    rows, width = normed_ref.shape
    wide = rows + 2 * SIDE
    n_taps = taps_ref.shape[0]
    n_cands = text_ref.shape[0]
    head_dim = width // 8
    root = jnp.sqrt(jnp.float32(width))

    stats = sums_ref[:, :, width:]
    tops, totals = stats[:, :, 0:1], stats[:, :, 1:2]
    top = jnp.max(tops, axis=0)
    scale = jnp.exp(tops - top[None])
    total = jnp.sum(scale * totals, axis=0)
    vbar = jnp.sum(scale * sums_ref[:, :, :width], axis=0) / total
    at = lax.broadcasted_iota(jnp.int32, (8, width), 1) // head_dim
    own_head = at == lax.broadcasted_iota(jnp.int32, (8, width), 0)
    w_value = w_value_ref[...]
    texts = text_ref[...]
    full = folded(dot(stacked(vbar), w_value))
    pooled = jnp.sum(jnp.where(own_head, full, 0.0), axis=0, keepdims=True)
    pooled = jnp.broadcast_to(pooled, (8, width))
    rms = jnp.sqrt(jnp.mean(pooled * pooled, axis=-1, keepdims=True) + 1e-06)
    emb = pooled / rms
    diff = folded(dot(stacked(emb), texts, NT)) / root - teacher_ref[...]
    loss = jnp.sum(diff * diff, axis=-1, keepdims=True) / n_cands
    demb = folded(dot(stacked(2.0 * diff / n_cands), texts)) / root
    dpooled = (demb - emb * jnp.mean(demb * emb, axis=-1, keepdims=True)) / rms
    dvbar = folded(dot(stacked(jnp.where(own_head, dpooled, 0.0)), w_value, NT))
    centre = jnp.sum(dvbar * vbar, axis=-1, keepdims=True)
    row = lax.broadcasted_iota(jnp.int32, (8, width), 0)
    loss_high = loss.astype(BF16).astype(F32)
    rest = jnp.where(row == 4, loss_high, jnp.where(row == 5, loss - loss_high, 0.0))[:, :LANES]
    blocks = [slice(c * LANES, (c + 1) * LANES) for c in range(width // LANES)]
    for c, cols in enumerate(blocks):
        rest = jnp.where(row[:, :LANES] == c, dpooled[:, cols], rest)
    episode = jnp.concatenate([*[vbar[:, cols] for cols in blocks], rest], axis=0)

    top_l, total_l, centre_l = across(top), across(total), across(centre)
    query = query_ref[...]
    d_high, d_mid, d_low = split3(dvbar)
    many = lambda piece: [piece] * (LANES // 8)
    both = jnp.concatenate(many(query) + many(d_high), axis=0)
    queries, dv_mid = both[:LANES], jnp.concatenate(many(d_mid), axis=0)
    mixing = jnp.concatenate(
        [d_high, d_mid, d_high, d_mid, query, query, query, jnp.zeros((LANES - 56, width), BF16)],
        axis=0,
    )
    w_out = w_out_ref[...]
    parts = 2
    chunk = wide // parts
    grad_query = jnp.zeros((LANES, width), F32)
    for i in range(parts):
        here = pl.ds(i * chunk, chunk)
        r_high, r_mid, r_low = split3(resid_ref[here, :])
        products = dot(r_high, both, NT) + dot(r_mid, both, NT)
        score = (products[:, :LANES] + dot(r_low, queries, NT)) / root
        valid = row_mask(place[0] - SIDE + i * chunk, chunk, place[1])
        probs = jnp.where(valid, jnp.exp(score - top_l), 0.0) / total_l
        proj = products[:, LANES:] + dot(r_high, dv_mid, NT)
        dscores = probs * (proj - centre_l) / root
        p_high, p_mid, unused = split3(probs)
        s_pieces = split3(dscores)
        mixed = lane_groups(probs.shape, (p_high, p_high, p_mid, p_mid, *s_pieces))
        dresid = dot(mixed, mixing).astype(BF16)
        dresid_s[here, :] = dresid
        own = lax.broadcasted_iota(jnp.int32, (chunk, 1), 0) + i * chunk
        own = (own >= SIDE) & (own < SIDE + rows)
        weights = lane_groups(probs.shape, s_pieces)
        weights = jnp.where(own, weights.astype(F32), 0.0).astype(BF16)
        for piece in (r_high, r_mid):
            grad_query = grad_query + dot(weights, piece, TN)
        dact = dot(dresid, w_out, NT)
        dconv = (dact * slope_ref[here, :].astype(F32)).astype(BF16)
        dconv_f[here, :] = dconv.astype(F32)
    query_sum = folded(grad_query)
    high = query_sum.astype(BF16).astype(F32)
    half = small_s.shape[0] // 2
    small_s[0:8, :] = jnp.where(row < 4, high, pltpu.roll(query_sum - high, 4, 0))
    small_s[half : half + 8, :] = jnp.where(row < 4, pltpu.roll(high, 4, 0), query_sum - high)

    glu_f[...] = glu_ref[...].astype(F32)
    tap_s[...] = jnp.zeros_like(tap_s)

    @pl.loop(0, rows // STEP)
    def _(i):
        start = pl.multiple_of(i * STEP, STEP)
        valid = row_mask(place[0] + start, STEP, place[1])
        for c in range(width // LANES):
            cols = slice(c * LANES, (c + 1) * LANES)
            views = shifted(dconv_f[pl.ds(start, 2 * STEP), cols])
            acc = jnp.zeros((STEP, LANES), F32)
            for k in range(n_taps):
                q, s = divmod(n_taps - k, 8)
                acc = acc + taps_ref[k : k + 1, cols] * views[s][8 * q : 8 * q + STEP]
            dglu = jnp.where(valid, acc, 0.0)
            here = pl.ds(start, STEP)
            dmixed_s[here, cols] = (dglu * sig_ref[here, cols].astype(F32)).astype(BF16)
            dmixed_s[here, slice(width + c * LANES, width + (c + 1) * LANES)] = (
                dglu * gate_slope_ref[here, cols].astype(F32)
            ).astype(BF16)
            own = views[0][SIDE : SIDE + STEP]
            views = shifted(glu_f[pl.ds(start + SIDE, 2 * STEP), cols])
            for k in range(n_taps):
                q, s = divmod(k + 1, 8)
                product = own * views[s][8 * q : 8 * q + STEP]
                tap_s[k, :, cols] += folded(product, STEP // 8)

    tap_sum = jnp.sum(tap_s[...], axis=1)
    small_s[8:half, :] = tap_sum[: half - 8]
    small_s[half + 8 :, :] = tap_sum[half - 8 :]

    grad_out = dot(act_ref[SIDE : SIDE + rows, :], dresid_s[SIDE : SIDE + rows, :], TN)
    in_s[...] = dot(normed_ref[...], dmixed_s[...], TN).astype(BF16)
    core = place[2]
    halves = grad_out.reshape(width // 16, 2, 8, width)
    first, second = (halves[:, j].reshape(width // 2, width) for j in range(2))
    low_lane = lax.broadcasted_iota(jnp.int32, (width // 2, LANES), 1) < LANES // 2
    for y in range(width // LANES):
        a = first[:, y * LANES : (y + 1) * LANES]
        b = second[:, y * LANES : (y + 1) * LANES]
        even = jnp.where(low_lane, a, pltpu.roll(b, LANES // 2, 1))
        odd = jnp.where(low_lane, pltpu.roll(a, LANES // 2, 1), b)
        for ref, which, block in (
            (mine_ref, core, jnp.where(core == 0, even, odd)),
            (other_ref, 1 - core, jnp.where(core == 0, odd, even)),
        ):
            at = pl.multiple_of((2 * y + which) * LANES, LANES)
            ref[y, 0:width, :] = in_s[:, pl.ds(at, LANES)]
            ref[y, width : width + width // 2, :] = block.astype(BF16)
            share = small_s[pl.ds(pl.multiple_of(which * half, 8), half), y * LANES : (y + 1) * LANES]
            ref[y, width + width // 2 :, :] = jnp.concatenate([share, episode], axis=0).astype(BF16)


def paired(rows):
    row = lax.broadcasted_iota(jnp.int32, rows.shape, 0)
    value = rows + pltpu.roll(rows, 4, 0)
    high = value.astype(BF16).astype(F32)
    return jnp.where(row < 4, high, value - high)


def cores_kernel(big, half, mine_ref, got_ref, out_ref):
    for y in range(mine_ref.shape[0]):
        total = mine_ref[y, 0:big, :].astype(F32) + got_ref[y, 0:big, :].astype(F32)
        out_ref[y, 0:big, :] = total.astype(BF16)
        mine, got = mine_ref[y, big:, :].astype(F32), got_ref[y, big:, :].astype(F32)
        share = mine[:half] + got[:half]
        out_ref[y, big:, :] = jnp.concatenate(
            [paired(share[:8]), share[8:], mine[half:], got[half:], jnp.zeros((8, LANES), F32)],
            axis=0,
        ).astype(BF16)


def rows_kernel(big, half, got_ref, out_ref):
    n_y, n_seq = got_ref.shape[0], out_ref.shape[0]
    total = got_ref[0, 0:big, :].astype(F32)
    share = got_ref[0, big:, :].astype(F32)[:half]
    for y in range(1, n_y):
        total = total + got_ref[y, 0:big, :].astype(F32)
        share = share + got_ref[y, big:, :].astype(F32)[:half]
    share = jnp.concatenate([paired(share[:8]), share[8:]], axis=0)
    split = 2 * big // 3
    out_ref[...] = jnp.concatenate(
        [
            total[:split].reshape(n_seq, split // n_seq, LANES),
            total[split:].reshape(n_seq, (big - split) // n_seq, LANES),
            jnp.broadcast_to(share[None], (n_seq, half, LANES)),
        ],
        axis=1,
    ).astype(BF16)


def value_kernel(big, half, got_ref, grad_ref, loss_ref):
    width = grad_ref.shape[0]
    head = lax.broadcasted_iota(jnp.int32, (8, width), 1) // (width // 8)
    own_head = head == lax.broadcasted_iota(jnp.int32, (8, width), 0)
    vectors, others = [], []
    loss = jnp.zeros((1, LANES), F32)
    n_blocks = width // LANES
    size = 8 * (n_blocks + 1)
    for y in range(got_ref.shape[0]):
        rows = got_ref[y, big:, :].astype(F32)
        for start in (half, half + size):
            episode = rows[start : start + size]
            rest = episode[8 * n_blocks :]
            vectors.append(
                jnp.concatenate([episode[8 * c : 8 * c + 8] for c in range(n_blocks)], axis=1)
            )
            dpooled = jnp.concatenate([rest[c : c + 1] for c in range(n_blocks)], axis=1)
            others.append(jnp.where(own_head, dpooled, 0.0))
            loss = loss + rest[4:5] + rest[5:6]
    vectors, others = (jnp.concatenate(v, axis=0).astype(BF16) for v in (vectors, others))
    grad_ref[...] = dot(vectors, others, TN)
    loss_ref[...] = loss


def owner_kernel(got_ref, grad_in_ref, grad_out_ref, out_ref):
    total = got_ref[0].astype(F32)
    for s in range(1, got_ref.shape[0]):
        total = total + got_ref[s].astype(F32)
    in_rows, cols = grad_in_ref.shape[0], grad_out_ref.shape[1]
    out_rows = grad_out_ref.shape[0] // 2
    grad_in_ref[...] = total[:in_rows]
    pair_rows = total[in_rows : in_rows + out_rows]
    grad_out_ref[0:out_rows, :] = pair_rows[:, :cols]
    grad_out_ref[out_rows:, :] = pair_rows[:, cols:]
    share = total[in_rows + out_rows :]
    share = jnp.concatenate([share[:8] + pltpu.roll(share[:8], 4, 0), share[8:]], axis=0)
    for e in range(out_ref.shape[0]):
        out_ref[e] = share


def last_kernel(got_ref, taps_ref, query_ref):
    n_taps = taps_ref.shape[0]
    for y in range(got_ref.shape[0] // 2):
        cols = slice(y * LANES, (y + 1) * LANES)
        first, second = got_ref[2 * y], got_ref[2 * y + 1]
        row = lax.broadcasted_iota(jnp.int32, (8, LANES), 0)
        query_ref[:, cols] = jnp.where(row < 4, first[:8], second[:8])
        taps_ref[0:16, cols] = first[8:]
        taps_ref[16:n_taps, cols] = second[8 : 8 + n_taps - 16]


def call(kernel, outs, scratch, n_args, flops, placed=True):
    vmem = pl.BlockSpec(memory_space=pltpu.VMEM)
    return pl.pallas_call(
        kernel,
        out_shape=outs,
        in_specs=[pl.BlockSpec(memory_space=pltpu.SMEM)] * placed + [vmem] * n_args,
        out_specs=[vmem] * len(outs),
        scratch_shapes=scratch,
        compiler_params=pltpu.CompilerParams(vmem_limit_bytes=24 * 2**20),
        cost_estimate=pl.CostEstimate(flops=flops, bytes_accessed=8 * 2**20, transcendentals=2**20),
    )


def shards(frames, lengths, w_in, kernel, w_out, pool_query, w_value, text_emb, teacher):
    n_ep, n_seq = lax.axis_size("ep"), lax.axis_size("seq")
    x = frames[0]
    rows, width = x.shape
    n_taps, n_heads = kernel.shape[0], pool_query.shape[0]
    wide, whole = rows + 2 * SIDE, rows + 2 * STEP
    shape = jax.ShapeDtypeStruct

    odd = lax.axis_index("seq") % 2 == 1
    near = [(i, i ^ 1) for i in range(n_seq)]
    far = [(i, (i + 1) % n_seq if i % 2 else (i - 1) % n_seq) for i in range(n_seq)]
    first, last = x[:STEP], x[rows - STEP :]
    inner = lax.ppermute(jnp.where(odd, first, last), "seq", near)
    outer = lax.ppermute(jnp.where(odd, last, first), "seq", far)
    low, high = jnp.where(odd, inner, outer), jnp.where(odd, outer, inner)
    core = lax.axis_index("ep") % 2
    place = jnp.stack([lax.axis_index("seq") * rows, lengths[0], core]).astype(jnp.int32)

    own = shape((rows, width), BF16)
    normed, sig, gate_slope, own_glu = call(
        project_kernel, [own] * 4, [], 2, 2 * rows * width * width * 2
    )(place, x, w_in)
    glu, act, slope, resid, sums = call(
        forward_kernel,
        [
            shape((whole, width), BF16),
            shape((wide, width), BF16),
            shape((wide, width), BF16),
            shape((wide, width), F32),
            shape((n_seq, n_heads, width + LANES), F32),
        ],
        [pltpu.VMEM((whole, width), F32)],
        8,
        2 * rows * width * width * 4,
    )(place, low, high, x, own_glu, w_in, kernel, w_out, pool_query)
    sums = lax.all_to_all(sums, "seq", 0, 0)

    small_rows = 48
    half = small_rows // 2
    big = width + width // 2
    n_y = n_ep // 2
    size = 8 * (width // LANES + 1)
    payload = shape((n_y, big + half + size, LANES), BF16)
    mine, other = call(
        backward_kernel,
        [payload, payload],
        [
            pltpu.VMEM((wide, width), F32),
            pltpu.VMEM((whole, width), F32),
            pltpu.VMEM((wide, width), BF16),
            pltpu.VMEM((rows, 2 * width), BF16),
            pltpu.VMEM((width, 2 * width), BF16),
            pltpu.VMEM((n_taps + 1, 8, width), F32),
            pltpu.VMEM((small_rows, width), F32),
        ],
        14,
        2 * rows * width * width * 8,
    )(
        place, sums, w_value, text_emb, teacher, pool_query, resid, act, slope,
        glu, normed, sig, gate_slope, w_out, kernel,
    )

    light = functools.partial(call, scratch=[], flops=2**20, placed=False)
    got = lax.ppermute(other, "ep", [(i, i ^ 1) for i in range(n_ep)])
    (total,) = light(
        functools.partial(cores_kernel, big, half),
        [shape((n_y, big + half + 2 * size + 8, LANES), BF16)],
        n_args=2,
    )(mine, got)
    groups = [[2 * y + c for y in range(n_y)] for c in range(2)]
    got = lax.all_to_all(total, "ep", 0, 0, axis_index_groups=groups)
    (total,) = light(
        functools.partial(rows_kernel, big, half),
        [shape((n_seq, big // n_seq + half, LANES), BF16)],
        n_args=1,
    )(got)
    grad_value, loss = light(
        functools.partial(value_kernel, big, half),
        [shape((width, width), F32), shape((1, LANES), F32)],
        n_args=1,
    )(got)
    loss = loss[0, 0]
    got = lax.all_to_all(total, "seq", 0, 0)
    grad_in, grad_out, share = light(
        owner_kernel,
        [
            shape((width // n_seq, 2 * width // n_ep), F32),
            shape((width // n_seq, width // n_ep), F32),
            shape((n_ep, half, LANES), F32),
        ],
        n_args=1,
    )(got)
    got = lax.all_to_all(share, "ep", 0, 0)
    grad_kernel, grad_query = light(
        last_kernel, [shape((n_taps, width), F32), shape((n_heads, width), F32)], n_args=1
    )(got)
    return (loss, grad_in, grad_out, grad_kernel, grad_query, grad_value)


def solution(mesh):
    return jax.shard_map(
        shards,
        mesh=mesh,
        in_specs=(P("ep", "seq", None), P("ep"), P(), P(), P(), P(), P(), P(), P("ep", None)),
        out_specs=(P(), P("seq", "ep"), P("seq", "ep"), P(), P(), P()),
        check_vma=False,
    )
```

```python
import functools

import jax
import jax.numpy as jnp
from jax import lax
from jax.experimental import pallas as pl
from jax.experimental.pallas import tpu as pltpu
from jax.sharding import PartitionSpec as P

F32, BF16 = jnp.float32, jnp.bfloat16
NN = (((1,), (0,)), ((), ()))
NT = (((1,), (1,)), ((), ()))
TN = (((0,), (0,)), ((), ()))
LANES = 128
STEP = 32
SIDE = 16


def dot(a, b, dims=NN):
    return lax.dot_general(a, b, dims, preferred_element_type=F32)


def split3(value):
    high = value.astype(BF16)
    rest = value - high.astype(F32)
    mid = rest.astype(BF16)
    return high, mid, (rest - mid.astype(F32)).astype(BF16)


def stacked(value):
    return jnp.concatenate(split3(value), axis=0)


def folded(value, count=3, rows=8):
    total = value[0:rows]
    for i in range(1, count):
        total = total + value[i * rows : (i + 1) * rows]
    return total


def lane_groups(shape, pieces):
    group = lax.broadcasted_iota(jnp.int32, shape, 1) // 8
    out = jnp.zeros(shape, F32)
    for g, piece in enumerate(pieces):
        out = jnp.where(group == g, piece.astype(F32), out)
    return out.astype(BF16)


def across(column):
    lane = lax.broadcasted_iota(jnp.int32, (8, LANES), 1)
    head = lax.broadcasted_iota(jnp.int32, (8, LANES), 0)
    return jnp.sum(jnp.where(lane % 8 == head, column, 0.0), axis=0, keepdims=True)


def down(row):
    lane = lax.broadcasted_iota(jnp.int32, (8, LANES), 1)
    head = lax.broadcasted_iota(jnp.int32, (8, LANES), 0)
    return jnp.sum(jnp.where(lane == head, row, 0.0), axis=1, keepdims=True)


def gated(x, w_in, width):
    xf = x.astype(F32)
    centred = xf - jnp.mean(xf, axis=-1, keepdims=True)
    var = jnp.mean(centred * centred, axis=-1, keepdims=True)
    normed = (centred * lax.rsqrt(var + 1e-05)).astype(BF16)
    mixed = dot(normed, w_in)
    return normed, mixed[:, :width], jax.nn.sigmoid(mixed[:, width:])


def row_mask(first, rows, length):
    at = first + lax.broadcasted_iota(jnp.int32, (rows, 1), 0)
    return (at >= 0) & (at < length)


def ends_kernel(place, first_ref, last_ref, inner_ref, outer_ref):
    odd = place[3] == 1
    first, last = first_ref[...].astype(F32), last_ref[...].astype(F32)
    inner_ref[...] = jnp.where(odd, first, last).astype(BF16)
    outer_ref[...] = jnp.where(odd, last, first).astype(BF16)


def project_kernel(place, x_ref, w_in_ref, normed_ref, sig_ref, slope_ref, glu_ref):
    rows, width = x_ref.shape
    chunk = rows // 4
    for i in range(4):
        part = pl.ds(i * chunk, chunk)
        normed, gate, sig = gated(x_ref[part, :], w_in_ref[...], width)
        valid = row_mask(place[0] + i * chunk, chunk, place[1])
        normed_ref[part, :] = normed
        sig_ref[part, :] = sig.astype(BF16)
        both = gate * sig
        slope_ref[part, :] = (both * (1.0 - sig)).astype(BF16)
        glu_ref[part, :] = jnp.where(valid, both, 0.0).astype(BF16)


def shifted(block):
    rows = block.shape[0]
    return [block if s == 0 else pltpu.roll(block, rows - s, 0) for s in range(8)]


def forward_kernel(
    place, inner_ref, outer_ref, x_ref, own_glu_ref, w_in_ref, taps_ref, w_out_ref, query_ref,
    glu_ref, act_ref, slope_ref, resid_ref, sums_ref, glu_f,
):
    rows, width = x_ref.shape
    wide = rows + 2 * SIDE
    n_taps = taps_ref.shape[0]
    odd = place[3] == 1
    inner, outer = inner_ref[...].astype(F32), outer_ref[...].astype(F32)
    halo = jnp.concatenate(
        [jnp.where(odd, inner, outer), jnp.where(odd, outer, inner)], axis=0
    )
    unused, gate, sig = gated(halo, w_in_ref[...], width)
    both = gate * sig
    valid_low = row_mask(place[0] - STEP, STEP, place[1])
    valid_high = row_mask(place[0] + rows, STEP, place[1])
    low = jnp.where(valid_low, both[:STEP], 0.0).astype(BF16)
    high = jnp.where(valid_high, both[STEP:], 0.0).astype(BF16)
    glu_ref[0:STEP, :] = low
    glu_ref[STEP : STEP + rows, :] = own_glu_ref[...]
    glu_ref[STEP + rows :, :] = high
    glu_f[0:STEP, :] = low.astype(F32)
    glu_f[STEP : STEP + rows, :] = own_glu_ref[...].astype(F32)
    glu_f[STEP + rows :, :] = high.astype(F32)

    @pl.loop(0, wide // STEP)
    def _(i):
        start = pl.multiple_of(i * STEP, STEP)
        for c in range(width // LANES):
            cols = slice(c * LANES, (c + 1) * LANES)
            views = shifted(glu_f[pl.ds(start, 2 * STEP), cols])
            acc = jnp.zeros((STEP, LANES), F32)
            for k in range(n_taps):
                q, s = divmod(k + 1, 8)
                acc = acc + taps_ref[k : k + 1, cols] * views[s][8 * q : 8 * q + STEP]
            s = jax.nn.sigmoid(acc)
            act_ref[pl.ds(start, STEP), cols] = (acc * s).astype(BF16)
            slope_ref[pl.ds(start, STEP), cols] = (s * (1.0 + acc * (1.0 - s))).astype(BF16)

    w_out = w_out_ref[...]
    resid_ref[0:SIDE, :] = halo[STEP - SIDE : STEP] + dot(act_ref[0:SIDE, :], w_out)
    resid_ref[SIDE + rows :, :] = halo[STEP : STEP + SIDE] + dot(
        act_ref[SIDE + rows :, :], w_out
    )
    queries = jnp.concatenate([query_ref[...]] * (LANES // 8), axis=0)
    root = jnp.sqrt(jnp.float32(width))
    parts = 2
    chunk = rows // parts
    scores = []
    for i in range(parts):
        own = pl.ds(SIDE + i * chunk, chunk)
        resid = x_ref[pl.ds(i * chunk, chunk), :].astype(F32) + dot(act_ref[own, :], w_out)
        resid_ref[own, :] = resid
        score = sum(dot(piece, queries, NT) for piece in split3(resid)) / root
        valid = row_mask(place[0] + i * chunk, chunk, place[1])
        scores.append(jnp.where(valid, score, -1e30))
    top = functools.reduce(
        jnp.maximum, [jnp.max(score, axis=0, keepdims=True) for score in scores]
    )
    total = jnp.zeros((1, LANES), F32)
    vec = jnp.zeros((LANES, width), F32)
    for i in range(parts):
        valid = row_mask(place[0] + i * chunk, chunk, place[1])
        expo = jnp.where(valid, jnp.exp(scores[i] - top), 0.0)
        total = total + jnp.sum(expo, axis=0, keepdims=True)
        weights = lane_groups(expo.shape, split3(expo))
        for piece in split3(resid_ref[pl.ds(SIDE + i * chunk, chunk), :])[:2]:
            vec = vec + dot(weights, piece, TN)
    lane = lax.broadcasted_iota(jnp.int32, (8, LANES), 1)
    sums = jnp.concatenate(
        [folded(vec), jnp.where(lane == 0, down(top), down(total))], axis=1
    )

    @pl.loop(0, sums_ref.shape[0])
    def _(i):
        sums_ref[i] = sums


def backward_kernel(
    place, sums_ref, w_value_ref, text_ref, teacher_ref, query_ref, resid_ref, act_ref, slope_ref,
    glu_ref, normed_ref, sig_ref, gate_slope_ref, w_out_ref, taps_ref,
    mine_ref, other_ref,
    dconv_f, glu_f, dresid_s, dmixed_s, in_s, tap_s, small_s,
):
    rows, width = normed_ref.shape
    wide = rows + 2 * SIDE
    n_taps = taps_ref.shape[0]
    n_cands = text_ref.shape[0]
    head_dim = width // 8
    root = jnp.sqrt(jnp.float32(width))

    stats = sums_ref[:, :, width:]
    tops, totals = stats[:, :, 0:1], stats[:, :, 1:2]
    top = jnp.max(tops, axis=0)
    scale = jnp.exp(tops - top[None])
    total = jnp.sum(scale * totals, axis=0)
    vbar = jnp.sum(scale * sums_ref[:, :, :width], axis=0) / total
    at = lax.broadcasted_iota(jnp.int32, (8, width), 1) // head_dim
    own_head = at == lax.broadcasted_iota(jnp.int32, (8, width), 0)
    w_value = w_value_ref[...]
    texts = text_ref[...]
    full = folded(dot(stacked(vbar), w_value))
    pooled = jnp.sum(jnp.where(own_head, full, 0.0), axis=0, keepdims=True)
    pooled = jnp.broadcast_to(pooled, (8, width))
    rms = jnp.sqrt(jnp.mean(pooled * pooled, axis=-1, keepdims=True) + 1e-06)
    emb = pooled / rms
    diff = folded(dot(stacked(emb), texts, NT)) / root - teacher_ref[...]
    loss = jnp.sum(diff * diff, axis=-1, keepdims=True) / n_cands
    demb = folded(dot(stacked(2.0 * diff / n_cands), texts)) / root
    dpooled = (demb - emb * jnp.mean(demb * emb, axis=-1, keepdims=True)) / rms
    dvbar = folded(dot(stacked(jnp.where(own_head, dpooled, 0.0)), w_value, NT))
    centre = jnp.sum(dvbar * vbar, axis=-1, keepdims=True)
    row = lax.broadcasted_iota(jnp.int32, (8, width), 0)
    loss_high = loss.astype(BF16).astype(F32)
    rest = jnp.where(row == 4, loss_high, jnp.where(row == 5, loss - loss_high, 0.0))[:, :LANES]
    blocks = [slice(c * LANES, (c + 1) * LANES) for c in range(width // LANES)]
    for c, cols in enumerate(blocks):
        rest = jnp.where(row[:, :LANES] == c, dpooled[:, cols], rest)
    episode = jnp.concatenate([*[vbar[:, cols] for cols in blocks], rest], axis=0)

    top_l, total_l, centre_l = across(top), across(total), across(centre)
    query = query_ref[...]
    d_high, d_mid, d_low = split3(dvbar)
    many = lambda piece: [piece] * (LANES // 8)
    both = jnp.concatenate(many(query) + many(d_high), axis=0)
    queries, dv_mid = both[:LANES], jnp.concatenate(many(d_mid), axis=0)
    mixing = jnp.concatenate(
        [d_high, d_mid, d_high, d_mid, query, query, query, jnp.zeros((LANES - 56, width), BF16)],
        axis=0,
    )
    w_out = w_out_ref[...]
    parts = 2
    chunk = wide // parts
    grad_query = jnp.zeros((LANES, width), F32)
    for i in range(parts):
        here = pl.ds(i * chunk, chunk)
        r_high, r_mid, r_low = split3(resid_ref[here, :])
        products = dot(r_high, both, NT) + dot(r_mid, both, NT)
        score = (products[:, :LANES] + dot(r_low, queries, NT)) / root
        valid = row_mask(place[0] - SIDE + i * chunk, chunk, place[1])
        probs = jnp.where(valid, jnp.exp(score - top_l), 0.0) / total_l
        proj = products[:, LANES:] + dot(r_high, dv_mid, NT)
        dscores = probs * (proj - centre_l) / root
        p_high, p_mid, unused = split3(probs)
        s_pieces = split3(dscores)
        mixed = lane_groups(probs.shape, (p_high, p_high, p_mid, p_mid, *s_pieces))
        dresid = dot(mixed, mixing).astype(BF16)
        dresid_s[here, :] = dresid
        own = lax.broadcasted_iota(jnp.int32, (chunk, 1), 0) + i * chunk
        own = (own >= SIDE) & (own < SIDE + rows)
        weights = lane_groups(probs.shape, s_pieces)
        weights = jnp.where(own, weights.astype(F32), 0.0).astype(BF16)
        for piece in (r_high, r_mid):
            grad_query = grad_query + dot(weights, piece, TN)
        dact = dot(dresid, w_out, NT)
        dconv = (dact * slope_ref[here, :].astype(F32)).astype(BF16)
        dconv_f[here, :] = dconv.astype(F32)
    query_sum = folded(grad_query)
    high = query_sum.astype(BF16).astype(F32)
    half = small_s.shape[0] // 2
    small_s[0:8, :] = jnp.where(row < 4, high, pltpu.roll(query_sum - high, 4, 0))
    small_s[half : half + 8, :] = jnp.where(row < 4, pltpu.roll(high, 4, 0), query_sum - high)

    glu_f[...] = glu_ref[...].astype(F32)
    tap_s[...] = jnp.zeros_like(tap_s)

    @pl.loop(0, rows // STEP)
    def _(i):
        start = pl.multiple_of(i * STEP, STEP)
        valid = row_mask(place[0] + start, STEP, place[1])
        for c in range(width // LANES):
            cols = slice(c * LANES, (c + 1) * LANES)
            views = shifted(dconv_f[pl.ds(start, 2 * STEP), cols])
            acc = jnp.zeros((STEP, LANES), F32)
            for k in range(n_taps):
                q, s = divmod(n_taps - k, 8)
                acc = acc + taps_ref[k : k + 1, cols] * views[s][8 * q : 8 * q + STEP]
            dglu = jnp.where(valid, acc, 0.0)
            here = pl.ds(start, STEP)
            dmixed_s[here, cols] = (dglu * sig_ref[here, cols].astype(F32)).astype(BF16)
            dmixed_s[here, slice(width + c * LANES, width + (c + 1) * LANES)] = (
                dglu * gate_slope_ref[here, cols].astype(F32)
            ).astype(BF16)
            own = views[0][SIDE : SIDE + STEP]
            views = shifted(glu_f[pl.ds(start + SIDE, 2 * STEP), cols])
            for k in range(n_taps):
                q, s = divmod(k + 1, 8)
                product = own * views[s][8 * q : 8 * q + STEP]
                tap_s[k, :, cols] += folded(product, STEP // 8)

    tap_sum = jnp.sum(tap_s[...], axis=1)
    small_s[8:half, :] = tap_sum[: half - 8]
    small_s[half + 8 :, :] = tap_sum[half - 8 :]

    grad_out = dot(act_ref[SIDE : SIDE + rows, :], dresid_s[SIDE : SIDE + rows, :], TN)
    in_s[...] = dot(normed_ref[...], dmixed_s[...], TN).astype(BF16)
    core = place[2]
    halves = grad_out.reshape(width // 16, 2, 8, width)
    first, second = (halves[:, j].reshape(width // 2, width) for j in range(2))
    low_lane = lax.broadcasted_iota(jnp.int32, (width // 2, LANES), 1) < LANES // 2
    for y in range(width // LANES):
        a = first[:, y * LANES : (y + 1) * LANES]
        b = second[:, y * LANES : (y + 1) * LANES]
        even = jnp.where(low_lane, a, pltpu.roll(b, LANES // 2, 1))
        odd = jnp.where(low_lane, pltpu.roll(a, LANES // 2, 1), b)
        for ref, which, block in (
            (mine_ref, core, jnp.where(core == 0, even, odd)),
            (other_ref, 1 - core, jnp.where(core == 0, odd, even)),
        ):
            at = pl.multiple_of((2 * y + which) * LANES, LANES)
            ref[y, 0:width, :] = in_s[:, pl.ds(at, LANES)]
            ref[y, width : width + width // 2, :] = block.astype(BF16)
            share = small_s[pl.ds(pl.multiple_of(which * half, 8), half), y * LANES : (y + 1) * LANES]
            ref[y, width + width // 2 :, :] = jnp.concatenate([share, episode], axis=0).astype(BF16)


def paired(rows):
    row = lax.broadcasted_iota(jnp.int32, rows.shape, 0)
    value = rows + pltpu.roll(rows, 4, 0)
    high = value.astype(BF16).astype(F32)
    return jnp.where(row < 4, high, value - high)


def cores_kernel(big, half, mine_ref, got_ref, out_ref):
    for y in range(mine_ref.shape[0]):
        total = mine_ref[y, 0:big, :].astype(F32) + got_ref[y, 0:big, :].astype(F32)
        out_ref[y, 0:big, :] = total.astype(BF16)
        mine, got = mine_ref[y, big:, :].astype(F32), got_ref[y, big:, :].astype(F32)
        share = mine[:half] + got[:half]
        out_ref[y, big:, :] = jnp.concatenate(
            [paired(share[:8]), share[8:], mine[half:], got[half:], jnp.zeros((8, LANES), F32)],
            axis=0,
        ).astype(BF16)


def rows_kernel(big, half, got_ref, out_ref):
    n_y, n_seq = got_ref.shape[0], out_ref.shape[0]
    total = got_ref[0, 0:big, :].astype(F32)
    share = got_ref[0, big:, :].astype(F32)[:half]
    for y in range(1, n_y):
        total = total + got_ref[y, 0:big, :].astype(F32)
        share = share + got_ref[y, big:, :].astype(F32)[:half]
    share = jnp.concatenate([paired(share[:8]), share[8:]], axis=0)
    split = 2 * big // 3
    out_ref[...] = jnp.concatenate(
        [
            total[:split].reshape(n_seq, split // n_seq, LANES),
            total[split:].reshape(n_seq, (big - split) // n_seq, LANES),
            jnp.broadcast_to(share[None], (n_seq, half, LANES)),
        ],
        axis=1,
    ).astype(BF16)


def value_kernel(big, half, got_ref, grad_ref, loss_ref):
    width = grad_ref.shape[0]
    head = lax.broadcasted_iota(jnp.int32, (8, width), 1) // (width // 8)
    own_head = head == lax.broadcasted_iota(jnp.int32, (8, width), 0)
    vectors, others = [], []
    loss = jnp.zeros((1, LANES), F32)
    n_blocks = width // LANES
    size = 8 * (n_blocks + 1)
    for y in range(got_ref.shape[0]):
        rows = got_ref[y, big:, :].astype(F32)
        for start in (half, half + size):
            episode = rows[start : start + size]
            rest = episode[8 * n_blocks :]
            vectors.append(
                jnp.concatenate([episode[8 * c : 8 * c + 8] for c in range(n_blocks)], axis=1)
            )
            dpooled = jnp.concatenate([rest[c : c + 1] for c in range(n_blocks)], axis=1)
            others.append(jnp.where(own_head, dpooled, 0.0))
            loss = loss + rest[4:5] + rest[5:6]
    vectors, others = (jnp.concatenate(v, axis=0).astype(BF16) for v in (vectors, others))
    grad_ref[...] = dot(vectors, others, TN)
    loss_ref[...] = loss


def owner_kernel(got_ref, grad_in_ref, grad_out_ref, out_ref):
    total = got_ref[0].astype(F32)
    for s in range(1, got_ref.shape[0]):
        total = total + got_ref[s].astype(F32)
    in_rows, cols = grad_in_ref.shape[0], grad_out_ref.shape[1]
    out_rows = grad_out_ref.shape[0] // 2
    grad_in_ref[...] = total[:in_rows]
    pair_rows = total[in_rows : in_rows + out_rows]
    grad_out_ref[0:out_rows, :] = pair_rows[:, :cols]
    grad_out_ref[out_rows:, :] = pair_rows[:, cols:]
    share = total[in_rows + out_rows :]
    share = jnp.concatenate([share[:8] + pltpu.roll(share[:8], 4, 0), share[8:]], axis=0)
    for e in range(out_ref.shape[0]):
        out_ref[e] = share


def last_kernel(got_ref, taps_ref, query_ref):
    n_taps = taps_ref.shape[0]
    for y in range(got_ref.shape[0] // 2):
        cols = slice(y * LANES, (y + 1) * LANES)
        first, second = got_ref[2 * y], got_ref[2 * y + 1]
        row = lax.broadcasted_iota(jnp.int32, (8, LANES), 0)
        query_ref[:, cols] = jnp.where(row < 4, first[:8], second[:8])
        taps_ref[0:16, cols] = first[8:]
        taps_ref[16:n_taps, cols] = second[8 : 8 + n_taps - 16]


def call(kernel, outs, scratch, n_args, flops, placed=True):
    vmem = pl.BlockSpec(memory_space=pltpu.VMEM)
    return pl.pallas_call(
        kernel,
        out_shape=outs,
        in_specs=[pl.BlockSpec(memory_space=pltpu.SMEM)] * placed + [vmem] * n_args,
        out_specs=[vmem] * len(outs),
        scratch_shapes=scratch,
        compiler_params=pltpu.CompilerParams(vmem_limit_bytes=24 * 2**20),
        cost_estimate=pl.CostEstimate(flops=flops, bytes_accessed=8 * 2**20, transcendentals=2**20),
    )


def shards(frames, lengths, w_in, kernel, w_out, pool_query, w_value, text_emb, teacher):
    n_ep, n_seq = lax.axis_size("ep"), lax.axis_size("seq")
    x = frames[0]
    rows, width = x.shape
    n_taps, n_heads = kernel.shape[0], pool_query.shape[0]
    wide, whole = rows + 2 * SIDE, rows + 2 * STEP
    shape = jax.ShapeDtypeStruct

    seq = lax.axis_index("seq")
    odd = seq % 2
    core = lax.axis_index("ep") % 2
    place = jnp.stack([seq * rows, lengths[0], core, odd]).astype(jnp.int32)
    near = [(i, i ^ 1) for i in range(n_seq)]
    far = [(i, (i + 1) % n_seq if i % 2 else (i - 1) % n_seq) for i in range(n_seq)]
    inner, outer = call(ends_kernel, [shape((STEP, width), BF16)] * 2, [], 2, 2**16)(
        place, x[:STEP], x[rows - STEP :]
    )
    inner = lax.ppermute(inner, "seq", near)
    outer = lax.ppermute(outer, "seq", far)

    own = shape((rows, width), BF16)
    normed, sig, gate_slope, own_glu = call(
        project_kernel, [own] * 4, [], 2, 2 * rows * width * width * 2
    )(place, x, w_in)
    glu, act, slope, resid, sums = call(
        forward_kernel,
        [
            shape((whole, width), BF16),
            shape((wide, width), BF16),
            shape((wide, width), BF16),
            shape((wide, width), F32),
            shape((n_seq, n_heads, width + LANES), F32),
        ],
        [pltpu.VMEM((whole, width), F32)],
        8,
        2 * rows * width * width * 4,
    )(place, inner, outer, x, own_glu, w_in, kernel, w_out, pool_query)
    sums = lax.all_to_all(sums, "seq", 0, 0)

    small_rows = 48
    half = small_rows // 2
    big = width + width // 2
    n_y = n_ep // 2
    size = 8 * (width // LANES + 1)
    payload = shape((n_y, big + half + size, LANES), BF16)
    mine, other = call(
        backward_kernel,
        [payload, payload],
        [
            pltpu.VMEM((wide, width), F32),
            pltpu.VMEM((whole, width), F32),
            pltpu.VMEM((wide, width), BF16),
            pltpu.VMEM((rows, 2 * width), BF16),
            pltpu.VMEM((width, 2 * width), BF16),
            pltpu.VMEM((n_taps + 1, 8, width), F32),
            pltpu.VMEM((small_rows, width), F32),
        ],
        14,
        2 * rows * width * width * 8,
    )(
        place, sums, w_value, text_emb, teacher, pool_query, resid, act, slope,
        glu, normed, sig, gate_slope, w_out, kernel,
    )

    light = functools.partial(call, scratch=[], flops=2**20, placed=False)
    got = lax.ppermute(other, "ep", [(i, i ^ 1) for i in range(n_ep)])
    (total,) = light(
        functools.partial(cores_kernel, big, half),
        [shape((n_y, big + half + 2 * size + 8, LANES), BF16)],
        n_args=2,
    )(mine, got)
    groups = [[2 * y + c for y in range(n_y)] for c in range(2)]
    got = lax.all_to_all(total, "ep", 0, 0, axis_index_groups=groups)
    (total,) = light(
        functools.partial(rows_kernel, big, half),
        [shape((n_seq, big // n_seq + half, LANES), BF16)],
        n_args=1,
    )(got)
    grad_value, loss = light(
        functools.partial(value_kernel, big, half),
        [shape((width, width), F32), shape((1, LANES), F32)],
        n_args=1,
    )(got)
    loss = loss[0, 0]
    got = lax.all_to_all(total, "seq", 0, 0)
    grad_in, grad_out, share = light(
        owner_kernel,
        [
            shape((width // n_seq, 2 * width // n_ep), F32),
            shape((width // n_seq, width // n_ep), F32),
            shape((n_ep, half, LANES), F32),
        ],
        n_args=1,
    )(got)
    got = lax.all_to_all(share, "ep", 0, 0)
    grad_kernel, grad_query = light(
        last_kernel, [shape((n_taps, width), F32), shape((n_heads, width), F32)], n_args=1
    )(got)
    return (loss, grad_in, grad_out, grad_kernel, grad_query, grad_value)


def solution(mesh):
    return jax.shard_map(
        shards,
        mesh=mesh,
        in_specs=(P("ep", "seq", None), P("ep"), P(), P(), P(), P(), P(), P(), P("ep", None)),
        out_specs=(P(), P("seq", "ep"), P("seq", "ep"), P(), P(), P()),
        check_vma=False,
    )
```

```python
import functools

import jax
import jax.numpy as jnp
from jax import lax
from jax.experimental import pallas as pl
from jax.experimental.pallas import tpu as pltpu
from jax.sharding import PartitionSpec as P

F32, BF16 = jnp.float32, jnp.bfloat16
NN = (((1,), (0,)), ((), ()))
NT = (((1,), (1,)), ((), ()))
TN = (((0,), (0,)), ((), ()))
LANES = 128
STEP = 32
SIDE = 16


def dot(a, b, dims=NN):
    return lax.dot_general(a, b, dims, preferred_element_type=F32)


def split3(value):
    high = value.astype(BF16)
    rest = value - high.astype(F32)
    mid = rest.astype(BF16)
    return high, mid, (rest - mid.astype(F32)).astype(BF16)


def stacked(value):
    return jnp.concatenate(split3(value), axis=0)


def folded(value, count=3, rows=8):
    total = value[0:rows]
    for i in range(1, count):
        total = total + value[i * rows : (i + 1) * rows]
    return total


def lane_groups(shape, pieces):
    group = lax.broadcasted_iota(jnp.int32, shape, 1) // 8
    out = jnp.zeros(shape, F32)
    for g, piece in enumerate(pieces):
        out = jnp.where(group == g, piece.astype(F32), out)
    return out.astype(BF16)


def across(column):
    lane = lax.broadcasted_iota(jnp.int32, (8, LANES), 1)
    head = lax.broadcasted_iota(jnp.int32, (8, LANES), 0)
    return jnp.sum(jnp.where(lane % 8 == head, column, 0.0), axis=0, keepdims=True)


def down(row):
    lane = lax.broadcasted_iota(jnp.int32, (8, LANES), 1)
    head = lax.broadcasted_iota(jnp.int32, (8, LANES), 0)
    return jnp.sum(jnp.where(lane == head, row, 0.0), axis=1, keepdims=True)


def gated(x, w_in, width):
    xf = x.astype(F32)
    centred = xf - jnp.mean(xf, axis=-1, keepdims=True)
    var = jnp.mean(centred * centred, axis=-1, keepdims=True)
    normed = (centred * lax.rsqrt(var + 1e-05)).astype(BF16)
    mixed = dot(normed, w_in)
    return normed, mixed[:, :width], jax.nn.sigmoid(mixed[:, width:])


def row_mask(first, rows, length):
    at = first + lax.broadcasted_iota(jnp.int32, (rows, 1), 0)
    return (at >= 0) & (at < length)


def ends_kernel(place, first_ref, last_ref, inner_ref, outer_ref):
    odd = place[3] == 1
    first, last = first_ref[...].astype(F32), last_ref[...].astype(F32)
    inner_ref[...] = jnp.where(odd, first, last).astype(BF16)
    outer_ref[...] = jnp.where(odd, last, first).astype(BF16)


def shifted(block):
    rows = block.shape[0]
    return [block if s == 0 else pltpu.roll(block, rows - s, 0) for s in range(8)]


def convolved(block, taps_ref, cols):
    views = shifted(block)
    acc = jnp.zeros((STEP, LANES), F32)
    for k in range(taps_ref.shape[0]):
        q, s = divmod(k + 1, 8)
        acc = acc + taps_ref[k : k + 1, cols] * views[s][8 * q : 8 * q + STEP]
    s = jax.nn.sigmoid(acc)
    return (acc * s).astype(BF16), (s * (1.0 + acc * (1.0 - s))).astype(BF16)


def project_kernel(
    place, x_ref, w_in_ref, taps_ref,
    normed_ref, sig_ref, gate_slope_ref, glu_ref, act_ref, slope_ref, glu_f,
):
    rows, width = x_ref.shape
    chunk = rows // 4
    for i in range(4):
        part = pl.ds(i * chunk, chunk)
        normed, gate, sig = gated(x_ref[part, :], w_in_ref[...], width)
        valid = row_mask(place[0] + i * chunk, chunk, place[1])
        normed_ref[part, :] = normed
        sig_ref[part, :] = sig.astype(BF16)
        both = gate * sig
        gate_slope_ref[part, :] = (both * (1.0 - sig)).astype(BF16)
        glu = jnp.where(valid, both, 0.0).astype(BF16)
        glu_ref[part, :] = glu
        glu_f[part, :] = glu.astype(F32)

    @pl.loop(0, act_ref.shape[0] // STEP)
    def _(i):
        start = pl.multiple_of(i * STEP, STEP)
        for c in range(width // LANES):
            cols = slice(c * LANES, (c + 1) * LANES)
            act, slope = convolved(glu_f[pl.ds(start, 2 * STEP), cols], taps_ref, cols)
            act_ref[pl.ds(start, STEP), cols] = act
            slope_ref[pl.ds(start, STEP), cols] = slope


def forward_kernel(
    place, inner_ref, outer_ref, x_ref, own_glu_ref, w_in_ref, taps_ref, w_out_ref, query_ref,
    own_act_ref, own_slope_ref,
    glu_ref, act_ref, slope_ref, resid_ref, sums_ref, glu_f,
):
    rows, width = x_ref.shape
    wide = rows + 2 * SIDE
    odd = place[3] == 1
    inner, outer = inner_ref[...].astype(F32), outer_ref[...].astype(F32)
    halo = jnp.concatenate(
        [jnp.where(odd, inner, outer), jnp.where(odd, outer, inner)], axis=0
    )
    unused, gate, sig = gated(halo, w_in_ref[...], width)
    both = gate * sig
    valid_low = row_mask(place[0] - STEP, STEP, place[1])
    valid_high = row_mask(place[0] + rows, STEP, place[1])
    low = jnp.where(valid_low, both[:STEP], 0.0).astype(BF16)
    high = jnp.where(valid_high, both[STEP:], 0.0).astype(BF16)
    glu_ref[0:STEP, :] = low
    glu_ref[STEP : STEP + rows, :] = own_glu_ref[...]
    glu_ref[STEP + rows :, :] = high
    glu_f[0:STEP, :] = low.astype(F32)
    glu_f[STEP : 2 * STEP, :] = own_glu_ref[0:STEP, :].astype(F32)
    glu_f[2 * STEP : 3 * STEP, :] = own_glu_ref[rows - STEP : rows, :].astype(F32)
    glu_f[3 * STEP :, :] = high.astype(F32)
    act_ref[STEP : wide - STEP, :] = own_act_ref[...]
    slope_ref[STEP : wide - STEP, :] = own_slope_ref[...]
    for source, target in ((0, 0), (2 * STEP, wide - STEP)):
        for c in range(width // LANES):
            cols = slice(c * LANES, (c + 1) * LANES)
            act, slope = convolved(glu_f[source : source + 2 * STEP, cols], taps_ref, cols)
            act_ref[target : target + STEP, cols] = act
            slope_ref[target : target + STEP, cols] = slope

    w_out = w_out_ref[...]
    resid_ref[0:SIDE, :] = halo[STEP - SIDE : STEP] + dot(act_ref[0:SIDE, :], w_out)
    resid_ref[SIDE + rows :, :] = halo[STEP : STEP + SIDE] + dot(
        act_ref[SIDE + rows :, :], w_out
    )
    queries = jnp.concatenate([query_ref[...]] * (LANES // 8), axis=0)
    root = jnp.sqrt(jnp.float32(width))
    parts = 2
    chunk = rows // parts
    scores = []
    for i in range(parts):
        own = pl.ds(SIDE + i * chunk, chunk)
        resid = x_ref[pl.ds(i * chunk, chunk), :].astype(F32) + dot(act_ref[own, :], w_out)
        resid_ref[own, :] = resid
        score = sum(dot(piece, queries, NT) for piece in split3(resid)) / root
        valid = row_mask(place[0] + i * chunk, chunk, place[1])
        scores.append(jnp.where(valid, score, -1e30))
    top = functools.reduce(
        jnp.maximum, [jnp.max(score, axis=0, keepdims=True) for score in scores]
    )
    total = jnp.zeros((1, LANES), F32)
    vec = jnp.zeros((LANES, width), F32)
    for i in range(parts):
        valid = row_mask(place[0] + i * chunk, chunk, place[1])
        expo = jnp.where(valid, jnp.exp(scores[i] - top), 0.0)
        total = total + jnp.sum(expo, axis=0, keepdims=True)
        weights = lane_groups(expo.shape, split3(expo))
        for piece in split3(resid_ref[pl.ds(SIDE + i * chunk, chunk), :])[:2]:
            vec = vec + dot(weights, piece, TN)
    lane = lax.broadcasted_iota(jnp.int32, (8, LANES), 1)
    sums = jnp.concatenate(
        [folded(vec), jnp.where(lane == 0, down(top), down(total))], axis=1
    )

    @pl.loop(0, sums_ref.shape[0])
    def _(i):
        sums_ref[i] = sums


def backward_kernel(
    place, sums_ref, w_value_ref, text_ref, teacher_ref, query_ref, resid_ref, act_ref, slope_ref,
    glu_ref, normed_ref, sig_ref, gate_slope_ref, w_out_ref, taps_ref,
    mine_ref, other_ref,
    dconv_f, glu_f, dresid_s, dmixed_s, in_s, tap_s, small_s,
):
    rows, width = normed_ref.shape
    wide = rows + 2 * SIDE
    n_taps = taps_ref.shape[0]
    n_cands = text_ref.shape[0]
    head_dim = width // 8
    root = jnp.sqrt(jnp.float32(width))

    stats = sums_ref[:, :, width:]
    tops, totals = stats[:, :, 0:1], stats[:, :, 1:2]
    top = jnp.max(tops, axis=0)
    scale = jnp.exp(tops - top[None])
    total = jnp.sum(scale * totals, axis=0)
    vbar = jnp.sum(scale * sums_ref[:, :, :width], axis=0) / total
    at = lax.broadcasted_iota(jnp.int32, (8, width), 1) // head_dim
    own_head = at == lax.broadcasted_iota(jnp.int32, (8, width), 0)
    w_value = w_value_ref[...]
    texts = text_ref[...]
    full = folded(dot(stacked(vbar), w_value))
    pooled = jnp.sum(jnp.where(own_head, full, 0.0), axis=0, keepdims=True)
    pooled = jnp.broadcast_to(pooled, (8, width))
    rms = jnp.sqrt(jnp.mean(pooled * pooled, axis=-1, keepdims=True) + 1e-06)
    emb = pooled / rms
    diff = folded(dot(stacked(emb), texts, NT)) / root - teacher_ref[...]
    loss = jnp.sum(diff * diff, axis=-1, keepdims=True) / n_cands
    demb = folded(dot(stacked(2.0 * diff / n_cands), texts)) / root
    dpooled = (demb - emb * jnp.mean(demb * emb, axis=-1, keepdims=True)) / rms
    dvbar = folded(dot(stacked(jnp.where(own_head, dpooled, 0.0)), w_value, NT))
    centre = jnp.sum(dvbar * vbar, axis=-1, keepdims=True)
    row = lax.broadcasted_iota(jnp.int32, (8, width), 0)
    loss_high = loss.astype(BF16).astype(F32)
    rest = jnp.where(row == 4, loss_high, jnp.where(row == 5, loss - loss_high, 0.0))[:, :LANES]
    blocks = [slice(c * LANES, (c + 1) * LANES) for c in range(width // LANES)]
    for c, cols in enumerate(blocks):
        rest = jnp.where(row[:, :LANES] == c, dpooled[:, cols], rest)
    episode = jnp.concatenate([*[vbar[:, cols] for cols in blocks], rest], axis=0)

    top_l, total_l, centre_l = across(top), across(total), across(centre)
    query = query_ref[...]
    d_high, d_mid, d_low = split3(dvbar)
    many = lambda piece: [piece] * (LANES // 8)
    both = jnp.concatenate(many(query) + many(d_high), axis=0)
    queries, dv_mid = both[:LANES], jnp.concatenate(many(d_mid), axis=0)
    mixing = jnp.concatenate(
        [d_high, d_mid, d_high, d_mid, query, query, query, jnp.zeros((LANES - 56, width), BF16)],
        axis=0,
    )
    w_out = w_out_ref[...]
    parts = 2
    chunk = wide // parts
    grad_query = jnp.zeros((LANES, width), F32)
    for i in range(parts):
        here = pl.ds(i * chunk, chunk)
        r_high, r_mid, r_low = split3(resid_ref[here, :])
        products = dot(r_high, both, NT) + dot(r_mid, both, NT)
        score = (products[:, :LANES] + dot(r_low, queries, NT)) / root
        valid = row_mask(place[0] - SIDE + i * chunk, chunk, place[1])
        probs = jnp.where(valid, jnp.exp(score - top_l), 0.0) / total_l
        proj = products[:, LANES:] + dot(r_high, dv_mid, NT)
        dscores = probs * (proj - centre_l) / root
        p_high, p_mid, unused = split3(probs)
        s_pieces = split3(dscores)
        mixed = lane_groups(probs.shape, (p_high, p_high, p_mid, p_mid, *s_pieces))
        dresid = dot(mixed, mixing).astype(BF16)
        dresid_s[here, :] = dresid
        own = lax.broadcasted_iota(jnp.int32, (chunk, 1), 0) + i * chunk
        own = (own >= SIDE) & (own < SIDE + rows)
        weights = lane_groups(probs.shape, s_pieces)
        weights = jnp.where(own, weights.astype(F32), 0.0).astype(BF16)
        for piece in (r_high, r_mid):
            grad_query = grad_query + dot(weights, piece, TN)
        dact = dot(dresid, w_out, NT)
        dconv = (dact * slope_ref[here, :].astype(F32)).astype(BF16)
        dconv_f[here, :] = dconv.astype(F32)
    query_sum = folded(grad_query)
    high = query_sum.astype(BF16).astype(F32)
    half = small_s.shape[0] // 2
    small_s[0:8, :] = jnp.where(row < 4, high, pltpu.roll(query_sum - high, 4, 0))
    small_s[half : half + 8, :] = jnp.where(row < 4, pltpu.roll(high, 4, 0), query_sum - high)

    glu_f[...] = glu_ref[...].astype(F32)
    tap_s[...] = jnp.zeros_like(tap_s)

    @pl.loop(0, rows // STEP)
    def _(i):
        start = pl.multiple_of(i * STEP, STEP)
        valid = row_mask(place[0] + start, STEP, place[1])
        for c in range(width // LANES):
            cols = slice(c * LANES, (c + 1) * LANES)
            views = shifted(dconv_f[pl.ds(start, 2 * STEP), cols])
            acc = jnp.zeros((STEP, LANES), F32)
            for k in range(n_taps):
                q, s = divmod(n_taps - k, 8)
                acc = acc + taps_ref[k : k + 1, cols] * views[s][8 * q : 8 * q + STEP]
            dglu = jnp.where(valid, acc, 0.0)
            here = pl.ds(start, STEP)
            dmixed_s[here, cols] = (dglu * sig_ref[here, cols].astype(F32)).astype(BF16)
            dmixed_s[here, slice(width + c * LANES, width + (c + 1) * LANES)] = (
                dglu * gate_slope_ref[here, cols].astype(F32)
            ).astype(BF16)
            own = views[0][SIDE : SIDE + STEP]
            views = shifted(glu_f[pl.ds(start + SIDE, 2 * STEP), cols])
            for k in range(n_taps):
                q, s = divmod(k + 1, 8)
                product = own * views[s][8 * q : 8 * q + STEP]
                tap_s[k, :, cols] += folded(product, STEP // 8)

    tap_sum = jnp.sum(tap_s[...], axis=1)
    small_s[8:half, :] = tap_sum[: half - 8]
    small_s[half + 8 :, :] = tap_sum[half - 8 :]

    grad_out = dot(act_ref[SIDE : SIDE + rows, :], dresid_s[SIDE : SIDE + rows, :], TN)
    in_s[...] = dot(normed_ref[...], dmixed_s[...], TN).astype(BF16)
    core = place[2]
    halves = grad_out.reshape(width // 16, 2, 8, width)
    first, second = (halves[:, j].reshape(width // 2, width) for j in range(2))
    low_lane = lax.broadcasted_iota(jnp.int32, (width // 2, LANES), 1) < LANES // 2
    for y in range(width // LANES):
        a = first[:, y * LANES : (y + 1) * LANES]
        b = second[:, y * LANES : (y + 1) * LANES]
        even = jnp.where(low_lane, a, pltpu.roll(b, LANES // 2, 1))
        odd = jnp.where(low_lane, pltpu.roll(a, LANES // 2, 1), b)
        for ref, which, block in (
            (mine_ref, core, jnp.where(core == 0, even, odd)),
            (other_ref, 1 - core, jnp.where(core == 0, odd, even)),
        ):
            at = pl.multiple_of((2 * y + which) * LANES, LANES)
            ref[y, 0:width, :] = in_s[:, pl.ds(at, LANES)]
            ref[y, width : width + width // 2, :] = block.astype(BF16)
            share = small_s[pl.ds(pl.multiple_of(which * half, 8), half), y * LANES : (y + 1) * LANES]
            ref[y, width + width // 2 :, :] = jnp.concatenate([share, episode], axis=0).astype(BF16)


def paired(rows):
    row = lax.broadcasted_iota(jnp.int32, rows.shape, 0)
    value = rows + pltpu.roll(rows, 4, 0)
    high = value.astype(BF16).astype(F32)
    return jnp.where(row < 4, high, value - high)


def cores_kernel(big, half, mine_ref, got_ref, out_ref):
    for y in range(mine_ref.shape[0]):
        total = mine_ref[y, 0:big, :].astype(F32) + got_ref[y, 0:big, :].astype(F32)
        out_ref[y, 0:big, :] = total.astype(BF16)
        mine, got = mine_ref[y, big:, :].astype(F32), got_ref[y, big:, :].astype(F32)
        share = mine[:half] + got[:half]
        out_ref[y, big:, :] = jnp.concatenate(
            [paired(share[:8]), share[8:], mine[half:], got[half:], jnp.zeros((8, LANES), F32)],
            axis=0,
        ).astype(BF16)


def rows_kernel(big, half, got_ref, out_ref):
    n_y, n_seq = got_ref.shape[0], out_ref.shape[0]
    total = got_ref[0, 0:big, :].astype(F32)
    share = got_ref[0, big:, :].astype(F32)[:half]
    for y in range(1, n_y):
        total = total + got_ref[y, 0:big, :].astype(F32)
        share = share + got_ref[y, big:, :].astype(F32)[:half]
    share = jnp.concatenate([paired(share[:8]), share[8:]], axis=0)
    split = 2 * big // 3
    out_ref[...] = jnp.concatenate(
        [
            total[:split].reshape(n_seq, split // n_seq, LANES),
            total[split:].reshape(n_seq, (big - split) // n_seq, LANES),
            jnp.broadcast_to(share[None], (n_seq, half, LANES)),
        ],
        axis=1,
    ).astype(BF16)


def value_kernel(big, half, got_ref, grad_ref, loss_ref):
    width = grad_ref.shape[0]
    head = lax.broadcasted_iota(jnp.int32, (8, width), 1) // (width // 8)
    own_head = head == lax.broadcasted_iota(jnp.int32, (8, width), 0)
    vectors, others = [], []
    loss = jnp.zeros((1, LANES), F32)
    n_blocks = width // LANES
    size = 8 * (n_blocks + 1)
    for y in range(got_ref.shape[0]):
        rows = got_ref[y, big:, :].astype(F32)
        for start in (half, half + size):
            episode = rows[start : start + size]
            rest = episode[8 * n_blocks :]
            vectors.append(
                jnp.concatenate([episode[8 * c : 8 * c + 8] for c in range(n_blocks)], axis=1)
            )
            dpooled = jnp.concatenate([rest[c : c + 1] for c in range(n_blocks)], axis=1)
            others.append(jnp.where(own_head, dpooled, 0.0))
            loss = loss + rest[4:5] + rest[5:6]
    vectors, others = (jnp.concatenate(v, axis=0).astype(BF16) for v in (vectors, others))
    grad_ref[...] = dot(vectors, others, TN)
    loss_ref[...] = loss


def owner_kernel(got_ref, grad_in_ref, grad_out_ref, out_ref):
    total = got_ref[0].astype(F32)
    for s in range(1, got_ref.shape[0]):
        total = total + got_ref[s].astype(F32)
    in_rows, cols = grad_in_ref.shape[0], grad_out_ref.shape[1]
    out_rows = grad_out_ref.shape[0] // 2
    grad_in_ref[...] = total[:in_rows]
    pair_rows = total[in_rows : in_rows + out_rows]
    grad_out_ref[0:out_rows, :] = pair_rows[:, :cols]
    grad_out_ref[out_rows:, :] = pair_rows[:, cols:]
    share = total[in_rows + out_rows :]
    share = jnp.concatenate([share[:8] + pltpu.roll(share[:8], 4, 0), share[8:]], axis=0)
    for e in range(out_ref.shape[0]):
        out_ref[e] = share


def last_kernel(got_ref, taps_ref, query_ref):
    n_taps = taps_ref.shape[0]
    for y in range(got_ref.shape[0] // 2):
        cols = slice(y * LANES, (y + 1) * LANES)
        first, second = got_ref[2 * y], got_ref[2 * y + 1]
        row = lax.broadcasted_iota(jnp.int32, (8, LANES), 0)
        query_ref[:, cols] = jnp.where(row < 4, first[:8], second[:8])
        taps_ref[0:16, cols] = first[8:]
        taps_ref[16:n_taps, cols] = second[8 : 8 + n_taps - 16]


def call(kernel, outs, scratch, n_args, flops, placed=True):
    vmem = pl.BlockSpec(memory_space=pltpu.VMEM)
    return pl.pallas_call(
        kernel,
        out_shape=outs,
        in_specs=[pl.BlockSpec(memory_space=pltpu.SMEM)] * placed + [vmem] * n_args,
        out_specs=[vmem] * len(outs),
        scratch_shapes=scratch,
        compiler_params=pltpu.CompilerParams(vmem_limit_bytes=24 * 2**20),
        cost_estimate=pl.CostEstimate(flops=flops, bytes_accessed=8 * 2**20, transcendentals=2**20),
    )


def shards(frames, lengths, w_in, kernel, w_out, pool_query, w_value, text_emb, teacher):
    n_ep, n_seq = lax.axis_size("ep"), lax.axis_size("seq")
    x = frames[0]
    rows, width = x.shape
    n_taps, n_heads = kernel.shape[0], pool_query.shape[0]
    wide, whole = rows + 2 * SIDE, rows + 2 * STEP
    shape = jax.ShapeDtypeStruct

    seq = lax.axis_index("seq")
    odd = seq % 2
    core = lax.axis_index("ep") % 2
    place = jnp.stack([seq * rows, lengths[0], core, odd]).astype(jnp.int32)
    near = [(i, i ^ 1) for i in range(n_seq)]
    far = [(i, (i + 1) % n_seq if i % 2 else (i - 1) % n_seq) for i in range(n_seq)]
    inner, outer = call(ends_kernel, [shape((STEP, width), BF16)] * 2, [], 2, 2**16)(
        place, x[:STEP], x[rows - STEP :]
    )
    inner = lax.ppermute(inner, "seq", near)
    outer = lax.ppermute(outer, "seq", far)

    own = shape((rows, width), BF16)
    mid = shape((rows - STEP, width), BF16)
    normed, sig, gate_slope, own_glu, own_act, own_slope = call(
        project_kernel,
        [own] * 4 + [mid] * 2,
        [pltpu.VMEM((rows, width), F32)],
        3,
        2 * rows * width * width * 4,
    )(place, x, w_in, kernel)
    glu, act, slope, resid, sums = call(
        forward_kernel,
        [
            shape((whole, width), BF16),
            shape((wide, width), BF16),
            shape((wide, width), BF16),
            shape((wide, width), F32),
            shape((n_seq, n_heads, width + LANES), F32),
        ],
        [pltpu.VMEM((4 * STEP, width), F32)],
        10,
        2 * rows * width * width * 4,
    )(place, inner, outer, x, own_glu, w_in, kernel, w_out, pool_query, own_act, own_slope)
    sums = lax.all_to_all(sums, "seq", 0, 0)

    small_rows = 48
    half = small_rows // 2
    big = width + width // 2
    n_y = n_ep // 2
    size = 8 * (width // LANES + 1)
    payload = shape((n_y, big + half + size, LANES), BF16)
    mine, other = call(
        backward_kernel,
        [payload, payload],
        [
            pltpu.VMEM((wide, width), F32),
            pltpu.VMEM((whole, width), F32),
            pltpu.VMEM((wide, width), BF16),
            pltpu.VMEM((rows, 2 * width), BF16),
            pltpu.VMEM((width, 2 * width), BF16),
            pltpu.VMEM((n_taps + 1, 8, width), F32),
            pltpu.VMEM((small_rows, width), F32),
        ],
        14,
        2 * rows * width * width * 8,
    )(
        place, sums, w_value, text_emb, teacher, pool_query, resid, act, slope,
        glu, normed, sig, gate_slope, w_out, kernel,
    )

    light = functools.partial(call, scratch=[], flops=2**20, placed=False)
    got = lax.ppermute(other, "ep", [(i, i ^ 1) for i in range(n_ep)])
    (total,) = light(
        functools.partial(cores_kernel, big, half),
        [shape((n_y, big + half + 2 * size + 8, LANES), BF16)],
        n_args=2,
    )(mine, got)
    groups = [[2 * y + c for y in range(n_y)] for c in range(2)]
    got = lax.all_to_all(total, "ep", 0, 0, axis_index_groups=groups)
    (total,) = light(
        functools.partial(rows_kernel, big, half),
        [shape((n_seq, big // n_seq + half, LANES), BF16)],
        n_args=1,
    )(got)
    grad_value, loss = light(
        functools.partial(value_kernel, big, half),
        [shape((width, width), F32), shape((1, LANES), F32)],
        n_args=1,
    )(got)
    loss = loss[0, 0]
    got = lax.all_to_all(total, "seq", 0, 0)
    grad_in, grad_out, share = light(
        owner_kernel,
        [
            shape((width // n_seq, 2 * width // n_ep), F32),
            shape((width // n_seq, width // n_ep), F32),
            shape((n_ep, half, LANES), F32),
        ],
        n_args=1,
    )(got)
    got = lax.all_to_all(share, "ep", 0, 0)
    grad_kernel, grad_query = light(
        last_kernel, [shape((n_taps, width), F32), shape((n_heads, width), F32)], n_args=1
    )(got)
    return (loss, grad_in, grad_out, grad_kernel, grad_query, grad_value)


def solution(mesh):
    return jax.shard_map(
        shards,
        mesh=mesh,
        in_specs=(P("ep", "seq", None), P("ep"), P(), P(), P(), P(), P(), P(), P("ep", None)),
        out_specs=(P(), P("seq", "ep"), P("seq", "ep"), P(), P(), P()),
        check_vma=False,
    )
```

```python
import functools

import jax
import jax.numpy as jnp
from jax import lax
from jax.experimental import pallas as pl
from jax.experimental.pallas import tpu as pltpu
from jax.sharding import PartitionSpec as P

F32, BF16 = jnp.float32, jnp.bfloat16
NN = (((1,), (0,)), ((), ()))
NT = (((1,), (1,)), ((), ()))
TN = (((0,), (0,)), ((), ()))
LANES = 128
STEP = 32
SIDE = 16


def dot(a, b, dims=NN):
    return lax.dot_general(a, b, dims, preferred_element_type=F32)


def split3(value):
    high = value.astype(BF16)
    rest = value - high.astype(F32)
    mid = rest.astype(BF16)
    return high, mid, (rest - mid.astype(F32)).astype(BF16)


def stacked(value):
    return jnp.concatenate(split3(value), axis=0)


def folded(value, count=3, rows=8):
    total = value[0:rows]
    for i in range(1, count):
        total = total + value[i * rows : (i + 1) * rows]
    return total


def lane_groups(shape, pieces):
    group = lax.broadcasted_iota(jnp.int32, shape, 1) // 8
    out = jnp.zeros(shape, F32)
    for g, piece in enumerate(pieces):
        out = jnp.where(group == g, piece.astype(F32), out)
    return out.astype(BF16)


def across(column):
    lane = lax.broadcasted_iota(jnp.int32, (8, LANES), 1)
    head = lax.broadcasted_iota(jnp.int32, (8, LANES), 0)
    return jnp.sum(jnp.where(lane % 8 == head, column, 0.0), axis=0, keepdims=True)


def down(row):
    lane = lax.broadcasted_iota(jnp.int32, (8, LANES), 1)
    head = lax.broadcasted_iota(jnp.int32, (8, LANES), 0)
    return jnp.sum(jnp.where(lane == head, row, 0.0), axis=1, keepdims=True)


def gated(x, w_in, width):
    xf = x.astype(F32)
    centred = xf - jnp.mean(xf, axis=-1, keepdims=True)
    var = jnp.mean(centred * centred, axis=-1, keepdims=True)
    normed = (centred * lax.rsqrt(var + 1e-05)).astype(BF16)
    mixed = dot(normed, w_in)
    return normed, mixed[:, :width], jax.nn.sigmoid(mixed[:, width:])


def row_mask(first, rows, length):
    at = first + lax.broadcasted_iota(jnp.int32, (rows, 1), 0)
    return (at >= 0) & (at < length)


def ends_kernel(place, first_ref, last_ref, inner_ref, outer_ref):
    odd = place[3] == 1
    first, last = first_ref[...].astype(F32), last_ref[...].astype(F32)
    inner_ref[...] = jnp.where(odd, first, last).astype(BF16)
    outer_ref[...] = jnp.where(odd, last, first).astype(BF16)


def shifted(block):
    rows = block.shape[0]
    return [block if s == 0 else pltpu.roll(block, rows - s, 0) for s in range(8)]


def convolved(block, taps_ref, cols):
    views = shifted(block)
    acc = jnp.zeros((STEP, LANES), F32)
    for k in range(taps_ref.shape[0]):
        q, s = divmod(k + 1, 8)
        acc = acc + taps_ref[k : k + 1, cols] * views[s][8 * q : 8 * q + STEP]
    s = jax.nn.sigmoid(acc)
    return (acc * s).astype(BF16), (s * (1.0 + acc * (1.0 - s))).astype(BF16)


def project_kernel(
    place, x_ref, w_in_ref, taps_ref,
    normed_ref, sig_ref, gate_slope_ref, glu_ref, act_ref, slope_ref, glu_f,
):
    rows, width = x_ref.shape
    chunk = rows // 4
    for i in range(4):
        part = pl.ds(i * chunk, chunk)
        normed, gate, sig = gated(x_ref[part, :], w_in_ref[...], width)
        valid = row_mask(place[0] + i * chunk, chunk, place[1])
        normed_ref[part, :] = normed
        sig_ref[part, :] = sig.astype(BF16)
        both = gate * sig
        gate_slope_ref[part, :] = (both * (1.0 - sig)).astype(BF16)
        glu = jnp.where(valid, both, 0.0).astype(BF16)
        glu_ref[part, :] = glu
        glu_f[part, :] = glu.astype(F32)

    @pl.loop(0, act_ref.shape[0] // STEP)
    def _(i):
        start = pl.multiple_of(i * STEP, STEP)
        for c in range(width // LANES):
            cols = slice(c * LANES, (c + 1) * LANES)
            act, slope = convolved(glu_f[pl.ds(start, 2 * STEP), cols], taps_ref, cols)
            act_ref[pl.ds(start, STEP), cols] = act
            slope_ref[pl.ds(start, STEP), cols] = slope


def forward_kernel(
    place, inner_ref, outer_ref, x_ref, own_glu_ref, w_in_ref, taps_ref, w_out_ref, query_ref,
    own_act_ref, own_slope_ref,
    glu_ref, act_ref, slope_ref, resid_ref, score_ref, sums_ref, glu_f,
):
    rows, width = x_ref.shape
    wide = rows + 2 * SIDE
    odd = place[3] == 1
    inner, outer = inner_ref[...].astype(F32), outer_ref[...].astype(F32)
    halo = jnp.concatenate(
        [jnp.where(odd, inner, outer), jnp.where(odd, outer, inner)], axis=0
    )
    unused, gate, sig = gated(halo, w_in_ref[...], width)
    both = gate * sig
    valid_low = row_mask(place[0] - STEP, STEP, place[1])
    valid_high = row_mask(place[0] + rows, STEP, place[1])
    low = jnp.where(valid_low, both[:STEP], 0.0).astype(BF16)
    high = jnp.where(valid_high, both[STEP:], 0.0).astype(BF16)
    glu_ref[0:STEP, :] = low
    glu_ref[STEP : STEP + rows, :] = own_glu_ref[...]
    glu_ref[STEP + rows :, :] = high
    glu_f[0:STEP, :] = low.astype(F32)
    glu_f[STEP : 2 * STEP, :] = own_glu_ref[0:STEP, :].astype(F32)
    glu_f[2 * STEP : 3 * STEP, :] = own_glu_ref[rows - STEP : rows, :].astype(F32)
    glu_f[3 * STEP :, :] = high.astype(F32)
    act_ref[STEP : wide - STEP, :] = own_act_ref[...]
    slope_ref[STEP : wide - STEP, :] = own_slope_ref[...]
    for source, target in ((0, 0), (2 * STEP, wide - STEP)):
        for c in range(width // LANES):
            cols = slice(c * LANES, (c + 1) * LANES)
            act, slope = convolved(glu_f[source : source + 2 * STEP, cols], taps_ref, cols)
            act_ref[target : target + STEP, cols] = act
            slope_ref[target : target + STEP, cols] = slope

    w_out = w_out_ref[...]
    resid_ref[0:SIDE, :] = halo[STEP - SIDE : STEP] + dot(act_ref[0:SIDE, :], w_out)
    resid_ref[SIDE + rows :, :] = halo[STEP : STEP + SIDE] + dot(
        act_ref[SIDE + rows :, :], w_out
    )
    queries = jnp.concatenate([query_ref[...]] * (LANES // 8), axis=0)
    root = jnp.sqrt(jnp.float32(width))

    def scored(resid):
        return sum(dot(piece, queries, NT) for piece in split3(resid)) / root

    score_ref[0:SIDE, :] = scored(resid_ref[0:SIDE, :])
    score_ref[SIDE + rows :, :] = scored(resid_ref[SIDE + rows :, :])
    parts = 2
    chunk = rows // parts
    scores = []
    for i in range(parts):
        own = pl.ds(SIDE + i * chunk, chunk)
        resid = x_ref[pl.ds(i * chunk, chunk), :].astype(F32) + dot(act_ref[own, :], w_out)
        resid_ref[own, :] = resid
        score = scored(resid)
        score_ref[own, :] = score
        valid = row_mask(place[0] + i * chunk, chunk, place[1])
        scores.append(jnp.where(valid, score, -1e30))
    top = functools.reduce(
        jnp.maximum, [jnp.max(score, axis=0, keepdims=True) for score in scores]
    )
    total = jnp.zeros((1, LANES), F32)
    vec = jnp.zeros((LANES, width), F32)
    for i in range(parts):
        valid = row_mask(place[0] + i * chunk, chunk, place[1])
        expo = jnp.where(valid, jnp.exp(scores[i] - top), 0.0)
        total = total + jnp.sum(expo, axis=0, keepdims=True)
        weights = lane_groups(expo.shape, split3(expo))
        for piece in split3(resid_ref[pl.ds(SIDE + i * chunk, chunk), :])[:2]:
            vec = vec + dot(weights, piece, TN)
    lane = lax.broadcasted_iota(jnp.int32, (8, LANES), 1)
    sums = jnp.concatenate(
        [folded(vec), jnp.where(lane == 0, down(top), down(total))], axis=1
    )

    @pl.loop(0, sums_ref.shape[0])
    def _(i):
        sums_ref[i] = sums


def backward_kernel(
    place, sums_ref, w_value_ref, text_ref, teacher_ref, query_ref, resid_ref, score_ref, act_ref, slope_ref,
    glu_ref, normed_ref, sig_ref, gate_slope_ref, w_out_ref, taps_ref,
    mine_ref, other_ref,
    dconv_f, glu_f, dresid_s, dmixed_s, in_s, tap_s, small_s,
):
    rows, width = normed_ref.shape
    wide = rows + 2 * SIDE
    n_taps = taps_ref.shape[0]
    n_cands = text_ref.shape[0]
    head_dim = width // 8
    root = jnp.sqrt(jnp.float32(width))

    stats = sums_ref[:, :, width:]
    tops, totals = stats[:, :, 0:1], stats[:, :, 1:2]
    top = jnp.max(tops, axis=0)
    scale = jnp.exp(tops - top[None])
    total = jnp.sum(scale * totals, axis=0)
    vbar = jnp.sum(scale * sums_ref[:, :, :width], axis=0) / total
    at = lax.broadcasted_iota(jnp.int32, (8, width), 1) // head_dim
    own_head = at == lax.broadcasted_iota(jnp.int32, (8, width), 0)
    w_value = w_value_ref[...]
    texts = text_ref[...]
    full = folded(dot(stacked(vbar), w_value))
    pooled = jnp.sum(jnp.where(own_head, full, 0.0), axis=0, keepdims=True)
    pooled = jnp.broadcast_to(pooled, (8, width))
    rms = jnp.sqrt(jnp.mean(pooled * pooled, axis=-1, keepdims=True) + 1e-06)
    emb = pooled / rms
    diff = folded(dot(stacked(emb), texts, NT)) / root - teacher_ref[...]
    loss = jnp.sum(diff * diff, axis=-1, keepdims=True) / n_cands
    demb = folded(dot(stacked(2.0 * diff / n_cands), texts)) / root
    dpooled = (demb - emb * jnp.mean(demb * emb, axis=-1, keepdims=True)) / rms
    dvbar = folded(dot(stacked(jnp.where(own_head, dpooled, 0.0)), w_value, NT))
    centre = jnp.sum(dvbar * vbar, axis=-1, keepdims=True)
    row = lax.broadcasted_iota(jnp.int32, (8, width), 0)
    loss_high = loss.astype(BF16).astype(F32)
    rest = jnp.where(row == 4, loss_high, jnp.where(row == 5, loss - loss_high, 0.0))[:, :LANES]
    blocks = [slice(c * LANES, (c + 1) * LANES) for c in range(width // LANES)]
    for c, cols in enumerate(blocks):
        rest = jnp.where(row[:, :LANES] == c, dpooled[:, cols], rest)
    episode = jnp.concatenate([*[vbar[:, cols] for cols in blocks], rest], axis=0)

    top_l, total_l, centre_l = across(top), across(total), across(centre)
    query = query_ref[...]
    d_high, d_mid, d_low = split3(dvbar)
    many = lambda piece: [piece] * (LANES // 8)
    pieces = jnp.concatenate(many(d_high) + many(d_mid), axis=0)
    mixing = jnp.concatenate(
        [d_high, d_mid, d_high, d_mid, query, query, query, jnp.zeros((LANES - 56, width), BF16)],
        axis=0,
    )
    w_out = w_out_ref[...]
    parts = 2
    chunk = wide // parts
    grad_query = jnp.zeros((LANES, width), F32)
    for i in range(parts):
        here = pl.ds(i * chunk, chunk)
        r_high, r_mid = split3(resid_ref[here, :])[:2]
        valid = row_mask(place[0] - SIDE + i * chunk, chunk, place[1])
        probs = jnp.where(valid, jnp.exp(score_ref[here, :] - top_l), 0.0) / total_l
        products = dot(r_high, pieces, NT)
        proj = products[:, :LANES] + (products[:, LANES:] + dot(r_mid, pieces[:LANES], NT))
        dscores = probs * (proj - centre_l) / root
        p_high, p_mid, unused = split3(probs)
        s_pieces = split3(dscores)
        mixed = lane_groups(probs.shape, (p_high, p_high, p_mid, p_mid, *s_pieces))
        dresid = dot(mixed, mixing).astype(BF16)
        dresid_s[here, :] = dresid
        own = lax.broadcasted_iota(jnp.int32, (chunk, 1), 0) + i * chunk
        own = (own >= SIDE) & (own < SIDE + rows)
        weights = lane_groups(probs.shape, s_pieces)
        weights = jnp.where(own, weights.astype(F32), 0.0).astype(BF16)
        for piece in (r_high, r_mid):
            grad_query = grad_query + dot(weights, piece, TN)
        dact = dot(dresid, w_out, NT)
        dconv = (dact * slope_ref[here, :].astype(F32)).astype(BF16)
        dconv_f[here, :] = dconv.astype(F32)
    query_sum = folded(grad_query)
    high = query_sum.astype(BF16).astype(F32)
    half = small_s.shape[0] // 2
    small_s[0:8, :] = jnp.where(row < 4, high, pltpu.roll(query_sum - high, 4, 0))
    small_s[half : half + 8, :] = jnp.where(row < 4, pltpu.roll(high, 4, 0), query_sum - high)

    glu_f[...] = glu_ref[...].astype(F32)
    tap_s[...] = jnp.zeros_like(tap_s)

    @pl.loop(0, rows // STEP)
    def _(i):
        start = pl.multiple_of(i * STEP, STEP)
        valid = row_mask(place[0] + start, STEP, place[1])
        for c in range(width // LANES):
            cols = slice(c * LANES, (c + 1) * LANES)
            views = shifted(dconv_f[pl.ds(start, 2 * STEP), cols])
            acc = jnp.zeros((STEP, LANES), F32)
            for k in range(n_taps):
                q, s = divmod(n_taps - k, 8)
                acc = acc + taps_ref[k : k + 1, cols] * views[s][8 * q : 8 * q + STEP]
            dglu = jnp.where(valid, acc, 0.0)
            here = pl.ds(start, STEP)
            dmixed_s[here, cols] = (dglu * sig_ref[here, cols].astype(F32)).astype(BF16)
            dmixed_s[here, slice(width + c * LANES, width + (c + 1) * LANES)] = (
                dglu * gate_slope_ref[here, cols].astype(F32)
            ).astype(BF16)
            own = views[0][SIDE : SIDE + STEP]
            views = shifted(glu_f[pl.ds(start + SIDE, 2 * STEP), cols])
            for k in range(n_taps):
                q, s = divmod(k + 1, 8)
                product = own * views[s][8 * q : 8 * q + STEP]
                tap_s[k, :, cols] += folded(product, STEP // 8)

    tap_sum = jnp.sum(tap_s[...], axis=1)
    small_s[8:half, :] = tap_sum[: half - 8]
    small_s[half + 8 :, :] = tap_sum[half - 8 :]

    grad_out = dot(act_ref[SIDE : SIDE + rows, :], dresid_s[SIDE : SIDE + rows, :], TN)
    in_s[...] = dot(normed_ref[...], dmixed_s[...], TN).astype(BF16)
    core = place[2]
    halves = grad_out.reshape(width // 16, 2, 8, width)
    first, second = (halves[:, j].reshape(width // 2, width) for j in range(2))
    low_lane = lax.broadcasted_iota(jnp.int32, (width // 2, LANES), 1) < LANES // 2
    for y in range(width // LANES):
        a = first[:, y * LANES : (y + 1) * LANES]
        b = second[:, y * LANES : (y + 1) * LANES]
        even = jnp.where(low_lane, a, pltpu.roll(b, LANES // 2, 1))
        odd = jnp.where(low_lane, pltpu.roll(a, LANES // 2, 1), b)
        for ref, which, block in (
            (mine_ref, core, jnp.where(core == 0, even, odd)),
            (other_ref, 1 - core, jnp.where(core == 0, odd, even)),
        ):
            at = pl.multiple_of((2 * y + which) * LANES, LANES)
            ref[y, 0:width, :] = in_s[:, pl.ds(at, LANES)]
            ref[y, width : width + width // 2, :] = block.astype(BF16)
            share = small_s[pl.ds(pl.multiple_of(which * half, 8), half), y * LANES : (y + 1) * LANES]
            ref[y, width + width // 2 :, :] = jnp.concatenate([share, episode], axis=0).astype(BF16)


def paired(rows):
    row = lax.broadcasted_iota(jnp.int32, rows.shape, 0)
    value = rows + pltpu.roll(rows, 4, 0)
    high = value.astype(BF16).astype(F32)
    return jnp.where(row < 4, high, value - high)


def cores_kernel(big, half, mine_ref, got_ref, out_ref):
    for y in range(mine_ref.shape[0]):
        total = mine_ref[y, 0:big, :].astype(F32) + got_ref[y, 0:big, :].astype(F32)
        out_ref[y, 0:big, :] = total.astype(BF16)
        mine, got = mine_ref[y, big:, :].astype(F32), got_ref[y, big:, :].astype(F32)
        share = mine[:half] + got[:half]
        out_ref[y, big:, :] = jnp.concatenate(
            [paired(share[:8]), share[8:], mine[half:], got[half:], jnp.zeros((8, LANES), F32)],
            axis=0,
        ).astype(BF16)


def rows_kernel(big, half, got_ref, out_ref):
    n_y, n_seq = got_ref.shape[0], out_ref.shape[0]
    total = got_ref[0, 0:big, :].astype(F32)
    share = got_ref[0, big:, :].astype(F32)[:half]
    for y in range(1, n_y):
        total = total + got_ref[y, 0:big, :].astype(F32)
        share = share + got_ref[y, big:, :].astype(F32)[:half]
    share = jnp.concatenate([paired(share[:8]), share[8:]], axis=0)
    split = 2 * big // 3
    out_ref[...] = jnp.concatenate(
        [
            total[:split].reshape(n_seq, split // n_seq, LANES),
            total[split:].reshape(n_seq, (big - split) // n_seq, LANES),
            jnp.broadcast_to(share[None], (n_seq, half, LANES)),
        ],
        axis=1,
    ).astype(BF16)


def value_kernel(big, half, got_ref, grad_ref, loss_ref):
    width = grad_ref.shape[0]
    head = lax.broadcasted_iota(jnp.int32, (8, width), 1) // (width // 8)
    own_head = head == lax.broadcasted_iota(jnp.int32, (8, width), 0)
    vectors, others = [], []
    loss = jnp.zeros((1, LANES), F32)
    n_blocks = width // LANES
    size = 8 * (n_blocks + 1)
    for y in range(got_ref.shape[0]):
        rows = got_ref[y, big:, :].astype(F32)
        for start in (half, half + size):
            episode = rows[start : start + size]
            rest = episode[8 * n_blocks :]
            vectors.append(
                jnp.concatenate([episode[8 * c : 8 * c + 8] for c in range(n_blocks)], axis=1)
            )
            dpooled = jnp.concatenate([rest[c : c + 1] for c in range(n_blocks)], axis=1)
            others.append(jnp.where(own_head, dpooled, 0.0))
            loss = loss + rest[4:5] + rest[5:6]
    vectors, others = (jnp.concatenate(v, axis=0).astype(BF16) for v in (vectors, others))
    grad_ref[...] = dot(vectors, others, TN)
    loss_ref[...] = loss


def owner_kernel(got_ref, grad_in_ref, grad_out_ref, out_ref):
    total = got_ref[0].astype(F32)
    for s in range(1, got_ref.shape[0]):
        total = total + got_ref[s].astype(F32)
    in_rows, cols = grad_in_ref.shape[0], grad_out_ref.shape[1]
    out_rows = grad_out_ref.shape[0] // 2
    grad_in_ref[...] = total[:in_rows]
    pair_rows = total[in_rows : in_rows + out_rows]
    grad_out_ref[0:out_rows, :] = pair_rows[:, :cols]
    grad_out_ref[out_rows:, :] = pair_rows[:, cols:]
    share = total[in_rows + out_rows :]
    share = jnp.concatenate([share[:8] + pltpu.roll(share[:8], 4, 0), share[8:]], axis=0)
    for e in range(out_ref.shape[0]):
        out_ref[e] = share


def last_kernel(got_ref, taps_ref, query_ref):
    n_taps = taps_ref.shape[0]
    for y in range(got_ref.shape[0] // 2):
        cols = slice(y * LANES, (y + 1) * LANES)
        first, second = got_ref[2 * y], got_ref[2 * y + 1]
        row = lax.broadcasted_iota(jnp.int32, (8, LANES), 0)
        query_ref[:, cols] = jnp.where(row < 4, first[:8], second[:8])
        taps_ref[0:16, cols] = first[8:]
        taps_ref[16:n_taps, cols] = second[8 : 8 + n_taps - 16]


def call(kernel, outs, scratch, n_args, flops, placed=True):
    vmem = pl.BlockSpec(memory_space=pltpu.VMEM)
    return pl.pallas_call(
        kernel,
        out_shape=outs,
        in_specs=[pl.BlockSpec(memory_space=pltpu.SMEM)] * placed + [vmem] * n_args,
        out_specs=[vmem] * len(outs),
        scratch_shapes=scratch,
        compiler_params=pltpu.CompilerParams(vmem_limit_bytes=24 * 2**20),
        cost_estimate=pl.CostEstimate(flops=flops, bytes_accessed=8 * 2**20, transcendentals=2**20),
    )


def shards(frames, lengths, w_in, kernel, w_out, pool_query, w_value, text_emb, teacher):
    n_ep, n_seq = lax.axis_size("ep"), lax.axis_size("seq")
    x = frames[0]
    rows, width = x.shape
    n_taps, n_heads = kernel.shape[0], pool_query.shape[0]
    wide, whole = rows + 2 * SIDE, rows + 2 * STEP
    shape = jax.ShapeDtypeStruct

    seq = lax.axis_index("seq")
    odd = seq % 2
    core = lax.axis_index("ep") % 2
    place = jnp.stack([seq * rows, lengths[0], core, odd]).astype(jnp.int32)
    near = [(i, i ^ 1) for i in range(n_seq)]
    far = [(i, (i + 1) % n_seq if i % 2 else (i - 1) % n_seq) for i in range(n_seq)]
    inner, outer = call(ends_kernel, [shape((STEP, width), BF16)] * 2, [], 2, 2**16)(
        place, x[:STEP], x[rows - STEP :]
    )
    inner = lax.ppermute(inner, "seq", near)
    outer = lax.ppermute(outer, "seq", far)

    own = shape((rows, width), BF16)
    mid = shape((rows - STEP, width), BF16)
    normed, sig, gate_slope, own_glu, own_act, own_slope = call(
        project_kernel,
        [own] * 4 + [mid] * 2,
        [pltpu.VMEM((rows, width), F32)],
        3,
        2 * rows * width * width * 4,
    )(place, x, w_in, kernel)
    glu, act, slope, resid, score, sums = call(
        forward_kernel,
        [
            shape((whole, width), BF16),
            shape((wide, width), BF16),
            shape((wide, width), BF16),
            shape((wide, width), F32),
            shape((wide, LANES), F32),
            shape((n_seq, n_heads, width + LANES), F32),
        ],
        [pltpu.VMEM((4 * STEP, width), F32)],
        10,
        2 * rows * width * width * 4,
    )(place, inner, outer, x, own_glu, w_in, kernel, w_out, pool_query, own_act, own_slope)
    sums = lax.all_to_all(sums, "seq", 0, 0)

    small_rows = 48
    half = small_rows // 2
    big = width + width // 2
    n_y = n_ep // 2
    size = 8 * (width // LANES + 1)
    payload = shape((n_y, big + half + size, LANES), BF16)
    mine, other = call(
        backward_kernel,
        [payload, payload],
        [
            pltpu.VMEM((wide, width), F32),
            pltpu.VMEM((whole, width), F32),
            pltpu.VMEM((wide, width), BF16),
            pltpu.VMEM((rows, 2 * width), BF16),
            pltpu.VMEM((width, 2 * width), BF16),
            pltpu.VMEM((n_taps + 1, 8, width), F32),
            pltpu.VMEM((small_rows, width), F32),
        ],
        15,
        2 * rows * width * width * 8,
    )(
        place, sums, w_value, text_emb, teacher, pool_query, resid, score, act, slope,
        glu, normed, sig, gate_slope, w_out, kernel,
    )

    light = functools.partial(call, scratch=[], flops=2**20, placed=False)
    got = lax.ppermute(other, "ep", [(i, i ^ 1) for i in range(n_ep)])
    (total,) = light(
        functools.partial(cores_kernel, big, half),
        [shape((n_y, big + half + 2 * size + 8, LANES), BF16)],
        n_args=2,
    )(mine, got)
    groups = [[2 * y + c for y in range(n_y)] for c in range(2)]
    got = lax.all_to_all(total, "ep", 0, 0, axis_index_groups=groups)
    (total,) = light(
        functools.partial(rows_kernel, big, half),
        [shape((n_seq, big // n_seq + half, LANES), BF16)],
        n_args=1,
    )(got)
    grad_value, loss = light(
        functools.partial(value_kernel, big, half),
        [shape((width, width), F32), shape((1, LANES), F32)],
        n_args=1,
    )(got)
    loss = loss[0, 0]
    got = lax.all_to_all(total, "seq", 0, 0)
    grad_in, grad_out, share = light(
        owner_kernel,
        [
            shape((width // n_seq, 2 * width // n_ep), F32),
            shape((width // n_seq, width // n_ep), F32),
            shape((n_ep, half, LANES), F32),
        ],
        n_args=1,
    )(got)
    got = lax.all_to_all(share, "ep", 0, 0)
    grad_kernel, grad_query = light(
        last_kernel, [shape((n_taps, width), F32), shape((n_heads, width), F32)], n_args=1
    )(got)
    return (loss, grad_in, grad_out, grad_kernel, grad_query, grad_value)


def solution(mesh):
    return jax.shard_map(
        shards,
        mesh=mesh,
        in_specs=(P("ep", "seq", None), P("ep"), P(), P(), P(), P(), P(), P(), P("ep", None)),
        out_specs=(P(), P("seq", "ep"), P("seq", "ep"), P(), P(), P()),
        check_vma=False,
    )
```

```python
import functools

import jax
import jax.numpy as jnp
from jax import lax
from jax.experimental import pallas as pl
from jax.experimental.pallas import tpu as pltpu
from jax.sharding import PartitionSpec as P

F32, BF16 = jnp.float32, jnp.bfloat16
NN = (((1,), (0,)), ((), ()))
NT = (((1,), (1,)), ((), ()))
TN = (((0,), (0,)), ((), ()))
LANES = 128
STEP = 32
SIDE = 16


def dot(a, b, dims=NN):
    return lax.dot_general(a, b, dims, preferred_element_type=F32)


def split3(value):
    high = value.astype(BF16)
    rest = value - high.astype(F32)
    mid = rest.astype(BF16)
    return high, mid, (rest - mid.astype(F32)).astype(BF16)


def stacked(value):
    return jnp.concatenate(split3(value), axis=0)


def folded(value, count=3, rows=8):
    total = value[0:rows]
    for i in range(1, count):
        total = total + value[i * rows : (i + 1) * rows]
    return total


def lane_groups(shape, pieces):
    group = lax.broadcasted_iota(jnp.int32, shape, 1) // 8
    out = jnp.zeros(shape, F32)
    for g, piece in enumerate(pieces):
        out = jnp.where(group == g, piece.astype(F32), out)
    return out.astype(BF16)


def across(column):
    lane = lax.broadcasted_iota(jnp.int32, (8, LANES), 1)
    head = lax.broadcasted_iota(jnp.int32, (8, LANES), 0)
    return jnp.sum(jnp.where(lane % 8 == head, column, 0.0), axis=0, keepdims=True)


def down(row):
    lane = lax.broadcasted_iota(jnp.int32, (8, LANES), 1)
    head = lax.broadcasted_iota(jnp.int32, (8, LANES), 0)
    return jnp.sum(jnp.where(lane == head, row, 0.0), axis=1, keepdims=True)


def gated(x, w_in, width):
    xf = x.astype(F32)
    centred = xf - jnp.mean(xf, axis=-1, keepdims=True)
    var = jnp.mean(centred * centred, axis=-1, keepdims=True)
    normed = (centred * lax.rsqrt(var + 1e-05)).astype(BF16)
    mixed = dot(normed, w_in)
    return normed, mixed[:, :width], jax.nn.sigmoid(mixed[:, width:])


def row_mask(first, rows, length):
    at = first + lax.broadcasted_iota(jnp.int32, (rows, 1), 0)
    return (at >= 0) & (at < length)


def ends_kernel(place, first_ref, last_ref, inner_ref, outer_ref):
    odd = place[3] == 1
    first, last = first_ref[...].astype(F32), last_ref[...].astype(F32)
    inner_ref[...] = jnp.where(odd, first, last).astype(BF16)
    outer_ref[...] = jnp.where(odd, last, first).astype(BF16)


def shifted(block):
    rows = block.shape[0]
    return [block if s == 0 else pltpu.roll(block, rows - s, 0) for s in range(8)]


def convolved(block, taps_ref, cols):
    views = shifted(block)
    acc = jnp.zeros((STEP, LANES), F32)
    for k in range(taps_ref.shape[0]):
        q, s = divmod(k + 1, 8)
        acc = acc + taps_ref[k : k + 1, cols] * views[s][8 * q : 8 * q + STEP]
    s = jax.nn.sigmoid(acc)
    return (acc * s).astype(BF16), (s * (1.0 + acc * (1.0 - s))).astype(BF16)


def project_kernel(
    place, x_ref, w_in_ref, taps_ref,
    normed_ref, sig_ref, gate_slope_ref, glu_ref, act_ref, slope_ref, glu_f,
):
    rows, width = x_ref.shape
    chunk = rows // 4
    for i in range(4):
        part = pl.ds(i * chunk, chunk)
        normed, gate, sig = gated(x_ref[part, :], w_in_ref[...], width)
        valid = row_mask(place[0] + i * chunk, chunk, place[1])
        normed_ref[part, :] = normed
        sig_ref[part, :] = sig.astype(BF16)
        both = gate * sig
        gate_slope_ref[part, :] = (both * (1.0 - sig)).astype(BF16)
        glu = jnp.where(valid, both, 0.0).astype(BF16)
        glu_ref[part, :] = glu
        glu_f[part, :] = glu.astype(F32)

    @pl.loop(0, act_ref.shape[0] // STEP)
    def _(i):
        start = pl.multiple_of(i * STEP, STEP)
        for c in range(width // LANES):
            cols = slice(c * LANES, (c + 1) * LANES)
            act, slope = convolved(glu_f[pl.ds(start, 2 * STEP), cols], taps_ref, cols)
            act_ref[pl.ds(start, STEP), cols] = act
            slope_ref[pl.ds(start, STEP), cols] = slope


def forward_kernel(
    place, inner_ref, outer_ref, x_ref, own_glu_ref, w_in_ref, taps_ref, w_out_ref, query_ref,
    own_act_ref, own_slope_ref,
    glu_ref, act_ref, slope_ref, resid_ref, score_ref, sums_ref, glu_f,
):
    rows, width = x_ref.shape
    wide = rows + 2 * SIDE
    odd = place[3] == 1
    inner, outer = inner_ref[...].astype(F32), outer_ref[...].astype(F32)
    halo = jnp.concatenate(
        [jnp.where(odd, inner, outer), jnp.where(odd, outer, inner)], axis=0
    )
    unused, gate, sig = gated(halo, w_in_ref[...], width)
    both = gate * sig
    valid_low = row_mask(place[0] - STEP, STEP, place[1])
    valid_high = row_mask(place[0] + rows, STEP, place[1])
    low = jnp.where(valid_low, both[:STEP], 0.0).astype(BF16)
    high = jnp.where(valid_high, both[STEP:], 0.0).astype(BF16)
    glu_ref[0:STEP, :] = low
    glu_ref[STEP : STEP + rows, :] = own_glu_ref[...]
    glu_ref[STEP + rows :, :] = high
    glu_f[0:STEP, :] = low.astype(F32)
    glu_f[STEP : 2 * STEP, :] = own_glu_ref[0:STEP, :].astype(F32)
    glu_f[2 * STEP : 3 * STEP, :] = own_glu_ref[rows - STEP : rows, :].astype(F32)
    glu_f[3 * STEP :, :] = high.astype(F32)
    act_ref[STEP : wide - STEP, :] = own_act_ref[...]
    slope_ref[STEP : wide - STEP, :] = own_slope_ref[...]
    for source, target in ((0, 0), (2 * STEP, wide - STEP)):
        for c in range(width // LANES):
            cols = slice(c * LANES, (c + 1) * LANES)
            act, slope = convolved(glu_f[source : source + 2 * STEP, cols], taps_ref, cols)
            act_ref[target : target + STEP, cols] = act
            slope_ref[target : target + STEP, cols] = slope

    w_out = w_out_ref[...]
    resid_ref[0:SIDE, :] = halo[STEP - SIDE : STEP] + dot(act_ref[0:SIDE, :], w_out)
    resid_ref[SIDE + rows :, :] = halo[STEP : STEP + SIDE] + dot(
        act_ref[SIDE + rows :, :], w_out
    )
    queries = jnp.concatenate([query_ref[...]] * (LANES // 8), axis=0)
    root = jnp.sqrt(jnp.float32(width))

    def scored(resid):
        return sum(dot(piece, queries, NT) for piece in split3(resid)) / root

    sides = scored(jnp.concatenate([resid_ref[0:SIDE, :], resid_ref[SIDE + rows :, :]], axis=0))
    score_ref[0:SIDE, :] = sides[:SIDE]
    score_ref[SIDE + rows :, :] = sides[SIDE:]
    parts = 2
    chunk = rows // parts
    scores = []
    for i in range(parts):
        own = pl.ds(SIDE + i * chunk, chunk)
        resid = x_ref[pl.ds(i * chunk, chunk), :].astype(F32) + dot(act_ref[own, :], w_out)
        resid_ref[own, :] = resid
        score = scored(resid)
        score_ref[own, :] = score
        valid = row_mask(place[0] + i * chunk, chunk, place[1])
        scores.append(jnp.where(valid, score, -1e30))
    top = functools.reduce(
        jnp.maximum, [jnp.max(score, axis=0, keepdims=True) for score in scores]
    )
    total = jnp.zeros((1, LANES), F32)
    vec = jnp.zeros((LANES, width), F32)
    for i in range(parts):
        valid = row_mask(place[0] + i * chunk, chunk, place[1])
        expo = jnp.where(valid, jnp.exp(scores[i] - top), 0.0)
        total = total + jnp.sum(expo, axis=0, keepdims=True)
        weights = lane_groups(expo.shape, split3(expo))
        for piece in split3(resid_ref[pl.ds(SIDE + i * chunk, chunk), :])[:2]:
            vec = vec + dot(weights, piece, TN)
    lane = lax.broadcasted_iota(jnp.int32, (8, LANES), 1)
    sums = jnp.concatenate(
        [folded(vec), jnp.where(lane == 0, down(top), down(total))], axis=1
    )

    @pl.loop(0, sums_ref.shape[0])
    def _(i):
        sums_ref[i] = sums


def backward_kernel(
    place, sums_ref, w_value_ref, text_ref, teacher_ref, query_ref, resid_ref, score_ref, act_ref, slope_ref,
    glu_ref, normed_ref, sig_ref, gate_slope_ref, w_out_ref, taps_ref,
    mine_ref, other_ref,
    dconv_f, glu_f, dresid_s, dmixed_s, in_s, tap_s, small_s,
):
    rows, width = normed_ref.shape
    wide = rows + 2 * SIDE
    n_taps = taps_ref.shape[0]
    n_cands = text_ref.shape[0]
    head_dim = width // 8
    root = jnp.sqrt(jnp.float32(width))

    stats = sums_ref[:, :, width:]
    tops, totals = stats[:, :, 0:1], stats[:, :, 1:2]
    top = jnp.max(tops, axis=0)
    scale = jnp.exp(tops - top[None])
    total = jnp.sum(scale * totals, axis=0)
    vbar = jnp.sum(scale * sums_ref[:, :, :width], axis=0) / total
    at = lax.broadcasted_iota(jnp.int32, (8, width), 1) // head_dim
    own_head = at == lax.broadcasted_iota(jnp.int32, (8, width), 0)
    w_value = w_value_ref[...]
    texts = text_ref[...]
    full = folded(dot(stacked(vbar), w_value))
    pooled = jnp.sum(jnp.where(own_head, full, 0.0), axis=0, keepdims=True)
    pooled = jnp.broadcast_to(pooled, (8, width))
    rms = jnp.sqrt(jnp.mean(pooled * pooled, axis=-1, keepdims=True) + 1e-06)
    emb = pooled / rms
    diff = folded(dot(stacked(emb), texts, NT)) / root - teacher_ref[...]
    loss = jnp.sum(diff * diff, axis=-1, keepdims=True) / n_cands
    demb = folded(dot(stacked(2.0 * diff / n_cands), texts)) / root
    dpooled = (demb - emb * jnp.mean(demb * emb, axis=-1, keepdims=True)) / rms
    dvbar = folded(dot(stacked(jnp.where(own_head, dpooled, 0.0)), w_value, NT))
    centre = jnp.sum(dvbar * vbar, axis=-1, keepdims=True)
    row = lax.broadcasted_iota(jnp.int32, (8, width), 0)
    loss_high = loss.astype(BF16).astype(F32)
    rest = jnp.where(row == 4, loss_high, jnp.where(row == 5, loss - loss_high, 0.0))[:, :LANES]
    blocks = [slice(c * LANES, (c + 1) * LANES) for c in range(width // LANES)]
    for c, cols in enumerate(blocks):
        rest = jnp.where(row[:, :LANES] == c, dpooled[:, cols], rest)
    episode = jnp.concatenate([*[vbar[:, cols] for cols in blocks], rest], axis=0)

    top_l, total_l, centre_l = across(top), across(total), across(centre)
    query = query_ref[...]
    d_high, d_mid, d_low = split3(dvbar)
    many = lambda piece: [piece] * (LANES // 8)
    pieces = jnp.concatenate(many(d_high) + many(d_mid), axis=0)
    mixing = jnp.concatenate(
        [d_high, d_mid, d_high, d_mid, query, query, query, jnp.zeros((LANES - 56, width), BF16)],
        axis=0,
    )
    w_out = w_out_ref[...]
    parts = 2
    chunk = wide // parts
    grad_query = jnp.zeros((LANES, width), F32)
    for i in range(parts):
        here = pl.ds(i * chunk, chunk)
        r_high, r_mid = split3(resid_ref[here, :])[:2]
        valid = row_mask(place[0] - SIDE + i * chunk, chunk, place[1])
        probs = jnp.where(valid, jnp.exp(score_ref[here, :] - top_l), 0.0) / total_l
        products = dot(r_high, pieces, NT)
        proj = products[:, :LANES] + (products[:, LANES:] + dot(r_mid, pieces[:LANES], NT))
        dscores = probs * (proj - centre_l) / root
        p_high, p_mid, unused = split3(probs)
        s_pieces = split3(dscores)
        mixed = lane_groups(probs.shape, (p_high, p_high, p_mid, p_mid, *s_pieces))
        dresid = dot(mixed, mixing).astype(BF16)
        dresid_s[here, :] = dresid
        own = lax.broadcasted_iota(jnp.int32, (chunk, 1), 0) + i * chunk
        own = (own >= SIDE) & (own < SIDE + rows)
        weights = lane_groups(probs.shape, s_pieces)
        weights = jnp.where(own, weights.astype(F32), 0.0).astype(BF16)
        for piece in (r_high, r_mid):
            grad_query = grad_query + dot(weights, piece, TN)
        dact = dot(dresid, w_out, NT)
        dconv = (dact * slope_ref[here, :].astype(F32)).astype(BF16)
        dconv_f[here, :] = dconv.astype(F32)
    query_sum = folded(grad_query)
    high = query_sum.astype(BF16).astype(F32)
    half = small_s.shape[0] // 2
    small_s[0:8, :] = jnp.where(row < 4, high, pltpu.roll(query_sum - high, 4, 0))
    small_s[half : half + 8, :] = jnp.where(row < 4, pltpu.roll(high, 4, 0), query_sum - high)

    glu_f[...] = glu_ref[...].astype(F32)
    tap_s[...] = jnp.zeros_like(tap_s)

    @pl.loop(0, rows // STEP)
    def _(i):
        start = pl.multiple_of(i * STEP, STEP)
        valid = row_mask(place[0] + start, STEP, place[1])
        for c in range(width // LANES):
            cols = slice(c * LANES, (c + 1) * LANES)
            views = shifted(dconv_f[pl.ds(start, 2 * STEP), cols])
            acc = jnp.zeros((STEP, LANES), F32)
            for k in range(n_taps):
                q, s = divmod(n_taps - k, 8)
                acc = acc + taps_ref[k : k + 1, cols] * views[s][8 * q : 8 * q + STEP]
            dglu = jnp.where(valid, acc, 0.0)
            here = pl.ds(start, STEP)
            dmixed_s[here, cols] = (dglu * sig_ref[here, cols].astype(F32)).astype(BF16)
            dmixed_s[here, slice(width + c * LANES, width + (c + 1) * LANES)] = (
                dglu * gate_slope_ref[here, cols].astype(F32)
            ).astype(BF16)
            own = views[0][SIDE : SIDE + STEP]
            views = shifted(glu_f[pl.ds(start + SIDE, 2 * STEP), cols])
            for k in range(n_taps):
                q, s = divmod(k + 1, 8)
                product = own * views[s][8 * q : 8 * q + STEP]
                tap_s[k, :, cols] += folded(product, STEP // 8)

    tap_sum = jnp.sum(tap_s[...], axis=1)
    small_s[8:half, :] = tap_sum[: half - 8]
    small_s[half + 8 :, :] = tap_sum[half - 8 :]

    grad_out = dot(act_ref[SIDE : SIDE + rows, :], dresid_s[SIDE : SIDE + rows, :], TN)
    in_s[...] = dot(normed_ref[...], dmixed_s[...], TN).astype(BF16)
    core = place[2]
    halves = grad_out.reshape(width // 16, 2, 8, width)
    first, second = (halves[:, j].reshape(width // 2, width) for j in range(2))
    low_lane = lax.broadcasted_iota(jnp.int32, (width // 2, LANES), 1) < LANES // 2
    for y in range(width // LANES):
        a = first[:, y * LANES : (y + 1) * LANES]
        b = second[:, y * LANES : (y + 1) * LANES]
        even = jnp.where(low_lane, a, pltpu.roll(b, LANES // 2, 1))
        odd = jnp.where(low_lane, pltpu.roll(a, LANES // 2, 1), b)
        for ref, which, block in (
            (mine_ref, core, jnp.where(core == 0, even, odd)),
            (other_ref, 1 - core, jnp.where(core == 0, odd, even)),
        ):
            at = pl.multiple_of((2 * y + which) * LANES, LANES)
            ref[y, 0:width, :] = in_s[:, pl.ds(at, LANES)]
            ref[y, width : width + width // 2, :] = block.astype(BF16)
            share = small_s[pl.ds(pl.multiple_of(which * half, 8), half), y * LANES : (y + 1) * LANES]
            ref[y, width + width // 2 :, :] = jnp.concatenate([share, episode], axis=0).astype(BF16)


def paired(rows):
    row = lax.broadcasted_iota(jnp.int32, rows.shape, 0)
    value = rows + pltpu.roll(rows, 4, 0)
    high = value.astype(BF16).astype(F32)
    return jnp.where(row < 4, high, value - high)


def cores_kernel(big, half, mine_ref, got_ref, out_ref):
    for y in range(mine_ref.shape[0]):
        total = mine_ref[y, 0:big, :].astype(F32) + got_ref[y, 0:big, :].astype(F32)
        out_ref[y, 0:big, :] = total.astype(BF16)
        mine, got = mine_ref[y, big:, :].astype(F32), got_ref[y, big:, :].astype(F32)
        share = mine[:half] + got[:half]
        out_ref[y, big:, :] = jnp.concatenate(
            [paired(share[:8]), share[8:], mine[half:], got[half:], jnp.zeros((8, LANES), F32)],
            axis=0,
        ).astype(BF16)


def rows_kernel(big, half, got_ref, out_ref):
    n_y, n_seq = got_ref.shape[0], out_ref.shape[0]
    total = got_ref[0, 0:big, :].astype(F32)
    share = got_ref[0, big:, :].astype(F32)[:half]
    for y in range(1, n_y):
        total = total + got_ref[y, 0:big, :].astype(F32)
        share = share + got_ref[y, big:, :].astype(F32)[:half]
    share = jnp.concatenate([paired(share[:8]), share[8:]], axis=0)
    split = 2 * big // 3
    out_ref[...] = jnp.concatenate(
        [
            total[:split].reshape(n_seq, split // n_seq, LANES),
            total[split:].reshape(n_seq, (big - split) // n_seq, LANES),
            jnp.broadcast_to(share[None], (n_seq, half, LANES)),
        ],
        axis=1,
    ).astype(BF16)


def value_kernel(big, half, got_ref, grad_ref, loss_ref):
    width = grad_ref.shape[0]
    head = lax.broadcasted_iota(jnp.int32, (8, width), 1) // (width // 8)
    own_head = head == lax.broadcasted_iota(jnp.int32, (8, width), 0)
    vectors, others = [], []
    loss = jnp.zeros((1, LANES), F32)
    n_blocks = width // LANES
    size = 8 * (n_blocks + 1)
    for y in range(got_ref.shape[0]):
        rows = got_ref[y, big:, :].astype(F32)
        for start in (half, half + size):
            episode = rows[start : start + size]
            rest = episode[8 * n_blocks :]
            vectors.append(
                jnp.concatenate([episode[8 * c : 8 * c + 8] for c in range(n_blocks)], axis=1)
            )
            dpooled = jnp.concatenate([rest[c : c + 1] for c in range(n_blocks)], axis=1)
            others.append(jnp.where(own_head, dpooled, 0.0))
            loss = loss + rest[4:5] + rest[5:6]
    vectors, others = (jnp.concatenate(v, axis=0).astype(BF16) for v in (vectors, others))
    grad_ref[...] = dot(vectors, others, TN)
    loss_ref[...] = loss


def owner_kernel(got_ref, grad_in_ref, grad_out_ref, out_ref):
    total = got_ref[0].astype(F32)
    for s in range(1, got_ref.shape[0]):
        total = total + got_ref[s].astype(F32)
    in_rows, cols = grad_in_ref.shape[0], grad_out_ref.shape[1]
    out_rows = grad_out_ref.shape[0] // 2
    grad_in_ref[...] = total[:in_rows]
    pair_rows = total[in_rows : in_rows + out_rows]
    grad_out_ref[0:out_rows, :] = pair_rows[:, :cols]
    grad_out_ref[out_rows:, :] = pair_rows[:, cols:]
    share = total[in_rows + out_rows :]
    share = jnp.concatenate([share[:8] + pltpu.roll(share[:8], 4, 0), share[8:]], axis=0)
    for e in range(out_ref.shape[0]):
        out_ref[e] = share


def last_kernel(got_ref, taps_ref, query_ref):
    n_taps = taps_ref.shape[0]
    for y in range(got_ref.shape[0] // 2):
        cols = slice(y * LANES, (y + 1) * LANES)
        first, second = got_ref[2 * y], got_ref[2 * y + 1]
        row = lax.broadcasted_iota(jnp.int32, (8, LANES), 0)
        query_ref[:, cols] = jnp.where(row < 4, first[:8], second[:8])
        taps_ref[0:16, cols] = first[8:]
        taps_ref[16:n_taps, cols] = second[8 : 8 + n_taps - 16]


def call(kernel, outs, scratch, n_args, flops, placed=True):
    vmem = pl.BlockSpec(memory_space=pltpu.VMEM)
    return pl.pallas_call(
        kernel,
        out_shape=outs,
        in_specs=[pl.BlockSpec(memory_space=pltpu.SMEM)] * placed + [vmem] * n_args,
        out_specs=[vmem] * len(outs),
        scratch_shapes=scratch,
        compiler_params=pltpu.CompilerParams(vmem_limit_bytes=24 * 2**20),
        cost_estimate=pl.CostEstimate(flops=flops, bytes_accessed=8 * 2**20, transcendentals=2**20),
    )


def shards(frames, lengths, w_in, kernel, w_out, pool_query, w_value, text_emb, teacher):
    n_ep, n_seq = lax.axis_size("ep"), lax.axis_size("seq")
    x = frames[0]
    rows, width = x.shape
    n_taps, n_heads = kernel.shape[0], pool_query.shape[0]
    wide, whole = rows + 2 * SIDE, rows + 2 * STEP
    shape = jax.ShapeDtypeStruct

    seq = lax.axis_index("seq")
    odd = seq % 2
    core = lax.axis_index("ep") % 2
    place = jnp.stack([seq * rows, lengths[0], core, odd]).astype(jnp.int32)
    near = [(i, i ^ 1) for i in range(n_seq)]
    far = [(i, (i + 1) % n_seq if i % 2 else (i - 1) % n_seq) for i in range(n_seq)]
    inner, outer = call(ends_kernel, [shape((STEP, width), BF16)] * 2, [], 2, 2**16)(
        place, x[:STEP], x[rows - STEP :]
    )
    inner = lax.ppermute(inner, "seq", near)
    outer = lax.ppermute(outer, "seq", far)

    own = shape((rows, width), BF16)
    mid = shape((rows - STEP, width), BF16)
    normed, sig, gate_slope, own_glu, own_act, own_slope = call(
        project_kernel,
        [own] * 4 + [mid] * 2,
        [pltpu.VMEM((rows, width), F32)],
        3,
        2 * rows * width * width * 4,
    )(place, x, w_in, kernel)
    glu, act, slope, resid, score, sums = call(
        forward_kernel,
        [
            shape((whole, width), BF16),
            shape((wide, width), BF16),
            shape((wide, width), BF16),
            shape((wide, width), F32),
            shape((wide, LANES), F32),
            shape((n_seq, n_heads, width + LANES), F32),
        ],
        [pltpu.VMEM((4 * STEP, width), F32)],
        10,
        2 * rows * width * width * 4,
    )(place, inner, outer, x, own_glu, w_in, kernel, w_out, pool_query, own_act, own_slope)
    sums = lax.all_to_all(sums, "seq", 0, 0)

    small_rows = 48
    half = small_rows // 2
    big = width + width // 2
    n_y = n_ep // 2
    size = 8 * (width // LANES + 1)
    payload = shape((n_y, big + half + size, LANES), BF16)
    mine, other = call(
        backward_kernel,
        [payload, payload],
        [
            pltpu.VMEM((wide, width), F32),
            pltpu.VMEM((whole, width), F32),
            pltpu.VMEM((wide, width), BF16),
            pltpu.VMEM((rows, 2 * width), BF16),
            pltpu.VMEM((width, 2 * width), BF16),
            pltpu.VMEM((n_taps + 1, 8, width), F32),
            pltpu.VMEM((small_rows, width), F32),
        ],
        15,
        2 * rows * width * width * 8,
    )(
        place, sums, w_value, text_emb, teacher, pool_query, resid, score, act, slope,
        glu, normed, sig, gate_slope, w_out, kernel,
    )

    light = functools.partial(call, scratch=[], flops=2**20, placed=False)
    got = lax.ppermute(other, "ep", [(i, i ^ 1) for i in range(n_ep)])
    (total,) = light(
        functools.partial(cores_kernel, big, half),
        [shape((n_y, big + half + 2 * size + 8, LANES), BF16)],
        n_args=2,
    )(mine, got)
    groups = [[2 * y + c for y in range(n_y)] for c in range(2)]
    got = lax.all_to_all(total, "ep", 0, 0, axis_index_groups=groups)
    (total,) = light(
        functools.partial(rows_kernel, big, half),
        [shape((n_seq, big // n_seq + half, LANES), BF16)],
        n_args=1,
    )(got)
    grad_value, loss = light(
        functools.partial(value_kernel, big, half),
        [shape((width, width), F32), shape((1, LANES), F32)],
        n_args=1,
    )(got)
    loss = loss[0, 0]
    got = lax.all_to_all(total, "seq", 0, 0)
    grad_in, grad_out, share = light(
        owner_kernel,
        [
            shape((width // n_seq, 2 * width // n_ep), F32),
            shape((width // n_seq, width // n_ep), F32),
            shape((n_ep, half, LANES), F32),
        ],
        n_args=1,
    )(got)
    got = lax.all_to_all(share, "ep", 0, 0)
    grad_kernel, grad_query = light(
        last_kernel, [shape((n_taps, width), F32), shape((n_heads, width), F32)], n_args=1
    )(got)
    return (loss, grad_in, grad_out, grad_kernel, grad_query, grad_value)


def solution(mesh):
    return jax.shard_map(
        shards,
        mesh=mesh,
        in_specs=(P("ep", "seq", None), P("ep"), P(), P(), P(), P(), P(), P(), P("ep", None)),
        out_specs=(P(), P("seq", "ep"), P("seq", "ep"), P(), P(), P()),
        check_vma=False,
    )
```
